128 devices in a mesh: dp: 8 (over x, core), fsdp: 4 (over y), tensor: 4 (over z).
Axes of the slice: x: 4, y: 4, z: 4, core: 2. Of those that a mesh axis runs over, the one named last changes fastest.
Arguments:
- tokens: bfloat16 [5120, 8192], P('dp', 'fsdp'), may hold values from -6 to 6
- cotangent: bfloat16 [5120, 28672], P('dp', 'tensor'), may hold values from -6 to 6
- left_factor: bfloat16 [8192, 512], P('fsdp'), may hold values from -0.0625 to 0.0625
- right_factor: bfloat16 [512, 4, 7168], P(None, 'tensor', 'fsdp'), may hold values from -0.25 to 0.25
- block_values: bfloat16 [512, 128, 128], P(('fsdp', 'tensor')), may hold values from -0.5 to 0.5
- block_rows: int32 [512], P(('fsdp', 'tensor')), may hold values from 0 to 15, as said below
- block_cols: int32 [512], P(('fsdp', 'tensor')), may hold values from 0 to 55
- block_counts: int32 [16], replicated, may hold values from 1 to 32, as said below
Outputs:
- mixed: bfloat16 [5120, 4, 7168], P('dp', 'tensor', 'fsdp')
- grad_left: bfloat16 [8192, 512], P('fsdp')
- grad_right: bfloat16 [512, 4, 7168], P(None, 'tensor', 'fsdp')
- grad_blocks: bfloat16 [512, 128, 128], P(('fsdp', 'tensor'))
The draws below stay inside these ranges and needn't reach their ends.
Inputs may be any that keep to these rules, and one draw needn't show every extreme that they name: Within one owner's 32 slots, the pairs (block_rows, block_cols) are all different. `block_counts`: some owner has exactly 32 live slots.
All inputs are finite; a program needn't handle non-finite values.
Results may differ from the reference program's by a relative error of at most 0.005.
Values may be sent and summed in bfloat16 or wider, within the bound.
No kernel may reach another device: no remote copies, remote signals or barrier semaphores. Data moves between devices by JAX's collectives and lax.ppermute only.
A program may use at most 192 MiB of HBM per device.

```python
import jax
import jax.numpy as jnp
from jax import lax

D = 8192
FF = 28672
R = 512
BS = 128
MAXB = 32
TOKENS = 5120
OWNERS = 16
BLOCKS = 512
SLICES = 4
QW = 7168
RBD = 16
CBD = 56
N_TENSOR = 4


def block_positions(key):
    keys = jax.random.split(key, OWNERS)
    chosen = jax.vmap(lambda single: jax.random.permutation(single, RBD * CBD)[:MAXB])(keys)
    return chosen.reshape(-1).astype(jnp.int32)


def draw_block_rows(key, part):
    places = block_positions(key)
    return (places // CBD).astype(jnp.int32)


def draw_block_cols(key, part):
    places = block_positions(key)
    return (places % CBD).astype(jnp.int32)


def draw_block_counts(key, part):
    key = jax.random.fold_in(key, 3)
    first, second = jax.random.split(key)
    lowest = max(MAXB // 8, 1)
    base = jax.random.randint(first, (OWNERS,), lowest, 3 * MAXB // 4 + 1)
    heavy = jax.random.randint(second, (), 0, OWNERS)
    return jnp.where(jnp.arange(OWNERS) == heavy, MAXB, base).astype(jnp.int32)


def shard_levels(stream_key, dims, pieces, least, high):
    gain = 1.0
    for dim, shards_of in pieces:
        draws = jax.random.uniform(jax.random.fold_in(jax.random.fold_in(stream_key, 6), dim), (shards_of,), jnp.float32, least / len(pieces), high / len(pieces))
        gain = gain * jnp.repeat(jnp.exp(draws), dims[dim] // shards_of).reshape((-1,) + (1,) * (len(dims) - 1 - dim))
    return gain


def gaussian(own_key, extent, deviation, most, shards=(), kind=jnp.bfloat16):
    array = jax.random.normal(own_key, extent, jnp.float32) * deviation
    if len(shards) > 0:
        array = shard_levels(own_key, extent, shards, -0.22, 0.18) * array
    return jnp.clip(array, min=-most, max=most).astype(kind)


def setup_inputs(seed: int = 0) -> dict:
    streams_of = jax.random.split(jax.random.key(seed), 9)
    tokens = gaussian(streams_of[0], (TOKENS, D), 1.0, 6.0, ((0, 8), (1, 4)))
    cotangent = gaussian(streams_of[1], (TOKENS, FF), 1.0, 6.0, ((0, 8), (1, 4)))
    left_factor = gaussian(streams_of[2], (D, R), D ** -0.5, 0.0625, ((0, 4),))
    right_factor = gaussian(streams_of[3], (R, SLICES, QW), R ** -0.5, 0.25, ((1, 4), (2, 4)))
    block_values = gaussian(streams_of[4], (BLOCKS, BS, BS), BS ** -0.5, 0.5, ((0, 16),))
    block_rows = draw_block_rows(jax.random.fold_in(streams_of[8], 71), 0)
    block_cols = draw_block_cols(jax.random.fold_in(streams_of[8], 71), 0)
    block_counts = draw_block_counts(jax.random.fold_in(streams_of[8], 71), 0)
    return {"tokens": tokens, "cotangent": cotangent, "left_factor": left_factor, "right_factor": right_factor, "block_values": block_values, "block_rows": block_rows, "block_cols": block_cols, "block_counts": block_counts}


def reference(tokens, cotangent, left_factor, right_factor, block_values, block_rows, block_cols, block_counts):
    rank = jnp.dot(tokens, left_factor, preferred_element_type=jnp.float32).astype(jnp.bfloat16)
    right_flat = right_factor.reshape(R, FF)
    low = jnp.dot(rank, right_flat, preferred_element_type=jnp.float32)
    slots = jnp.arange(BLOCKS, dtype=jnp.int32)
    owner = slots // MAXB
    owner_f = owner // N_TENSOR
    owner_t = owner % N_TENSOR
    live = slots % MAXB < block_counts[owner]
    grow = (owner_f * RBD + block_rows).astype(jnp.int32)
    gcol = (owner_t * CBD + block_cols).astype(jnp.int32)
    rows3 = tokens.reshape(TOKENS, D // BS, BS)
    cols3 = cotangent.reshape(TOKENS, FF // BS, BS)

    def add_block(i, acc):
        panel = lax.dynamic_index_in_dim(rows3, grow[i], 1, keepdims=False)
        prod = jnp.dot(panel, block_values[i], preferred_element_type=jnp.float32)
        prod = jnp.where(live[i], prod, jnp.zeros_like(prod))
        current = lax.dynamic_index_in_dim(acc, gcol[i], 1, keepdims=False)
        return lax.dynamic_update_index_in_dim(acc, current + prod, gcol[i], 1)
    sparse = lax.fori_loop(0, BLOCKS, add_block, jnp.zeros((TOKENS, FF // BS, BS), jnp.float32))
    mixed = (low + sparse.reshape(TOKENS, FF)).astype(jnp.bfloat16).reshape(TOKENS, SLICES, QW)
    back = lax.dot_general(cotangent, right_flat, (((1,), (1,)), ((), ())), preferred_element_type=jnp.float32).astype(jnp.bfloat16)
    grad_left = lax.dot_general(tokens, back, (((0,), (0,)), ((), ())), preferred_element_type=jnp.float32).astype(jnp.bfloat16)
    grad_right = lax.dot_general(rank, cotangent, (((0,), (0,)), ((), ())), preferred_element_type=jnp.float32)
    grad_right = grad_right.astype(jnp.bfloat16).reshape(R, SLICES, QW)

    def one_grad(i):
        panel = lax.dynamic_index_in_dim(rows3, grow[i], 1, keepdims=False)
        cpanel = lax.dynamic_index_in_dim(cols3, gcol[i], 1, keepdims=False)
        grad = lax.dot_general(panel, cpanel, (((0,), (0,)), ((), ())), preferred_element_type=jnp.float32)
        return jnp.where(live[i], grad, jnp.zeros_like(grad))
    grad_blocks = lax.map(one_grad, slots).astype(jnp.bfloat16)
    return (mixed, grad_left, grad_right, grad_blocks)
```

```python
import jax
import jax.numpy as jnp
from jax import lax
from jax.experimental import pallas as pl
from jax.experimental.pallas import tpu as pltpu
from jax.sharding import PartitionSpec as P

F32 = jnp.float32
BF16 = jnp.bfloat16
SIDE = 128


def lanes(block):
    return pl.ds(pl.multiple_of(block * SIDE, SIDE), SIDE)


def block_grads_kernel(live_ref, rows_ref, cols_ref, tok_ref, cot_ref, out_ref):
    out_ref[...] = jnp.zeros_like(out_ref)

    def body(s, carry):
        panel = tok_ref[:, lanes(rows_ref[s])]
        cpanel = cot_ref[:, lanes(cols_ref[s])]
        grad = lax.dot_general(
            panel, cpanel, (((0,), (0,)), ((), ())), preferred_element_type=F32
        )
        out_ref[pl.ds(s, 1)] = grad.astype(BF16)[None]
        return carry

    lax.fori_loop(0, live_ref[0], body, 0)


def block_grads(live, rows, cols, tokens, cotangent, vmem_mib=40):
    maxb = rows.shape[0]
    smem = pl.BlockSpec(memory_space=pltpu.SMEM)
    vmem = pl.BlockSpec(memory_space=pltpu.VMEM)
    tok_rows = tokens.shape[0]
    return pl.pallas_call(
        block_grads_kernel,
        out_shape=jax.ShapeDtypeStruct((maxb, SIDE, SIDE), BF16),
        in_specs=[smem, smem, smem, vmem, vmem],
        out_specs=vmem,
        cost_estimate=pl.CostEstimate(
            flops=2 * maxb * tok_rows * SIDE * SIDE,
            bytes_accessed=2 * tokens.size + 2 * cotangent.size + 2 * maxb * SIDE * SIDE,
            transcendentals=0,
        ),
        compiler_params=pltpu.CompilerParams(vmem_limit_bytes=vmem_mib << 20),
    )(live, rows, cols, tokens, cotangent)


DEPTH = 6


def mixed_kernel(
    n_owners, maxb, q_blocks, chunk,
    info_ref, rows_ref, cols_ref, rank_ref, right_ref, tok_ref, val_ref, out_ref,
    acc, list_ref, panels, vals, sems,
):
    me = info_ref[n_owners]

    def scan(i, n):
        owner = i // maxb
        col = cols_ref[i]
        use = (i - owner * maxb < info_ref[owner]) & (col // q_blocks == me)
        list_ref[n] = i
        return n + use.astype(jnp.int32)

    total = lax.fori_loop(0, n_owners * maxb, scan, 0)
    per = chunk // SIDE
    owner_chunks = tok_ref.shape[0] // n_owners

    def copies(k):
        i = list_ref[k]
        slot = lax.rem(k, DEPTH)
        row = rows_ref[i]
        src = tok_ref.at[(i // maxb) * owner_chunks + row // per, :, lanes(lax.rem(row, per))]
        return (
            pltpu.make_async_copy(src, panels.at[slot], sems.at[slot, 0]),
            pltpu.make_async_copy(val_ref.at[i], vals.at[slot], sems.at[slot, 1]),
        )

    def start(k):
        @pl.when(k < total)
        def _():
            for c in copies(k):
                c.start()

    for k in range(DEPTH - 1):
        start(jnp.int32(k))
    acc[...] = jnp.dot(rank_ref[...], right_ref[...], preferred_element_type=F32)

    def body(k, carry):
        start(k + DEPTH - 1)
        for c in copies(k):
            c.wait()
        slot = lax.rem(k, DEPTH)
        col = cols_ref[list_ref[k]] - me * q_blocks
        acc[:, lanes(col)] += jnp.dot(panels[slot], vals[slot], preferred_element_type=F32)
        return carry

    lax.fori_loop(0, total, body, 0)
    out_ref[...] = acc[...].astype(BF16)


def mixed_product(info, rows, cols, rank, right, tok, vals, maxb, q_blocks):
    n_owners = rows.shape[0] // maxb
    tok_rows, quarter = rank.shape[0], right.shape[1]
    chunk = tok.shape[2]
    smem = pl.BlockSpec(memory_space=pltpu.SMEM)
    vmem = pl.BlockSpec(memory_space=pltpu.VMEM)
    hbm = pl.BlockSpec(memory_space=pl.ANY)

    def kernel(*refs):
        mixed_kernel(n_owners, maxb, q_blocks, chunk, *refs)

    return pl.pallas_call(
        kernel,
        out_shape=jax.ShapeDtypeStruct((tok_rows, quarter), BF16),
        in_specs=[smem, smem, smem, vmem, vmem, hbm, hbm],
        out_specs=vmem,
        scratch_shapes=[
            pltpu.VMEM((tok_rows, quarter), F32),
            pltpu.SMEM((n_owners * maxb + 1,), jnp.int32),
            pltpu.VMEM((DEPTH, tok_rows, SIDE), BF16),
            pltpu.VMEM((DEPTH, SIDE, SIDE), BF16),
            pltpu.SemaphoreType.DMA((DEPTH, 2)),
        ],
        cost_estimate=pl.CostEstimate(
            flops=2 * tok_rows * quarter * rank.shape[1],
            bytes_accessed=2 * tok.size,
            transcendentals=0,
        ),
        compiler_params=pltpu.CompilerParams(vmem_limit_bytes=40 << 20),
    )(info, rows, cols, rank, right, tok, vals)


def shift(x, axis, n, k):
    return lax.ppermute(x, axis, [(i, (i + k) % n) for i in range(n)])


def chip_shift(x, n_data, k):
    chips = n_data // 2
    perm = [(2 * a + c, 2 * ((a + k) % chips) + c) for a in range(chips) for c in range(2)]
    return lax.ppermute(x, "dp", perm)


def scatter_dp(x, n_data, d_index):
    chips = n_data // 2
    chip, core = d_index // 2, d_index % 2
    parts = x.reshape((chips, 2, x.shape[0] // n_data) + x.shape[1:])
    theirs = lax.dynamic_index_in_dim(parts, 1 - core, 1, keepdims=False).astype(BF16)
    mine = lax.dynamic_index_in_dim(parts, core, 1, keepdims=False).astype(F32)
    got = lax.ppermute(theirs, "dp", [(i, i ^ 1) for i in range(n_data)])
    both = mine + got.astype(F32)
    total = lax.dynamic_index_in_dim(both, chip, 0, keepdims=False)
    low = both.astype(BF16)
    for k in range(1, chips):
        piece = lax.dynamic_index_in_dim(low, (chip + k) % chips, 0, keepdims=False)
        total = total + chip_shift(piece, n_data, k).astype(F32)
    return total.astype(BF16)


def per_device(
    tokens, cotangent, left_factor, right_factor, block_values, block_rows, block_cols, block_counts
):
    n_fsdp = lax.axis_size("fsdp")
    n_tensor = lax.axis_size("tensor")
    n_data = lax.axis_size("dp")
    f_index = lax.axis_index("fsdp")
    t_index = lax.axis_index("tensor")
    d_index = lax.axis_index("dp")
    maxb = block_values.shape[0]
    tok_rows, features = tokens.shape
    right = right_factor.reshape(right_factor.shape[0], -1)
    rank_size, quarter = right.shape
    q_blocks = quarter // SIDE
    r_part = rank_size // n_tensor
    counts = block_counts.reshape(n_fsdp, n_tensor)[:, t_index]
    live = counts[f_index]

    chunk = features // n_tensor
    my_tok = lax.dynamic_slice_in_dim(tokens, t_index * chunk, chunk, 1)
    all_tok = lax.all_gather(my_tok, ("fsdp", "tensor"), axis=0)
    per = maxb // n_data
    my_vals = lax.dynamic_slice_in_dim(block_values, d_index * per, per, 0)
    all_vals = lax.all_gather(my_vals, ("fsdp", "dp"), axis=0, tiled=True)
    places = lax.all_gather(jnp.stack([block_rows, block_cols]), "fsdp", axis=0)
    all_rows = places[:, 0].reshape(-1)
    all_cols = places[:, 1].reshape(-1)

    left_part = lax.dynamic_slice_in_dim(left_factor, t_index * r_part, r_part, 1)
    rank_part = jnp.dot(tokens, left_part, preferred_element_type=F32)
    rank_low = rank_part.astype(BF16)
    for k in range(1, n_fsdp):
        rank_part = rank_part + shift(rank_low, "fsdp", n_fsdp, k).astype(F32)
    rank_t = rank_part.astype(BF16)
    rank = lax.all_gather(rank_t, "tensor", axis=1, tiled=True)

    my_cot = lax.dynamic_slice_in_dim(cotangent, f_index * quarter, quarter, 1)
    back_all = jnp.einsum("tq,rq->tr", my_cot, right, preferred_element_type=F32)
    back_sum = lax.dynamic_slice_in_dim(back_all, t_index * r_part, r_part, 1)
    back_low = back_all.astype(BF16)
    for k in range(1, n_tensor):
        piece = lax.dynamic_slice_in_dim(back_low, ((t_index + k) % n_tensor) * r_part, r_part, 1)
        back_sum = back_sum + shift(piece, "tensor", n_tensor, k).astype(F32)
    back_low = back_sum.astype(BF16)
    for k in range(1, n_fsdp):
        back_sum = back_sum + shift(back_low, "fsdp", n_fsdp, k).astype(F32)
    back = back_sum.astype(BF16)

    grads = block_grads(live.reshape(1), block_rows, block_cols, tokens, cotangent)
    block_part = scatter_dp(grads, n_data, d_index)
    out_blocks = lax.all_gather(block_part, "dp", axis=0, tiled=True)

    grad_right = jnp.einsum("tr,tq->rq", rank, my_cot, preferred_element_type=F32)
    right_part = scatter_dp(grad_right, n_data, d_index)
    out_right = lax.all_gather(right_part, "dp", axis=0, tiled=True).reshape(right_factor.shape)

    grad_left = jnp.einsum("tf,tr->fr", tokens, back, preferred_element_type=F32)
    left_part = scatter_dp(grad_left, n_data, d_index)
    left_all = lax.all_gather(left_part, ("dp", "tensor"), axis=0)
    left_all = left_all.reshape(n_data, n_tensor, features // n_data, r_part)
    out_left = jnp.transpose(left_all, (0, 2, 1, 3)).reshape(features, rank_size)

    info = jnp.concatenate([counts, f_index.reshape(1)]).astype(jnp.int32)
    mixed = mixed_product(
        info, all_rows, all_cols, rank, right, all_tok, all_vals, maxb, q_blocks
    ).reshape(tok_rows, 1, quarter)
    return (mixed, out_left, out_right, out_blocks)


def solution(mesh):
    return jax.shard_map(
        per_device,
        mesh=mesh,
        in_specs=(
            P("dp", "fsdp"),
            P("dp", "tensor"),
            P("fsdp", None),
            P(None, "tensor", "fsdp"),
            P(("fsdp", "tensor"), None, None),
            P(("fsdp", "tensor")),
            P(("fsdp", "tensor")),
            P(),
        ),
        out_specs=(
            P("dp", "tensor", "fsdp"),
            P("fsdp", None),
            P(None, "tensor", "fsdp"),
            P(("fsdp", "tensor"), None, None),
        ),
        check_vma=False,
    )
```

```python
import jax
import jax.numpy as jnp
from jax import lax
from jax.experimental import pallas as pl
from jax.experimental.pallas import tpu as pltpu
from jax.sharding import PartitionSpec as P

F32 = jnp.float32
BF16 = jnp.bfloat16
SIDE = 128
SMEM = pl.BlockSpec(memory_space=pltpu.SMEM)
VMEM = pl.BlockSpec(memory_space=pltpu.VMEM)
HBM = pl.BlockSpec(memory_space=pl.ANY)


def lanes(block):
    return pl.ds(pl.multiple_of(block * SIDE, SIDE), SIDE)


def params(mib):
    return pltpu.CompilerParams(vmem_limit_bytes=mib << 20)


def shape(dims, dtype):
    return jax.ShapeDtypeStruct(dims, dtype)


def cost(flops, nbytes):
    return pl.CostEstimate(flops=int(flops), bytes_accessed=int(nbytes), transcendentals=0)


def far_kernel(
    n_f, q_blocks, info, rows, cols, tok, vals, left, top, bottom, part, part_low, acc
):
    quarter = lax.rem(info[1] + n_f // 2, n_f)
    acc[...] = jnp.zeros_like(acc)

    def body(s, carry):
        col = cols[s]

        @pl.when(col // q_blocks == quarter)
        def _():
            acc[:, lanes(col - quarter * q_blocks)] += jnp.dot(
                tok[:, lanes(rows[s])], vals[s], preferred_element_type=F32
            )

        return carry

    lax.fori_loop(0, info[0], body, 0)
    half = top.shape[0]
    top[...] = acc[:half].astype(BF16)
    bottom[...] = acc[half:].astype(BF16)
    rank = jnp.dot(tok[...], left[:, lanes(info[2])], preferred_element_type=F32)
    part[...] = rank
    part_low[...] = rank.astype(BF16)


def near_kernel(
    n_f, q_blocks, info, rows, cols, tok, vals, p1t, p1b, p3t, p3b, p0, acc
):
    acc[...] = jnp.zeros_like(acc)
    p0[...] = jnp.zeros_like(p0)

    def body(s, carry):
        col = cols[s]
        q = col // q_blocks
        k = lax.rem(q - info[1] + n_f, n_f)
        here = lanes(col - q * q_blocks)

        @pl.when(k != n_f // 2)
        def _():
            prod = jnp.dot(tok[:, lanes(rows[s])], vals[s], preferred_element_type=F32)

            @pl.when(k == 0)
            def _():
                p0[:, here] += prod

            @pl.when(k != 0)
            def _():
                acc[k // 2, :, here] += prod

        return carry

    lax.fori_loop(0, info[0], body, 0)
    half = p1t.shape[0]
    p1t[...] = acc[0, :half]
    p1b[...] = acc[0, half:].astype(BF16)
    p3t[...] = acc[1, :half].astype(BF16)
    p3b[...] = acc[1, half:]


def back_kernel(n_t, info, cot, right, own, s1, s2, s3, cotq, full, sem):
    quarter = cotq.shape[1]
    src = cot.at[:, pl.ds(pl.multiple_of(info[1] * quarter, SIDE), quarter)]
    copy = pltpu.make_async_copy(src, cotq, sem)
    copy.start()
    copy.wait()
    full[...] = lax.dot_general(
        cotq[...], right[...], (((1,), (1,)), ((), ())), preferred_element_type=F32
    )
    own[...] = full[:, lanes(info[2])]
    for k, out in ((1, s1), (2, s2), (3, s3)):
        out[...] = full[:, lanes(lax.rem(info[2] + k, n_t))].astype(BF16)


def blocks_kernel(chips, info, rows, cols, tok, cot, mine, theirs):
    mine[...] = jnp.zeros_like(mine)
    theirs[...] = jnp.zeros_like(theirs)
    per = mine.shape[1]

    def body(s, carry):
        grad = lax.dot_general(
            tok[:, lanes(rows[s])],
            cot[:, lanes(cols[s])],
            (((0,), (0,)), ((), ())),
            preferred_element_type=F32,
        )
        owner = s // per
        j = lax.rem(owner // 2 - info[3] + chips, chips)
        at = lax.rem(s, per)
        keep = lax.rem(owner, 2) == info[4]

        @pl.when(keep)
        def _():
            mine[j, at] = grad

        @pl.when(jnp.logical_not(keep))
        def _():
            theirs[j, at] = grad.astype(BF16)

        return carry

    lax.fori_loop(0, info[0], body, 0)


def factors_kernel(
    n_t, chips, info, tok, cot, g0, g1, g2, g3, back,
    m0, m1, m2, m3, theirs, cotq, left, right, sem,
):
    quarter = cotq.shape[1]
    src = cot.at[:, pl.ds(pl.multiple_of(info[1] * quarter, SIDE), quarter)]
    copy = pltpu.make_async_copy(src, cotq, sem)
    copy.start()
    left[...] = lax.dot_general(
        back[...], tok[...], (((0,), (0,)), ((), ())), preferred_element_type=F32
    ).T
    copy.wait()
    for k, g in enumerate((g0, g1, g2, g3)):
        row = pl.multiple_of(lax.rem(info[2] - k + n_t, n_t) * SIDE, SIDE)
        right[pl.ds(row, SIDE), :] = lax.dot_general(
            g[...], cotq[...], (((0,), (0,)), ((), ())), preferred_element_type=F32
        )
    n_l = left.shape[0] // (2 * chips)
    n_r = right.shape[0] // (2 * chips)
    for j, mine in enumerate((m0, m1, m2, m3)):
        chip = lax.rem(info[3] + j, chips)
        for core, out in ((info[4], mine), (1 - info[4], theirs.at[j])):
            at = chip * 2 + core
            out[:n_l] = left[pl.ds(pl.multiple_of(at * n_l, n_l), n_l), :].astype(out.dtype)
            for p in range(quarter // SIDE):
                out[n_l + p * n_r : n_l + (p + 1) * n_r] = right[
                    pl.ds(pl.multiple_of(at * n_r, n_r), n_r), p * SIDE : (p + 1) * SIDE
                ].astype(out.dtype)


def finish_kernel(n_t, info, g0, g1, g2, g3, right, p0, at, ab, bt, bb, out):
    i = pl.program_id(0)
    acc = p0[...]
    for k, g in enumerate((g0, g1, g2, g3)):
        row = pl.multiple_of(lax.rem(info[2] - k + n_t, n_t) * SIDE, SIDE)
        acc += jnp.dot(g[...], right[pl.ds(row, SIDE), :], preferred_element_type=F32)

    @pl.when(i < pl.num_programs(0) // 2)
    def _():
        out[...] = (acc + at[...].astype(F32) + bt[...].astype(F32)).astype(BF16)

    @pl.when(i >= pl.num_programs(0) // 2)
    def _():
        out[...] = (acc + ab[...].astype(F32) + bb[...].astype(F32)).astype(BF16)


def spread_kernel(n_t, chips, n_l, n_r, *refs):
    info, ours, partner, left, right, blocks, sem = refs
    quarter = right.shape[1]
    panels = quarter // SIDE
    copies = []
    for who, src in ((info[4], ours), (1 - info[4], partner)):
        for j in range(chips):
            at = lax.rem(info[3] - j + chips, chips) * 2 + who
            for k in range(n_t):
                col = lax.rem(info[2] - k + n_t, n_t)
                dst = left.at[pl.ds(pl.multiple_of(at * n_l, n_l), n_l), lanes(col)]
                copies.append((src.at[j, pl.ds(k * n_l, n_l)], dst))
            base = n_t * n_l
            for p in range(panels):
                dst = right.at[
                    pl.ds(pl.multiple_of(at * n_r, n_r), n_r), pl.ds(p * SIDE, SIDE)
                ]
                copies.append((src.at[j, pl.ds(base + p * n_r, n_r)], dst))
            base += panels * n_r
            per = blocks.shape[0] // (2 * chips * SIDE) * SIDE
            dst = blocks.at[pl.ds(pl.multiple_of(at * per, per), per)]
            copies.append((src.at[j, pl.ds(base, per)], dst))
    for src, dst in copies:
        dst[...] = src[...]


def shift(x, axis, n, k):
    return lax.ppermute(x, axis, [(i, (i + k) % n) for i in range(n)])


def chip_shift(x, n_data, k):
    chips = n_data // 2
    perm = [(2 * a + c, 2 * ((a + k) % chips) + c) for a in range(chips) for c in range(2)]
    return lax.ppermute(x, "dp", perm)


def core_swap(x, n_data):
    return lax.ppermute(x, "dp", [(i, i ^ 1) for i in range(n_data)])


def scatter_chips(mine, got, n_data):
    chips = n_data // 2
    total = mine[0] + got[0].astype(F32)
    for k in range(1, chips):
        piece = (mine[k] + got[k].astype(F32)).astype(BF16)
        total = total + chip_shift(piece, n_data, k).astype(F32)
    return total.astype(BF16)


def per_device(
    tokens, cotangent, left_factor, right_factor, block_values, block_rows, block_cols, block_counts
):
    n_fsdp = lax.axis_size("fsdp")
    n_tensor = lax.axis_size("tensor")
    n_data = lax.axis_size("dp")
    f_index = lax.axis_index("fsdp")
    t_index = lax.axis_index("tensor")
    d_index = lax.axis_index("dp")
    chips = n_data // 2
    maxb = block_values.shape[0]
    tok_rows, features = tokens.shape
    right = right_factor.reshape(right_factor.shape[0], -1)
    rank_size, quarter = right.shape
    q_blocks = quarter // SIDE
    r_part = rank_size // n_tensor
    half = tok_rows // 2
    live = block_counts[f_index * n_tensor + t_index]
    info = jnp.stack([live, f_index, t_index, d_index // 2, d_index % 2]).astype(jnp.int32)
    block_flops = 2 * tok_rows * SIDE * SIDE * maxb

    half_low = shape((half, quarter), BF16)
    half_wide = shape((half, quarter), F32)
    part = shape((tok_rows, r_part), F32)
    part_low = shape((tok_rows, r_part), BF16)
    p2t, p2b, rank_part, rank_low = pl.pallas_call(
        lambda *refs: far_kernel(n_fsdp, q_blocks, *refs),
        out_shape=(half_low, half_low, part, part_low),
        in_specs=[SMEM, SMEM, SMEM, VMEM, VMEM, VMEM],
        out_specs=(VMEM,) * 4,
        scratch_shapes=[pltpu.VMEM((tok_rows, quarter), F32)],
        cost_estimate=cost(block_flops / 2, 8 << 20),
        compiler_params=params(32),
    )(info, block_rows, block_cols, tokens, block_values, left_factor)
    in_t = shift(p2t, "fsdp", n_fsdp, 1)
    in_b = shift(p2b, "fsdp", n_fsdp, -1)
    for k in range(1, n_fsdp):
        rank_part = rank_part + shift(rank_low, "fsdp", n_fsdp, k).astype(F32)
    rank_t = rank_part.astype(BF16)
    ranks = [rank_t] + [shift(rank_t, "tensor", n_tensor, k) for k in range(1, n_tensor)]

    back_sum, b1, b2, b3 = pl.pallas_call(
        lambda *refs: back_kernel(n_tensor, *refs),
        out_shape=(part, part_low, part_low, part_low),
        in_specs=[SMEM, HBM, VMEM],
        out_specs=(VMEM,) * 4,
        scratch_shapes=[
            pltpu.VMEM((tok_rows, quarter), BF16),
            pltpu.VMEM((tok_rows, rank_size), F32),
            pltpu.SemaphoreType.DMA,
        ],
        cost_estimate=cost(2 * tok_rows * quarter * rank_size, 6 << 20),
        compiler_params=params(24),
    )(info, cotangent, right)
    for k, b in ((1, b1), (2, b2), (3, b3)):
        back_sum = back_sum + shift(b, "tensor", n_tensor, k).astype(F32)
    back_low = back_sum.astype(BF16)
    for k in range(1, n_fsdp):
        back_sum = back_sum + shift(back_low, "fsdp", n_fsdp, k).astype(F32)
    back = back_sum.astype(BF16)

    p1t, p1b, p3t, p3b, p0 = pl.pallas_call(
        lambda *refs: near_kernel(n_fsdp, q_blocks, *refs),
        out_shape=(half_wide, half_low, half_low, half_wide, shape((tok_rows, quarter), F32)),
        in_specs=[SMEM, SMEM, SMEM, VMEM, VMEM],
        out_specs=(VMEM,) * 5,
        scratch_shapes=[pltpu.VMEM((2, tok_rows, quarter), F32)],
        cost_estimate=cost(block_flops, 15 << 20),
        compiler_params=params(40),
    )(info, block_rows, block_cols, tokens, block_values)
    ab = shift(p1b, "fsdp", n_fsdp, 1)
    bt = shift(p3t, "fsdp", n_fsdp, -1)
    at = shift((p1t + in_t.astype(F32)).astype(BF16), "fsdp", n_fsdp, 1)
    bb = shift((p3b + in_b.astype(F32)).astype(BF16), "fsdp", n_fsdp, -1)

    per = maxb // n_data
    blocks_mine, blocks_theirs = pl.pallas_call(
        lambda *refs: blocks_kernel(chips, *refs),
        out_shape=(
            shape((chips, per, SIDE, SIDE), F32),
            shape((chips, per, SIDE, SIDE), BF16),
        ),
        in_specs=[SMEM, SMEM, SMEM, VMEM, VMEM],
        out_specs=(VMEM,) * 2,
        cost_estimate=cost(block_flops, 15 << 20),
        compiler_params=params(40),
    )(info, block_rows, block_cols, tokens, cotangent)
    blocks_got = core_swap(blocks_theirs, n_data)
    block_part = scatter_chips(blocks_mine, blocks_got, n_data).reshape(per * SIDE, SIDE)

    n_l = features // n_data
    n_r = rank_size // n_data
    rows_lr = n_l + q_blocks * n_r
    wide = shape((rows_lr, SIDE), F32)
    m0, m1, m2, m3, theirs = pl.pallas_call(
        lambda *refs: factors_kernel(n_tensor, chips, *refs),
        out_shape=(wide,) * 4 + (shape((chips, rows_lr, SIDE), BF16),),
        in_specs=[SMEM, VMEM, HBM] + [VMEM] * 5,
        out_specs=(VMEM,) * 5,
        scratch_shapes=[
            pltpu.VMEM((tok_rows, quarter), BF16),
            pltpu.VMEM((features, r_part), F32),
            pltpu.VMEM((rank_size, quarter), F32),
            pltpu.SemaphoreType.DMA,
        ],
        cost_estimate=cost(2 * tok_rows * (quarter * rank_size + features * r_part), 10 << 20),
        compiler_params=params(40),
    )(info, tokens, cotangent, *ranks, back)
    got = core_swap(theirs, n_data)
    chunk = scatter_chips((m0, m1, m2, m3), got, n_data)
    left_own = chunk[:n_l]
    lefts = [left_own] + [shift(left_own, "tensor", n_tensor, k) for k in range(1, n_tensor)]
    message = jnp.concatenate(lefts + [chunk[n_l:], block_part], axis=0)
    ours = jnp.stack([message] + [chip_shift(message, n_data, k) for k in range(1, chips)])
    partner = core_swap(ours, n_data)
    out_left, out_right, out_blocks = pl.pallas_call(
        lambda *refs: spread_kernel(n_tensor, chips, n_l, n_r, *refs),
        out_shape=(
            shape((features, rank_size), BF16),
            shape((rank_size, quarter), BF16),
            shape((maxb * SIDE, SIDE), BF16),
        ),
        in_specs=[SMEM, VMEM, VMEM],
        out_specs=(VMEM,) * 3,
        scratch_shapes=[pltpu.SemaphoreType.DMA],
        cost_estimate=cost(0, 10 << 20),
        compiler_params=params(32),
    )(info, ours, partner)

    steps = 4
    block = tok_rows // steps
    whole = lambda dims: pl.BlockSpec(dims, lambda i: (0, 0))
    by_row = lambda width: pl.BlockSpec((block, width), lambda i: (i, 0))
    first = pl.BlockSpec((block, quarter), lambda i: (jnp.minimum(i, steps // 2 - 1), 0))
    last = pl.BlockSpec((block, quarter), lambda i: (jnp.maximum(i - steps // 2, 0), 0))
    mixed = pl.pallas_call(
        lambda *refs: finish_kernel(n_tensor, *refs),
        out_shape=shape((tok_rows, quarter), BF16),
        grid=(steps,),
        in_specs=[SMEM] + [by_row(r_part)] * 4
        + [whole((rank_size, quarter)), by_row(quarter), first, last, first, last],
        out_specs=by_row(quarter),
        cost_estimate=cost(2 * tok_rows * quarter * rank_size, 14 << 20),
        compiler_params=params(32),
    )(info, *ranks, right, p0, at, ab, bt, bb)
    return (
        mixed.reshape(tok_rows, 1, quarter),
        out_left,
        out_right.reshape(right_factor.shape),
        out_blocks.reshape(maxb, SIDE, SIDE),
    )


def solution(mesh):
    return jax.shard_map(
        per_device,
        mesh=mesh,
        in_specs=(
            P("dp", "fsdp"),
            P("dp", "tensor"),
            P("fsdp", None),
            P(None, "tensor", "fsdp"),
            P(("fsdp", "tensor"), None, None),
            P(("fsdp", "tensor")),
            P(("fsdp", "tensor")),
            P(),
        ),
        out_specs=(
            P("dp", "tensor", "fsdp"),
            P("fsdp", None),
            P(None, "tensor", "fsdp"),
            P(("fsdp", "tensor"), None, None),
        ),
        check_vma=False,
    )
```

```python
import jax
import jax.numpy as jnp
from jax import lax
from jax.experimental import pallas as pl
from jax.experimental.pallas import tpu as pltpu
from jax.sharding import PartitionSpec as P

F32 = jnp.float32
BF16 = jnp.bfloat16
SIDE = 128
SMEM = pl.BlockSpec(memory_space=pltpu.SMEM)
VMEM = pl.BlockSpec(memory_space=pltpu.VMEM)
HBM = pl.BlockSpec(memory_space=pl.ANY)


def lanes(block):
    return pl.ds(pl.multiple_of(block * SIDE, SIDE), SIDE)


def sublanes(block, size):
    return pl.ds(pl.multiple_of(block * size, size), size)


def shape(dims, dtype):
    return jax.ShapeDtypeStruct(dims, dtype)


def call(kernel, outs, smem, vmem, scratch=(), after=None, flops=0, mib=40):
    tokens = () if after is None else (after,)
    n_in, n_out = len(smem) + len(vmem), len(outs)

    def body(*refs):
        ins, rest = refs[:n_in], refs[n_in + len(tokens) :]
        rest[n_out][0] = 0
        kernel(*ins, *rest[:n_out], *rest[n_out + 1 :])

    nbytes = sum(a.size * a.dtype.itemsize for a in (*vmem, *outs))
    return pl.pallas_call(
        body,
        out_shape=(*outs, shape((1,), jnp.int32)),
        in_specs=[SMEM] * len(smem) + [VMEM] * len(vmem) + [SMEM] * len(tokens),
        out_specs=(VMEM,) * n_out + (SMEM,),
        scratch_shapes=list(scratch),
        cost_estimate=pl.CostEstimate(
            flops=0, bytes_accessed=0, transcendentals=0
        ),
        compiler_params=pltpu.CompilerParams(vmem_limit_bytes=mib << 20),
    )(*smem, *vmem, *tokens)


class Place:
    def __init__(self, n_f, n_t, n_d):
        self.n_f, self.n_t, self.n_d, self.chips = n_f, n_t, n_d, n_d // 2

    f = property(lambda self: lax.axis_index("fsdp"))
    t = property(lambda self: lax.axis_index("tensor"))
    chip = property(lambda self: lax.axis_index("dp") // 2)
    core = property(lambda self: lax.rem(lax.axis_index("dp"), 2))

    def live(self, counts):
        return counts[self.f * self.n_t + self.t]


def far_kernel(place, q_blocks, counts, rows, cols, tok, left, vals, top, bottom, part, low, acc):
    rank = jnp.dot(tok[...], left[:, lanes(place.t)], preferred_element_type=F32)
    part[...] = rank
    for k in range(place.n_f):
        low[k] = rank.astype(BF16)
    quarter = lax.rem(place.f + place.n_f // 2, place.n_f)
    acc[...] = jnp.zeros_like(acc)

    def body(s, carry):
        col = cols[s]

        @pl.when(col // q_blocks == quarter)
        def _():
            acc[:, lanes(col - quarter * q_blocks)] += jnp.dot(
                tok[:, lanes(rows[s])], vals[s], preferred_element_type=F32
            )

        return carry

    lax.fori_loop(0, place.live(counts), body, 0)
    half = top.shape[0]
    top[...] = acc[:half].astype(BF16)
    bottom[...] = acc[half:].astype(BF16)


def near_kernel(place, q_blocks, counts, rows, cols, tok, vals, p1t, p1b, p3t, p3b, p0, acc):
    acc[...] = jnp.zeros_like(acc)
    p0[...] = jnp.zeros_like(p0)
    n_f, f = place.n_f, place.f

    def body(s, carry):
        col = cols[s]
        q = col // q_blocks
        k = lax.rem(q - f + n_f, n_f)
        here = lanes(col - q * q_blocks)

        @pl.when(k != n_f // 2)
        def _():
            prod = jnp.dot(tok[:, lanes(rows[s])], vals[s], preferred_element_type=F32)

            @pl.when(k == 0)
            def _():
                p0[:, here] += prod

            @pl.when(k != 0)
            def _():
                acc[k // 2, :, here] += prod

        return carry

    lax.fori_loop(0, place.live(counts), body, 0)
    half = p1t.shape[0]
    p1t[...] = acc[0, :half]
    p1b[...] = acc[0, half:].astype(BF16)
    p3t[...] = acc[1, :half].astype(BF16)
    p3b[...] = acc[1, half:]


def back_kernel(place, cot, right, own, parts, full):
    quarter = right.shape[1]
    here = pl.ds(pl.multiple_of(place.f * quarter, SIDE), quarter)
    full[...] = lax.dot_general(
        cot[:, here], right[...], (((1,), (1,)), ((), ())), preferred_element_type=F32
    )
    own[...] = full[:, lanes(place.t)]
    for k in range(place.n_t):
        parts[k] = full[:, k * SIDE : (k + 1) * SIDE].astype(BF16)


def blocks_kernel(place, counts, rows, cols, tok, cot, mine, theirs):
    mine[...] = jnp.zeros_like(mine)
    theirs[...] = jnp.zeros_like(theirs)
    per = mine.shape[1] // SIDE
    core = place.core

    def body(s, carry):
        grad = lax.dot_general(
            tok[:, lanes(rows[s])],
            cot[:, lanes(cols[s])],
            (((0,), (0,)), ((), ())),
            preferred_element_type=F32,
        )
        owner = s // per
        j = owner // 2
        at = sublanes(lax.rem(s, per), SIDE)
        keep = lax.rem(owner, 2) == core

        @pl.when(keep)
        def _():
            mine[j, at] = grad

        @pl.when(jnp.logical_not(keep))
        def _():
            theirs[j, at] = grad.astype(BF16)

        return carry

    lax.fori_loop(0, place.live(counts), body, 0)


def factors_kernel(place, tok, cot, ranks, back_part, back_in, mine, theirs, left, right):
    quarter = right.shape[1]
    here = pl.ds(pl.multiple_of(place.f * quarter, SIDE), quarter)
    back = back_part[...]
    for k in range(1, place.n_f):
        back = back + back_in[lax.rem(place.f + k, place.n_f)].astype(F32)
    left[...] = lax.dot_general(
        back.astype(BF16), tok[...], (((0,), (0,)), ((), ())), preferred_element_type=F32
    ).T
    for k in range(place.n_t):
        right[k * SIDE : (k + 1) * SIDE, :] = lax.dot_general(
            ranks[k], cot[:, here], (((0,), (0,)), ((), ())), preferred_element_type=F32
        )
    n_l = left.shape[0] // place.n_d
    n_r = right.shape[0] // place.n_d
    for chip in range(place.chips):
        for core, out in ((place.core, mine), (1 - place.core, theirs)):
            at = chip * 2 + core
            out[chip, :n_l] = left[sublanes(at, n_l), :].astype(out.dtype)
            for p in range(quarter // SIDE):
                out[chip, n_l + p * n_r : n_l + (p + 1) * n_r] = right[
                    sublanes(at, n_r), p * SIDE : (p + 1) * SIDE
                ].astype(out.dtype)


def cores_kernel(place, mine, got, own, parts):
    for k in range(place.chips):
        parts[k] = (mine[k] + got[k].astype(F32)).astype(BF16)
    own[...] = mine[place.chip] + got[place.chip].astype(F32)


def total_kernel(place, axis, own, got, *outs):
    n = got.shape[0]
    me = getattr(place, axis)
    total = own[...]
    for k in range(1, n):
        total = total + got[lax.rem(me + k, n)].astype(F32)
    row = 0
    for out in outs:
        if len(out.shape) == 2:
            out[...] = total.astype(out.dtype)
            continue
        for k in range(out.shape[0]):
            out[k] = total[row : row + out.shape[1]].astype(out.dtype)
        row += out.shape[1]


def copies_kernel(parts, out):
    rows = parts.shape[1]
    for k in range(out.shape[0]):
        for p in range(parts.shape[0]):
            out[k, p * rows : (p + 1) * rows] = parts[p]


def add_kernel(a, x, b, y, a_out, b_out):
    a_out[...] = (a[...] + x[...].astype(F32)).astype(BF16)
    b_out[...] = (b[...] + y[...].astype(F32)).astype(BF16)


def low_kernel(place, ranks, right, p0, bottom, top, out):
    half = top.shape[0]
    acc = p0[...]
    for k in range(place.n_t):
        acc += jnp.dot(ranks[k], right[k * SIDE : (k + 1) * SIDE, :], preferred_element_type=F32)
    out[:half] = acc[:half] + top[...].astype(F32)
    out[half:] = acc[half:] + bottom[...].astype(F32)


def finish_kernel(pre, top, bottom, out):
    half = top.shape[0]
    out[:half] = (pre[:half] + top[...].astype(F32)).astype(BF16)
    out[half:] = (pre[half:] + bottom[...].astype(F32)).astype(BF16)


def spread_kernel(place, ours_l, theirs_l, ours_r, theirs_r, ours_b, theirs_b, left, right, blocks):
    n_l = left.shape[0] // place.n_d
    n_r = right.shape[0] // place.n_d
    n_b = blocks.shape[0] // place.n_d
    for core, src_l, src_r, src_b in (
        (place.core, ours_l, ours_r, ours_b),
        (1 - place.core, theirs_l, theirs_r, theirs_b),
    ):
        for chip in range(place.chips):
            at = chip * 2 + core
            for k in range(place.n_t):
                left[sublanes(at, n_l), k * SIDE : (k + 1) * SIDE] = src_l[
                    chip, k * n_l : (k + 1) * n_l
                ]
            for p in range(right.shape[1] // SIDE):
                right[sublanes(at, n_r), p * SIDE : (p + 1) * SIDE] = src_r[
                    chip, p * n_r : (p + 1) * n_r
                ]
            blocks[sublanes(at, n_b)] = src_b[chip]


def shift(x, axis, n, k):
    return lax.ppermute(x, axis, [(i, (i + k) % n) for i in range(n)])


def core_swap(x, n_data):
    return lax.ppermute(x, "dp", [(i, i ^ 1) for i in range(n_data)])


def exchange(x, axis):
    return lax.all_to_all(x, axis, 0, 0, tiled=True)


def chip_exchange(x, n_data):
    groups = [[c + 2 * a for a in range(n_data // 2)] for c in range(2)]
    return lax.all_to_all(x, "dp", 0, 0, axis_index_groups=groups, tiled=True)


def per_device(
    tokens, cotangent, left_factor, right_factor, block_values, block_rows, block_cols, block_counts
):
    n_f = lax.axis_size("fsdp")
    n_t = lax.axis_size("tensor")
    n_d = lax.axis_size("dp")
    place = Place(n_f, n_t, n_d)
    chips = n_d // 2
    maxb = block_values.shape[0]
    tok_rows, features = tokens.shape
    right = right_factor.reshape(right_factor.shape[0], -1)
    rank_size, quarter = right.shape
    q_blocks = quarter // SIDE
    r_part = rank_size // n_t
    half = tok_rows // 2
    lists = (block_counts, block_rows, block_cols)
    block_flops = 2 * tok_rows * SIDE * SIDE * maxb

    def bind(kernel, *args):
        return lambda *refs: kernel(place, *args, *refs)

    half_low = shape((half, quarter), BF16)
    half_wide = shape((half, quarter), F32)
    part = shape((tok_rows, r_part), F32)
    parts_f = shape((n_f, tok_rows, r_part), BF16)
    parts_t = shape((n_t, tok_rows, r_part), BF16)

    p2t, p2b, rank_part, rank_low, step = call(
        bind(far_kernel, q_blocks),
        (half_low, half_low, part, parts_f),
        lists,
        (tokens, left_factor, block_values),
        [pltpu.VMEM((tok_rows, quarter), F32)],
        flops=block_flops,
    )
    rank_in = exchange(rank_low, "fsdp")
    in_t = shift(p2t, "fsdp", n_f, 1)
    in_b = shift(p2b, "fsdp", n_f, -1)

    back_part, back_out, step = call(
        bind(back_kernel),
        (part, parts_t),
        (),
        (cotangent, right),
        [pltpu.VMEM((tok_rows, rank_size), F32)],
        after=step,
        flops=2 * tok_rows * quarter * rank_size,
    )
    back_in = exchange(back_out, "tensor")

    p1t, p1b, p3t, p3b, p0, step = call(
        bind(near_kernel, q_blocks),
        (half_wide, half_low, half_low, half_wide, shape((tok_rows, quarter), F32)),
        lists,
        (tokens, block_values),
        [pltpu.VMEM((2, tok_rows, quarter), F32)],
        after=step,
        flops=block_flops,
    )
    ab = shift(p1b, "fsdp", n_f, 1)
    bt = shift(p3t, "fsdp", n_f, -1)

    rank_out, step = call(
        bind(total_kernel, "f"), (parts_t,), (), (rank_part, rank_in), after=step
    )
    ranks = exchange(rank_out, "tensor")
    back_part, back_out, step = call(
        bind(total_kernel, "t"), (part, parts_f), (), (back_part, back_in), after=step
    )
    back_in = exchange(back_out, "fsdp")

    n_b = maxb // n_d * SIDE
    blocks_mine, blocks_theirs, step = call(
        bind(blocks_kernel),
        (shape((chips, n_b, SIDE), F32), shape((chips, n_b, SIDE), BF16)),
        lists,
        (tokens, cotangent),
        after=step,
        flops=block_flops,
    )
    blocks_got = core_swap(blocks_theirs, n_d)

    n_l = features // n_d
    n_r = rank_size // n_d
    n_lr = n_l + q_blocks * n_r
    mine, theirs, step = call(
        bind(factors_kernel),
        (shape((chips, n_lr, SIDE), F32), shape((chips, n_lr, SIDE), BF16)),
        (),
        (tokens, cotangent, ranks, back_part, back_in),
        [pltpu.VMEM((features, r_part), F32), pltpu.VMEM((rank_size, quarter), F32)],
        after=step,
        flops=2 * tok_rows * (quarter * rank_size + features * r_part),
    )
    got = core_swap(theirs, n_d)

    block_own, block_out, step = call(
        bind(cores_kernel),
        (shape((n_b, SIDE), F32), shape((chips, n_b, SIDE), BF16)),
        (),
        (blocks_mine, blocks_got),
        after=step,
    )
    block_in = chip_exchange(block_out, n_d)
    own, out, step = call(
        bind(cores_kernel),
        (shape((n_lr, SIDE), F32), shape((chips, n_lr, SIDE), BF16)),
        (),
        (mine, got),
        after=step,
    )
    lr_in = chip_exchange(out, n_d)
    at_out, bb_out, step = call(
        add_kernel, (half_low, half_low), (), (p1t, in_t, p3b, in_b), after=step
    )
    at = shift(at_out, "fsdp", n_f, 1)
    bb = shift(bb_out, "fsdp", n_f, -1)
    block_copies, step = call(
        bind(total_kernel, "chip"),
        (shape((chips, n_b, SIDE), BF16),),
        (),
        (block_own, block_in),
        after=step,
    )
    blocks_ours = chip_exchange(block_copies, n_d)
    left_copies, right_copies, step = call(
        bind(total_kernel, "chip"),
        (shape((n_t, n_l, SIDE), BF16), shape((chips, q_blocks * n_r, SIDE), BF16)),
        (),
        (own, lr_in),
        after=step,
    )
    right_ours = chip_exchange(right_copies, n_d)
    lefts = exchange(left_copies, "tensor")
    left_copies, step = call(
        copies_kernel, (shape((chips, n_t * n_l, SIDE), BF16),), (), (lefts,), after=step
    )
    left_ours = chip_exchange(left_copies, n_d)
    pre, step = call(
        bind(low_kernel),
        (shape((tok_rows, quarter), F32),),
        (),
        (ranks, right, p0, ab, bt),
        after=step,
        flops=2 * tok_rows * quarter * rank_size,
    )
    blocks_theirs = core_swap(blocks_ours, n_d)
    right_theirs = core_swap(right_ours, n_d)
    left_theirs = core_swap(left_ours, n_d)
    mixed, step = call(
        finish_kernel, (shape((tok_rows, quarter), BF16),), (), (pre, at, bb), after=step
    )
    out_left, out_right, out_blocks, _ = call(
        bind(spread_kernel),
        (
            shape((features, rank_size), BF16),
            shape((rank_size, quarter), BF16),
            shape((maxb * SIDE, SIDE), BF16),
        ),
        (),
        (left_ours, left_theirs, right_ours, right_theirs, blocks_ours, blocks_theirs),
    )
    return (
        mixed.reshape(tok_rows, 1, quarter),
        out_left,
        out_right.reshape(right_factor.shape),
        out_blocks.reshape(maxb, SIDE, SIDE),
    )


def solution(mesh):
    return jax.shard_map(
        per_device,
        mesh=mesh,
        in_specs=(
            P("dp", "fsdp"),
            P("dp", "tensor"),
            P("fsdp", None),
            P(None, "tensor", "fsdp"),
            P(("fsdp", "tensor"), None, None),
            P(("fsdp", "tensor")),
            P(("fsdp", "tensor")),
            P(),
        ),
        out_specs=(
            P("dp", "tensor", "fsdp"),
            P("fsdp", None),
            P(None, "tensor", "fsdp"),
            P(("fsdp", "tensor"), None, None),
        ),
        check_vma=False,
    )
```

```python
import jax
import jax.numpy as jnp
from jax import lax
from jax.experimental import pallas as pl
from jax.experimental.pallas import tpu as pltpu
from jax.sharding import PartitionSpec as P

F32 = jnp.float32
BF16 = jnp.bfloat16
SIDE = 128
SMEM = pl.BlockSpec(memory_space=pltpu.SMEM)
VMEM = pl.BlockSpec(memory_space=pltpu.VMEM)
HBM = pl.BlockSpec(memory_space=pl.ANY)


def lanes(block):
    return pl.ds(pl.multiple_of(block * SIDE, SIDE), SIDE)


def sublanes(block, size):
    return pl.ds(pl.multiple_of(block * size, size), size)


def shape(dims, dtype):
    return jax.ShapeDtypeStruct(dims, dtype)


def call(kernel, outs, smem, vmem, scratch=(), flops=0, mib=8, hbm_outs=0):
    nbytes = sum(a.size * a.dtype.itemsize for a in (*vmem, *outs))
    return pl.pallas_call(
        kernel,
        out_shape=tuple(outs),
        in_specs=[SMEM] * len(smem) + [VMEM] * len(vmem),
        out_specs=(HBM,) * hbm_outs + (VMEM,) * (len(outs) - hbm_outs),
        scratch_shapes=list(scratch),
        cost_estimate=pl.CostEstimate(
            flops=int(flops), bytes_accessed=int(nbytes), transcendentals=0
        ),
        compiler_params=pltpu.CompilerParams(vmem_limit_bytes=mib << 20),
    )(*smem, *vmem)


class Place:
    def __init__(self, n_f, n_t, n_d):
        self.n_f, self.n_t, self.n_d, self.chips = n_f, n_t, n_d, n_d // 2

    f = property(lambda self: lax.axis_index("fsdp"))
    t = property(lambda self: lax.axis_index("tensor"))
    chip = property(lambda self: lax.axis_index("dp") // 2)
    core = property(lambda self: lax.rem(lax.axis_index("dp"), 2))

    def live(self, counts):
        return counts[self.f * self.n_t + self.t]


def first_kernel(
    place, q_blocks, counts, rows, cols, tok, left, vals, sums, part, low, acc, stage, sems
):
    rank = jnp.dot(tok[...], left[:, lanes(place.t)], preferred_element_type=F32)
    part[...] = rank
    low[...] = rank.astype(BF16)
    live = place.live(counts)
    copies = []
    for quarter in range(place.n_f):
        acc[...] = jnp.zeros_like(acc)

        def body(s, carry):
            col = cols[s] - quarter * q_blocks

            @pl.when((col >= 0) & (col < q_blocks))
            def _():
                acc[:, lanes(col)] += jnp.dot(
                    tok[:, lanes(rows[s])], vals[s], preferred_element_type=F32
                )

            return carry

        lax.fori_loop(0, live, body, 0)
        slot = quarter % 2
        if quarter >= 2:
            copies[quarter - 2].wait()
        stage[slot] = acc[...].astype(BF16)
        copies.append(pltpu.make_async_copy(stage.at[slot], sums.at[quarter], sems.at[slot]))
        copies[-1].start()
    for copy in copies[-2:]:
        copy.wait()


def back_kernel(place, cot, right, own, s1, s2, s3, full):
    quarter = right.shape[1]
    here = pl.ds(pl.multiple_of(place.f * quarter, SIDE), quarter)
    full[...] = lax.dot_general(
        cot[:, here], right[...], (((1,), (1,)), ((), ())), preferred_element_type=F32
    )
    own[...] = full[:, lanes(place.t)]
    for k, out in ((1, s1), (2, s2), (3, s3)):
        out[...] = full[:, lanes(lax.rem(place.t + k, place.n_t))].astype(BF16)


def blocks_kernel(place, counts, rows, cols, tok, cot, mine, theirs):
    mine[...] = jnp.zeros_like(mine)
    theirs[...] = jnp.zeros_like(theirs)
    per = mine.shape[1] // SIDE
    chip, core = place.chip, place.core

    def body(s, carry):
        grad = lax.dot_general(
            tok[:, lanes(rows[s])],
            cot[:, lanes(cols[s])],
            (((0,), (0,)), ((), ())),
            preferred_element_type=F32,
        )
        owner = s // per
        j = lax.rem(owner // 2 - chip + place.chips, place.chips)
        at = sublanes(lax.rem(s, per), SIDE)
        keep = lax.rem(owner, 2) == core

        @pl.when(keep)
        def _():
            mine[j, at] = grad

        @pl.when(jnp.logical_not(keep))
        def _():
            theirs[j, at] = grad.astype(BF16)

        return carry

    lax.fori_loop(0, place.live(counts), body, 0)


def factors_kernel(
    place, tok, cot, g0, g1, g2, g3, back, blocks_mine, blocks_theirs, mine, theirs, left, right
):
    quarter = right.shape[1]
    here = pl.ds(pl.multiple_of(place.f * quarter, SIDE), quarter)
    left[...] = lax.dot_general(
        back[...], tok[...], (((0,), (0,)), ((), ())), preferred_element_type=F32
    ).T
    for k, g in enumerate((g0, g1, g2, g3)):
        right[sublanes(lax.rem(place.t - k + place.n_t, place.n_t), SIDE), :] = lax.dot_general(
            g[...], cot[:, here], (((0,), (0,)), ((), ())), preferred_element_type=F32
        )
    n_l = left.shape[0] // place.n_d
    n_r = right.shape[0] // place.n_d
    n_lr = n_l + quarter // SIDE * n_r
    for j in range(place.chips):
        chip = lax.rem(place.chip + j, place.chips)
        for core, out in ((place.core, mine), (1 - place.core, theirs)):
            at = chip * 2 + core
            out[j, :n_l] = left[sublanes(at, n_l), :].astype(out.dtype)
            for p in range(quarter // SIDE):
                out[j, n_l + p * n_r : n_l + (p + 1) * n_r] = right[
                    sublanes(at, n_r), p * SIDE : (p + 1) * SIDE
                ].astype(out.dtype)
        mine[j, n_lr:] = blocks_mine[j]
        theirs[j, n_lr:] = blocks_theirs[j]


def cores_kernel(mine, got, own, *pieces):
    own[...] = mine[0] + got[0].astype(F32)
    for k, piece in enumerate(pieces):
        piece[...] = (mine[k + 1] + got[k + 1].astype(F32)).astype(BF16)


def total_kernel(n_in, *refs):
    total = refs[0][...]
    for r in refs[1:n_in]:
        total = total + r[...].astype(F32)
    row = 0
    for out in refs[n_in:]:
        out[...] = total[row : row + out.shape[0]].astype(BF16)
        row += out.shape[0]


def stack_kernel(*refs):
    out, rows = refs[-1], refs[0].shape[0]
    for k, part in enumerate(refs[:-1]):
        out[k * rows : (k + 1) * rows] = part[...]


def low_kernel(place, g0, g1, g2, g3, right, out):
    acc = jnp.zeros(out.shape, F32)
    for k, g in enumerate((g0, g1, g2, g3)):
        rows = sublanes(lax.rem(place.t - k + place.n_t, place.n_t), SIDE)
        acc += jnp.dot(g[...], right[rows, :], preferred_element_type=F32)
    out[...] = acc


def finish_kernel(low, residual, out):
    out[...] = (low[...] + residual[...].astype(F32)).astype(BF16)


def spread_kernel(place, ours_l, theirs_l, ours_r, theirs_r, left, right, blocks):
    n_l = left.shape[0] // place.n_d
    n_r = right.shape[0] // place.n_d
    n_b = blocks.shape[0] // place.n_d
    panels = right.shape[1] // SIDE
    for core, src_l, src_r in ((place.core, ours_l, ours_r), (1 - place.core, theirs_l, theirs_r)):
        for j in range(place.chips):
            at = lax.rem(place.chip - j + place.chips, place.chips) * 2 + core
            for k in range(place.n_t):
                col = lax.rem(place.t - k + place.n_t, place.n_t)
                left[sublanes(at, n_l), lanes(col)] = src_l[j, k * n_l : (k + 1) * n_l]
            for p in range(panels):
                right[sublanes(at, n_r), p * SIDE : (p + 1) * SIDE] = src_r[
                    j, p * n_r : (p + 1) * n_r
                ]
            blocks[sublanes(at, n_b)] = src_r[j, panels * n_r :]


def shift(x, axis, n, k):
    return lax.ppermute(x, axis, [(i, (i + k) % n) for i in range(n)])


def chip_shift(x, n_data, k):
    chips = n_data // 2
    perm = [(2 * a + c, 2 * ((a + k) % chips) + c) for a in range(chips) for c in range(2)]
    return lax.ppermute(x, "dp", perm)


def core_swap(x, n_data):
    return lax.ppermute(x, "dp", [(i, i ^ 1) for i in range(n_data)])


def per_device(
    tokens, cotangent, left_factor, right_factor, block_values, block_rows, block_cols, block_counts
):
    n_f = lax.axis_size("fsdp")
    n_t = lax.axis_size("tensor")
    n_d = lax.axis_size("dp")
    place = Place(n_f, n_t, n_d)
    chips = n_d // 2
    maxb = block_values.shape[0]
    tok_rows, features = tokens.shape
    right = right_factor.reshape(right_factor.shape[0], -1)
    rank_size, quarter = right.shape
    q_blocks = quarter // SIDE
    r_part = rank_size // n_t
    lists = (block_counts, block_rows, block_cols)
    block_flops = 2 * tok_rows * SIDE * SIDE * maxb

    def bind(kernel, *args):
        return lambda *refs: kernel(place, *args, *refs)

    def over(n, k_shift):
        return [k_shift(k) for k in range(1, n)]

    def total(parts, outs):
        n_in = len(parts)
        return call(lambda *refs: total_kernel(n_in, *refs), outs, (), parts)

    part = shape((tok_rows, r_part), F32)
    part_low = shape((tok_rows, r_part), BF16)

    sums, rank_part, rank_low = call(
        bind(first_kernel, q_blocks),
        (shape((n_f, tok_rows, quarter), BF16), part, part_low),
        lists,
        (tokens, left_factor, block_values),
        [
            pltpu.VMEM((tok_rows, quarter), F32),
            pltpu.VMEM((2, tok_rows, quarter), BF16),
            pltpu.SemaphoreType.DMA((2,)),
        ],
        flops=block_flops,
        mib=24,
        hbm_outs=1,
    )
    residual = lax.psum_scatter(sums, "fsdp", scatter_dimension=0, tiled=False)
    rank_in = over(n_f, lambda k: shift(rank_low, "fsdp", n_f, k))
    (rank_t,) = total((rank_part, *rank_in), (part_low,))
    ranks = [rank_t] + over(n_t, lambda k: shift(rank_t, "tensor", n_t, k))

    back_part, *back_out = call(
        bind(back_kernel),
        (part, part_low, part_low, part_low),
        (),
        (cotangent, right),
        [pltpu.VMEM((tok_rows, rank_size), F32)],
        flops=2 * tok_rows * quarter * rank_size,
        mib=16,
    )
    back_in = [shift(b, "tensor", n_t, k + 1) for k, b in enumerate(back_out)]
    back_sum = back_part
    for b in back_in:
        back_sum = back_sum + b.astype(F32)
    back_low = back_sum.astype(BF16)
    for b in over(n_f, lambda k: shift(back_low, "fsdp", n_f, k)):
        back_sum = back_sum + b.astype(F32)
    back = back_sum.astype(BF16)

    n_b = maxb // n_d * SIDE
    blocks_mine, blocks_theirs = call(
        bind(blocks_kernel),
        (shape((chips, n_b, SIDE), F32), shape((chips, n_b, SIDE), BF16)),
        lists,
        (tokens, cotangent),
        flops=block_flops,
        mib=20,
    )

    n_l = features // n_d
    n_r = rank_size // n_d
    n_rb = q_blocks * n_r + n_b
    mine, theirs = call(
        bind(factors_kernel),
        (shape((chips, n_l + n_rb, SIDE), F32), shape((chips, n_l + n_rb, SIDE), BF16)),
        (),
        (tokens, cotangent, *ranks, back, blocks_mine, blocks_theirs),
        [pltpu.VMEM((features, r_part), F32), pltpu.VMEM((rank_size, quarter), F32)],
        flops=2 * tok_rows * (quarter * rank_size + features * r_part),
        mib=28,
    )
    got = core_swap(theirs, n_d)
    own, *out = call(
        cores_kernel,
        (shape((n_l + n_rb, SIDE), F32),) + (shape((n_l + n_rb, SIDE), BF16),) * (chips - 1),
        (),
        (mine, got),
        mib=10,
    )
    pieces = [chip_shift(b, n_d, k + 1) for k, b in enumerate(out)]
    left_part, rest_part = total(
        (own, *pieces), (shape((n_l, SIDE), BF16), shape((n_rb, SIDE), BF16))
    )

    def gather_chips(x):
        return jnp.stack([x] + over(chips, lambda k: chip_shift(x, n_d, k)))

    lefts = [left_part] + over(n_t, lambda k: shift(left_part, "tensor", n_t, k))
    rest_ours = gather_chips(rest_part)
    rest_theirs = core_swap(rest_ours, n_d)
    (left_chunk,) = call(stack_kernel, (shape((n_t * n_l, SIDE), BF16),), (), lefts)
    left_ours = gather_chips(left_chunk)
    left_theirs = core_swap(left_ours, n_d)
    out_left, out_right, out_blocks = call(
        bind(spread_kernel),
        (
            shape((features, rank_size), BF16),
            shape((rank_size, quarter), BF16),
            shape((maxb * SIDE, SIDE), BF16),
        ),
        (),
        (left_ours, left_theirs, rest_ours, rest_theirs),
        mib=14,
    )
    (low,) = call(
        bind(low_kernel),
        (shape((tok_rows, quarter), F32),),
        (),
        (*ranks, right),
        flops=2 * tok_rows * quarter * rank_size,
        mib=16,
    )
    (mixed,) = call(
        finish_kernel, (shape((tok_rows, quarter), BF16),), (), (low, residual), mib=14
    )
    return (
        mixed.reshape(tok_rows, 1, quarter),
        out_left,
        out_right.reshape(right_factor.shape),
        out_blocks.reshape(maxb, SIDE, SIDE),
    )


def solution(mesh):
    return jax.shard_map(
        per_device,
        mesh=mesh,
        in_specs=(
            P("dp", "fsdp"),
            P("dp", "tensor"),
            P("fsdp", None),
            P(None, "tensor", "fsdp"),
            P(("fsdp", "tensor"), None, None),
            P(("fsdp", "tensor")),
            P(("fsdp", "tensor")),
            P(),
        ),
        out_specs=(
            P("dp", "tensor", "fsdp"),
            P("fsdp", None),
            P(None, "tensor", "fsdp"),
            P(("fsdp", "tensor"), None, None),
        ),
        check_vma=False,
    )
```

```python
import jax
import jax.numpy as jnp
from jax import lax
from jax.experimental import pallas as pl
from jax.experimental.pallas import tpu as pltpu
from jax.sharding import PartitionSpec as P

F32 = jnp.float32
BF16 = jnp.bfloat16
SIDE = 128
SMEM = pl.BlockSpec(memory_space=pltpu.SMEM)
VMEM = pl.BlockSpec(memory_space=pltpu.VMEM)
HBM = pl.BlockSpec(memory_space=pl.ANY)
ROWS = (((0,), (0,)), ((), ()))
COLS = (((1,), (1,)), ((), ()))


def lanes(block):
    return pl.ds(pl.multiple_of(block * SIDE, SIDE), SIDE)


def span(block, size):
    return pl.ds(pl.multiple_of(block * size, size), size)


def shape(dims, dtype):
    return jax.ShapeDtypeStruct(dims, dtype)


def call(kernel, outs, smem=(), hbm=(), vmem=(), scratch=(), after=(), mib=8):
    n_in, n_out = len(smem) + len(hbm) + len(vmem), len(outs)

    def body(*refs):
        rest = refs[n_in + len(after) :]
        rest[n_out][0] = 0
        kernel(*refs[:n_in], *rest[:n_out], *rest[n_out + 1 :])

    return pl.pallas_call(
        body,
        out_shape=(*outs, shape((1,), jnp.int32)),
        in_specs=[SMEM] * len(smem) + [HBM] * len(hbm) + [VMEM] * len(vmem) + [SMEM] * len(after),
        out_specs=(VMEM,) * n_out + (SMEM,),
        scratch_shapes=list(scratch),
        cost_estimate=pl.CostEstimate(flops=0, bytes_accessed=0, transcendentals=0),
        compiler_params=pltpu.CompilerParams(vmem_limit_bytes=mib << 20),
    )(*smem, *hbm, *vmem, *after)


class Place:
    def __init__(self, n_f, n_t, n_d):
        self.n_f, self.n_t, self.n_d, self.chips = n_f, n_t, n_d, n_d // 2

    f = property(lambda self: lax.axis_index("fsdp"))
    t = property(lambda self: lax.axis_index("tensor"))
    chip = property(lambda self: lax.axis_index("dp") // 2)
    core = property(lambda self: lax.rem(lax.axis_index("dp"), 2))

    def live(self, counts):
        return counts[self.f * self.n_t + self.t]


def fetch(*pairs_and_sems):
    copies = [pltpu.make_async_copy(src, dst, sem) for src, dst, sem in pairs_and_sems]
    for copy in copies:
        copy.start()
    return copies


def front_kernel(place, tok, left, cot, right, own, s1, s2, s3, tokv, leftv, cotv, rightv, both, sems):
    quarter, r = cotv.shape[1], rightv.shape[0]
    here = pl.ds(pl.multiple_of(place.f * quarter, SIDE), quarter)
    c_tok, c_left, c_cot, c_right = fetch(
        (tok, tokv, sems.at[0]),
        (left.at[:, lanes(place.t)], leftv, sems.at[1]),
        (cot.at[:, here], cotv, sems.at[2]),
        (right, rightv, sems.at[3]),
    )
    c_tok.wait()
    c_left.wait()
    both[:, r:] = jnp.dot(tokv[...], leftv[...], preferred_element_type=F32)
    c_cot.wait()
    c_right.wait()
    both[:, :r] = lax.dot_general(cotv[...], rightv[...], COLS, preferred_element_type=F32)
    rows = own.shape[0]
    own[...] = both[span(place.f, rows), :]
    for k, out in ((1, s1), (2, s2), (3, s3)):
        out[...] = both[span(lax.rem(place.f + k, place.n_f), rows), :].astype(BF16)


def columns_kernel(place, own, g1, g2, g3, back, rank, s1, s2, s3, total):
    r = place.n_t * SIDE
    total[...] = own[...] + g1[...].astype(F32) + g2[...].astype(F32) + g3[...].astype(F32)
    back[...] = total[:, lanes(place.t)]
    low = total[:, r:].astype(BF16)
    rank[...] = low
    for k, out in ((1, s1), (2, s2), (3, s3)):
        out[:, :SIDE] = total[:, lanes(lax.rem(place.t + k, place.n_t))].astype(BF16)
        out[:, SIDE:] = low


def rows_kernel(place, back, rank, g1, g2, g3, out):
    total = back[...]
    out[:, lanes(place.t + 1)] = rank[...]
    for k, g in ((1, g1), (2, g2), (3, g3)):
        total = total + g[:, :SIDE].astype(F32)
        out[:, lanes(lax.rem(place.t - k + place.n_t, place.n_t) + 1)] = g[:, SIDE:]
    out[:, :SIDE] = total.astype(BF16)


def residual_kernel(place, q_blocks, steps, counts, rows, cols, tok, vals, *refs):
    outs, (tokv, valv, acc, sems) = refs[:-4], refs[-4:]
    n_out = len(outs) // len(steps)
    c_tok, c_val = fetch((tok, tokv, sems.at[0]), (vals, valv, sems.at[1]))
    live = place.live(counts)
    c_tok.wait()
    c_val.wait()
    for step in steps:
        acc[...] = jnp.zeros_like(acc)
        first = lax.rem(place.f + step, place.n_f) * q_blocks

        def body(s, carry):
            col = cols[s] - first

            @pl.when((col >= 0) & (col < q_blocks))
            def _():
                acc[:, lanes(col)] += jnp.dot(
                    tokv[:, lanes(rows[s])], valv[s], preferred_element_type=F32
                )

            return carry

        lax.fori_loop(0, live, body, 0)
        row = 0
        for out in outs[:n_out]:
            out[...] = acc[row : row + out.shape[0]].astype(BF16)
            row += out.shape[0]
        outs = outs[n_out:]


PANELS = 8


def blocks_kernel(place, counts, rows, cols, tok, cot, mine, theirs, tokv, panels, sems, tok_sem):
    live = place.live(counts)

    def panel(s):
        slot = lax.rem(s, PANELS)
        return pltpu.make_async_copy(cot.at[:, lanes(cols[s])], panels.at[slot], sems.at[slot])

    def start(s):
        @pl.when(s < live)
        def _():
            panel(s).start()

    (c_tok,) = fetch((tok, tokv, tok_sem))
    for s in range(PANELS - 1):
        start(jnp.int32(s))
    mine[...] = jnp.zeros_like(mine)
    theirs[...] = jnp.zeros_like(theirs)
    per = mine.shape[1] // SIDE
    c_tok.wait()

    def body(s, carry):
        start(s + PANELS - 1)
        panel(s).wait()
        grad = lax.dot_general(
            tokv[:, lanes(rows[s])], panels[lax.rem(s, PANELS)], ROWS, preferred_element_type=F32
        )
        owner = s // per
        j = lax.rem(owner // 2 - place.chip + place.chips, place.chips)
        at = span(lax.rem(s, per), SIDE)
        keep = lax.rem(owner, 2) == place.core

        @pl.when(keep)
        def _():
            mine[j, at] = grad

        @pl.when(jnp.logical_not(keep))
        def _():
            theirs[j, at] = grad.astype(BF16)

        return carry

    lax.fori_loop(0, live, body, 0)


def factors_kernel(
    place, tok, cot, g0, g1, g2, g3, blocks_mine, blocks_theirs, mine, theirs0, theirs1, theirs2, theirs3,
    tokv, cotv, both, left, right, sems,
):
    quarter, n_rows = cotv.shape[1], g0.shape[0]
    here = pl.ds(pl.multiple_of(place.f * quarter, SIDE), quarter)
    c_tok, c_cot = fetch((tok, tokv, sems.at[0]), (cot.at[:, here], cotv, sems.at[1]))
    for k, g in enumerate((g0, g1, g2, g3)):
        both[span(lax.rem(place.f - k + place.n_f, place.n_f), n_rows), :] = g[...]
    n_l = left.shape[0] // place.n_d
    n_r = right.shape[0] // place.n_d
    n_lr = n_l + quarter // SIDE * n_r
    theirs = (theirs0, theirs1, theirs2, theirs3)
    for j in range(place.chips):
        mine[j, n_lr:] = blocks_mine[j]
        theirs[j][n_lr:] = blocks_theirs[j]
    c_tok.wait()
    left[...] = lax.dot_general(both[:, :SIDE], tokv[...], ROWS, preferred_element_type=F32).T
    c_cot.wait()
    right[...] = lax.dot_general(both[:, SIDE:], cotv[...], ROWS, preferred_element_type=F32)
    for j in range(place.chips):
        chip = lax.rem(place.chip + j, place.chips)
        for core, out in ((place.core, mine.at[j]), (1 - place.core, theirs[j])):
            at = chip * 2 + core
            out[:n_l] = left[span(at, n_l), :].astype(out.dtype)
            for p in range(quarter // SIDE):
                out[n_l + p * n_r : n_l + (p + 1) * n_r] = right[
                    span(at, n_r), p * SIDE : (p + 1) * SIDE
                ].astype(out.dtype)


def cores_kernel(mine, got0, got1, got2, got3, own, ahead, behind, near):
    half = own.shape[0] // 2
    got = (got0, got1, got2, got3)
    own[...] = mine[0] + got[0][...].astype(F32)
    far = (mine[2] + got[2][...].astype(F32)).astype(BF16)
    ahead[:half] = far[:half]
    behind[:half] = far[half:]
    ahead[half:] = (mine[1, half:] + got[1][half:].astype(F32)).astype(BF16)
    behind[half:] = (mine[3, :half] + got[3][:half].astype(F32)).astype(BF16)
    near[:half] = mine[1, :half] + got[1][:half].astype(F32)
    near[half:] = mine[3, half:] + got[3][half:].astype(F32)


def relay_kernel(near, from_behind, from_ahead, ahead, behind):
    half = ahead.shape[0]
    ahead[...] = (near[:half].astype(F32) + from_behind[:half].astype(F32)).astype(BF16)
    behind[...] = (near[half:].astype(F32) + from_ahead[:half].astype(F32)).astype(BF16)


def pass_kernel(p1, p3, from_behind, from_ahead, ahead, behind):
    half = from_behind.shape[0]
    ahead[:half] = (p1[:half].astype(F32) + from_behind[...].astype(F32)).astype(BF16)
    ahead[half:] = p1[half:]
    behind[:half] = p3[:half]
    behind[half:] = (p3[half:].astype(F32) + from_ahead[...].astype(F32)).astype(BF16)


def chunk_kernel(own, from_behind, from_ahead, last_behind, last_ahead, left, rest, total):
    half = last_behind.shape[0]
    n_l = left.shape[0]
    total[:half] = own[:half] + from_ahead[half:].astype(F32) + last_behind[...].astype(F32)
    total[half:] = own[half:] + from_behind[half:].astype(F32) + last_ahead[...].astype(F32)
    left[...] = total[:n_l].astype(BF16)
    rest[...] = total[n_l:].astype(BF16)


def stack_kernel(*refs):
    out, row = refs[-1], 0
    for part in refs[:-1]:
        out[row : row + part.shape[0]] = part[...]
        row += part.shape[0]


def second_kernel(left_pair, left_far, rest_behind, rest_ahead, ahead, behind):
    n = left_pair.shape[0]
    half = rest_behind.shape[0] // 2
    for out, piece in ((ahead, rest_behind[:half]), (behind, rest_ahead[half:])):
        out[:n] = left_pair[...]
        out[n : 2 * n] = left_far[...]
        out[2 * n :] = piece


def low_kernel(place, g0, g1, g2, g3, right, p0, out):
    n_rows = g0.shape[0]
    for k, g in enumerate((g0, g1, g2, g3)):
        at = span(lax.rem(place.f - k + place.n_f, place.n_f), n_rows)
        prod = jnp.dot(g[:, SIDE:], right[...], preferred_element_type=F32)
        out[at, :] = prod + p0[at, :].astype(F32)


def finish_kernel(low, from_behind, from_ahead, out):
    out[...] = (low[...] + from_behind[...].astype(F32) + from_ahead[...].astype(F32)).astype(BF16)


def spread_kernel(place, *refs):
    refs, (left, right, blocks) = refs[:-3], refs[-3:]
    n_l = left.shape[0] // place.n_d
    n_r = right.shape[0] // place.n_d
    n_b = blocks.shape[0] // place.n_d
    panels = right.shape[1] // SIDE
    n_rest = panels * n_r + n_b
    n_left = place.n_t * n_l
    t = place.t
    near_t = t + 1 - 2 * lax.rem(t, 2)
    far_t = place.n_t - 1 - t
    order = (t, near_t, far_t, place.n_t - 1 - near_t)
    n = len(refs) // 2
    for core, mine in ((place.core, refs[:n]), (1 - place.core, refs[n:])):
        rest, rest_behind, rest_ahead, pair, far, behind, ahead, left_behind, left_ahead = mine
        for j, whole, lefts in (
            (0, rest, (pair, far)),
            (-1, rest_behind, (behind.at[: n_left // 2], behind.at[n_left // 2 : n_left])),
            (1, rest_ahead, (ahead.at[: n_left // 2], ahead.at[n_left // 2 : n_left])),
            (2, None, (left_behind, left_ahead)),
        ):
            at = lax.rem(place.chip + j + place.chips, place.chips) * 2 + core
            for k in range(place.n_t):
                row = k % 2 * n_l
                left[span(at, n_l), lanes(order[k])] = lefts[k // 2][row : row + n_l]

            def piece(lo, hi):
                if whole is not None:
                    return whole[lo:hi]
                if lo < n_rest // 2:
                    return behind[n_left + lo : n_left + hi]
                base = n_left - n_rest // 2
                return ahead[base + lo : base + hi]

            for p in range(panels):
                right[span(at, n_r), p * SIDE : (p + 1) * SIDE] = piece(p * n_r, (p + 1) * n_r)
            blocks[span(at, n_b)] = piece(panels * n_r, n_rest)


def shift(x, axis, n, k):
    return lax.ppermute(x, axis, [(i, (i + k) % n) for i in range(n)])


def chip_shift(x, n_data, k):
    chips = n_data // 2
    perm = [(2 * a + c, 2 * ((a + k) % chips) + c) for a in range(chips) for c in range(2)]
    return lax.ppermute(x, "dp", perm)


def core_swap(x, n_data):
    return lax.ppermute(x, "dp", [(i, i ^ 1) for i in range(n_data)])


def per_device(
    tokens, cotangent, left_factor, right_factor, block_values, block_rows, block_cols, block_counts
):
    n_f = lax.axis_size("fsdp")
    n_t = lax.axis_size("tensor")
    n_d = lax.axis_size("dp")
    place = Place(n_f, n_t, n_d)
    chips = n_d // 2
    maxb = block_values.shape[0]
    tok_rows, features = tokens.shape
    right = right_factor.reshape(right_factor.shape[0], -1)
    rank_size, quarter = right.shape
    q_blocks = quarter // SIDE
    n_rows = tok_rows // n_f
    width = rank_size + SIDE
    half = tok_rows // 2
    lists = (block_counts, block_rows, block_cols)
    vm, dma = pltpu.VMEM, pltpu.SemaphoreType.DMA

    def bind(kernel, *args):
        return lambda *refs: kernel(place, *args, *refs)

    def over(n, k_shift):
        return [k_shift(k) for k in range(1, n)]

    def residual(steps, outs, after, mib):
        return call(
            bind(residual_kernel, q_blocks, steps),
            outs,
            smem=lists,
            hbm=(tokens, block_values),
            scratch=[
                vm((tok_rows, features), BF16),
                vm((maxb, SIDE, SIDE), BF16),
                vm((tok_rows, quarter), F32),
                dma((2,)),
            ],
            after=after,
            mib=mib,
        )

    part, whole = shape((half, quarter), BF16), shape((tok_rows, quarter), BF16)
    ahead, behind, step = residual((2,), (part, part), (), 56)
    from_behind = shift(ahead, "fsdp", n_f, 1)
    from_ahead = shift(behind, "fsdp", n_f, -1)

    message = shape((n_rows, width), BF16)
    own, *out, step = call(
        bind(front_kernel),
        (shape((n_rows, width), F32),) + (message,) * 3,
        hbm=(tokens, left_factor, cotangent, right),
        scratch=[
            vm((tok_rows, features), BF16),
            vm((features, SIDE), BF16),
            vm((tok_rows, quarter), BF16),
            vm((rank_size, quarter), BF16),
            vm((tok_rows, width), F32),
            dma((4,)),
        ],
        after=(step,),
        mib=52,
    )
    shares = [shift(x, "fsdp", n_f, k + 1) for k, x in enumerate(out)]
    p1, p3, p0, step = residual((1, 3, 0), (whole,) * 3, (step,), 24)

    back, rank, *out, step = call(
        bind(columns_kernel),
        (shape((n_rows, SIDE), F32), shape((n_rows, SIDE), BF16))
        + (shape((n_rows, 2 * SIDE), BF16),) * 3,
        vmem=(own, *shares),
        scratch=[vm((n_rows, width), F32)],
        after=(step,),
    )
    shares = [shift(x, "tensor", n_t, k + 1) for k, x in enumerate(out)]

    n_b = maxb // n_d * SIDE
    blocks_mine, blocks_theirs, step = call(
        bind(blocks_kernel),
        (shape((chips, n_b, SIDE), F32), shape((chips, n_b, SIDE), BF16)),
        smem=lists,
        hbm=(tokens, cotangent),
        scratch=[
            vm((tok_rows, features), BF16),
            vm((PANELS, tok_rows, SIDE), BF16),
            dma((PANELS,)),
            dma,
        ],
        after=(step,),
        mib=48,
    )

    rows, step = call(bind(rows_kernel), (message,), vmem=(back, rank, *shares), after=(step,))
    gathered = [rows] + over(n_f, lambda k: shift(rows, "fsdp", n_f, k))

    ahead, behind, step = call(
        pass_kernel, (whole, whole), vmem=(p1, p3, from_behind, from_ahead), after=(step,), mib=16
    )
    last_behind = shift(ahead, "fsdp", n_f, 1)
    last_ahead = shift(behind, "fsdp", n_f, -1)

    n_l = features // n_d
    n_r = rank_size // n_d
    n_rest = q_blocks * n_r + n_b
    n_all = n_l + n_rest
    chunk = shape((n_all, SIDE), BF16)
    mine, *theirs, step = call(
        bind(factors_kernel),
        (shape((chips, n_all, SIDE), F32),) + (chunk,) * chips,
        hbm=(tokens, cotangent),
        vmem=(*gathered, blocks_mine, blocks_theirs),
        scratch=[
            vm((tok_rows, features), BF16),
            vm((tok_rows, quarter), BF16),
            vm((tok_rows, width), BF16),
            vm((features, SIDE), F32),
            vm((rank_size, quarter), F32),
            dma((2,)),
        ],
        after=(step,),
        mib=36,
    )
    got = [core_swap(x, n_d) for x in theirs]
    own, c_ahead, c_behind, c_near, step = call(
        cores_kernel,
        (shape((n_all, SIDE), F32), chunk, chunk, shape((n_all, SIDE), F32)),
        vmem=(mine, *got),
        mib=16,
    )
    c_from_behind = chip_shift(c_ahead, n_d, 1)
    c_from_ahead = chip_shift(c_behind, n_d, -1)
    low, step = call(
        bind(low_kernel),
        (shape((tok_rows, quarter), F32),),
        vmem=(*gathered, right, p0),
        after=(step,),
        mib=20,
    )
    c_ahead, c_behind, step = call(
        relay_kernel,
        (shape((n_all // 2, SIDE), BF16),) * 2,
        vmem=(c_near, c_from_behind, c_from_ahead),
        after=(step,),
    )
    c_last_behind = chip_shift(c_ahead, n_d, 1)
    c_last_ahead = chip_shift(c_behind, n_d, -1)
    left, rest, step = call(
        chunk_kernel,
        (shape((n_l, SIDE), BF16), shape((n_rest, SIDE), BF16)),
        vmem=(own, c_from_behind, c_from_ahead, c_last_behind, c_last_ahead),
        scratch=[vm((n_all, SIDE), F32)],
    )

    rest_behind = chip_shift(rest, n_d, 1)
    rest_ahead = chip_shift(rest, n_d, -1)
    left_near = lax.ppermute(left, "tensor", [(i, i ^ 1) for i in range(n_t)])
    left_pair, step = call(
        stack_kernel, (shape((2 * n_l, SIDE), BF16),), vmem=(left, left_near)
    )
    left_far = lax.ppermute(left_pair, "tensor", [(i, n_t - 1 - i) for i in range(n_t)])

    n_msg = n_t * n_l + n_rest // 2
    c_ahead, c_behind, step = call(
        second_kernel,
        (shape((n_msg, SIDE), BF16),) * 2,
        vmem=(left_pair, left_far, rest_behind, rest_ahead),
    )
    c_from_behind = chip_shift(c_ahead, n_d, 1)
    c_from_ahead = chip_shift(c_behind, n_d, -1)
    n_left = n_t * n_l
    left_behind = chip_shift(c_from_behind[: n_left // 2], n_d, 1)
    left_ahead = chip_shift(c_from_ahead[n_left // 2 : n_left], n_d, -1)
    ours = (
        rest, rest_behind, rest_ahead, left_pair, left_far,
        c_from_behind, c_from_ahead, left_behind, left_ahead,
    )
    partner = [core_swap(x, n_d) for x in ours]

    out_left, out_right, out_blocks, step = call(
        bind(spread_kernel),
        (
            shape((features, rank_size), BF16),
            shape((rank_size, quarter), BF16),
            shape((maxb * SIDE, SIDE), BF16),
        ),
        vmem=(*ours, *partner),
        mib=14,
    )
    mixed, _ = call(
        finish_kernel, (whole,), vmem=(low, last_behind, last_ahead), mib=12
    )
    return (
        mixed.reshape(tok_rows, 1, quarter),
        out_left,
        out_right.reshape(right_factor.shape),
        out_blocks.reshape(maxb, SIDE, SIDE),
    )


def solution(mesh):
    return jax.shard_map(
        per_device,
        mesh=mesh,
        in_specs=(
            P("dp", "fsdp"),
            P("dp", "tensor"),
            P("fsdp", None),
            P(None, "tensor", "fsdp"),
            P(("fsdp", "tensor"), None, None),
            P(("fsdp", "tensor")),
            P(("fsdp", "tensor")),
            P(),
        ),
        out_specs=(
            P("dp", "tensor", "fsdp"),
            P("fsdp", None),
            P(None, "tensor", "fsdp"),
            P(("fsdp", "tensor"), None, None),
        ),
        check_vma=False,
    )
```

```python
import jax
import jax.numpy as jnp
from jax import lax
from jax.experimental import pallas as pl
from jax.experimental.pallas import tpu as pltpu
from jax.sharding import PartitionSpec as P

F32 = jnp.float32
BF16 = jnp.bfloat16
SIDE = 128
SMEM = pl.BlockSpec(memory_space=pltpu.SMEM)
VMEM = pl.BlockSpec(memory_space=pltpu.VMEM)
HBM = pl.BlockSpec(memory_space=pl.ANY)
ROWS = (((0,), (0,)), ((), ()))
COLS = (((1,), (1,)), ((), ()))


def lanes(block):
    return pl.ds(pl.multiple_of(block * SIDE, SIDE), SIDE)


def span(block, size):
    return pl.ds(pl.multiple_of(block * size, size), size)


def shape(dims, dtype):
    return jax.ShapeDtypeStruct(dims, dtype)


def call(kernel, outs, smem=(), hbm=(), vmem=(), scratch=(), after=(), mib=8):
    n_in, n_out = len(smem) + len(hbm) + len(vmem), len(outs)

    def body(*refs):
        rest = refs[n_in + len(after) :]
        rest[n_out][0] = 0
        kernel(*refs[:n_in], *rest[:n_out], *rest[n_out + 1 :])

    return pl.pallas_call(
        body,
        out_shape=(*outs, shape((1,), jnp.int32)),
        in_specs=[SMEM] * len(smem) + [HBM] * len(hbm) + [VMEM] * len(vmem) + [SMEM] * len(after),
        out_specs=(VMEM,) * n_out + (SMEM,),
        scratch_shapes=list(scratch),
        cost_estimate=pl.CostEstimate(flops=0, bytes_accessed=0, transcendentals=0),
        compiler_params=pltpu.CompilerParams(vmem_limit_bytes=mib << 20),
    )(*smem, *hbm, *vmem, *after)


class Place:
    def __init__(self, n_f, n_t, n_d):
        self.n_f, self.n_t, self.n_d, self.chips = n_f, n_t, n_d, n_d // 2

    f = property(lambda self: lax.axis_index("fsdp"))
    t = property(lambda self: lax.axis_index("tensor"))
    chip = property(lambda self: lax.axis_index("dp") // 2)
    core = property(lambda self: lax.rem(lax.axis_index("dp"), 2))

    def live(self, counts):
        return counts[self.f * self.n_t + self.t]


def fetch(*pairs_and_sems):
    copies = [pltpu.make_async_copy(src, dst, sem) for src, dst, sem in pairs_and_sems]
    for copy in copies:
        copy.start()
    return copies


def front_kernel(
    place, tok, left, cot, right, rank, low, back, s1, s2, s3, tokv, leftv, cotv, rightv, full, sems
):
    quarter = cotv.shape[1]
    here = pl.ds(pl.multiple_of(place.f * quarter, SIDE), quarter)
    c_tok, c_left, c_cot, c_right = fetch(
        (tok, tokv, sems.at[0]),
        (left.at[:, lanes(place.t)], leftv, sems.at[1]),
        (cot.at[:, here], cotv, sems.at[2]),
        (right, rightv, sems.at[3]),
    )
    c_tok.wait()
    c_left.wait()
    rank[...] = jnp.dot(tokv[...], leftv[...], preferred_element_type=F32)
    low[...] = rank[...].astype(BF16)
    c_cot.wait()
    c_right.wait()
    full[...] = lax.dot_general(cotv[...], rightv[...], COLS, preferred_element_type=F32)
    back[...] = full[:, lanes(place.t)]
    for k, out in ((1, s1), (2, s2), (3, s3)):
        out[...] = full[:, lanes(lax.rem(place.t + k, place.n_t))].astype(BF16)


def total_kernel(own, g1, g2, g3, *outs):
    total = own[...] + g1[...].astype(F32) + g2[...].astype(F32) + g3[...].astype(F32)
    for out in outs:
        out[...] = total.astype(out.dtype)


def residual_kernel(
    place, q_blocks, counts, rows, cols, tok, vals, ahead, behind, p1, p3, p0, tokv, valv, acc, sems
):
    c_tok, c_val = fetch((tok, tokv, sems.at[0]), (vals, valv, sems.at[1]))
    live = place.live(counts)
    half = ahead.shape[0]
    c_tok.wait()
    c_val.wait()
    for step in (2, 1, 3, 0):
        acc[...] = jnp.zeros_like(acc)
        first = lax.rem(place.f + step, place.n_f) * q_blocks

        def body(s, carry):
            col = cols[s] - first

            @pl.when((col >= 0) & (col < q_blocks))
            def _():
                acc[:, lanes(col)] += jnp.dot(
                    tokv[:, lanes(rows[s])], valv[s], preferred_element_type=F32
                )

            return carry

        lax.fori_loop(0, live, body, 0)
        if step == 2:
            ahead[...] = acc[:half].astype(BF16)
            behind[...] = acc[half:].astype(BF16)
        else:
            {1: p1, 3: p3, 0: p0}[step][...] = acc[...].astype(BF16)


PANELS = 8


def blocks_kernel(place, counts, rows, cols, tok, cot, mine, theirs, tokv, panels, sems, tok_sem):
    live = place.live(counts)

    def panel(s):
        slot = lax.rem(s, PANELS)
        return pltpu.make_async_copy(cot.at[:, lanes(cols[s])], panels.at[slot], sems.at[slot])

    def start(s):
        @pl.when(s < live)
        def _():
            panel(s).start()

    (c_tok,) = fetch((tok, tokv, tok_sem))
    for s in range(PANELS - 1):
        start(jnp.int32(s))
    mine[...] = jnp.zeros_like(mine)
    theirs[...] = jnp.zeros_like(theirs)
    per = mine.shape[1] // SIDE
    c_tok.wait()

    def body(s, carry):
        start(s + PANELS - 1)
        panel(s).wait()
        grad = lax.dot_general(
            tokv[:, lanes(rows[s])], panels[lax.rem(s, PANELS)], ROWS, preferred_element_type=F32
        )
        owner = s // per
        j = lax.rem(owner // 2 - place.chip + place.chips, place.chips)
        at = span(lax.rem(s, per), SIDE)
        keep = lax.rem(owner, 2) == place.core

        @pl.when(keep)
        def _():
            mine[j, at] = grad

        @pl.when(jnp.logical_not(keep))
        def _():
            theirs[j, at] = grad.astype(BF16)

        return carry

    lax.fori_loop(0, live, body, 0)


def factors_kernel(
    place, tok, cot, g0, g1, g2, g3, b0, b1, b2, b3, blocks_mine, blocks_theirs,
    mine, theirs0, theirs1, theirs2, theirs3, tokv, cotv, left, right, sems,
):
    quarter = cotv.shape[1]
    here = pl.ds(pl.multiple_of(place.f * quarter, SIDE), quarter)
    c_tok, c_cot = fetch((tok, tokv, sems.at[0]), (cot.at[:, here], cotv, sems.at[1]))
    n_l = left.shape[0] // place.n_d
    n_r = right.shape[0] // place.n_d
    n_lr = n_l + quarter // SIDE * n_r
    theirs = (theirs0, theirs1, theirs2, theirs3)
    for j in range(place.chips):
        mine[j, n_lr:] = blocks_mine[j]
        theirs[j][n_lr:] = blocks_theirs[j]
    c_tok.wait()
    back = b0[...] + b1[...].astype(F32) + b2[...].astype(F32) + b3[...].astype(F32)
    left[...] = lax.dot_general(
        back.astype(BF16), tokv[...], ROWS, preferred_element_type=F32
    ).T
    c_cot.wait()
    for k, g in enumerate((g0, g1, g2, g3)):
        at = span(lax.rem(place.t - k + place.n_t, place.n_t), SIDE)
        right[at, :] = lax.dot_general(g[...], cotv[...], ROWS, preferred_element_type=F32)
    for j in range(place.chips):
        chip = lax.rem(place.chip + j, place.chips)
        for core, out in ((place.core, mine.at[j]), (1 - place.core, theirs[j])):
            at = chip * 2 + core
            out[:n_l] = left[span(at, n_l), :].astype(out.dtype)
            for p in range(quarter // SIDE):
                out[n_l + p * n_r : n_l + (p + 1) * n_r] = right[
                    span(at, n_r), p * SIDE : (p + 1) * SIDE
                ].astype(out.dtype)


def cores_kernel(mine, got0, got1, got2, got3, own, ahead, behind, near):
    half = own.shape[0] // 2
    got = (got0, got1, got2, got3)
    own[...] = mine[0] + got[0][...].astype(F32)
    far = (mine[2] + got[2][...].astype(F32)).astype(BF16)
    ahead[:half] = far[:half]
    behind[:half] = far[half:]
    ahead[half:] = (mine[1, half:] + got[1][half:].astype(F32)).astype(BF16)
    behind[half:] = (mine[3, :half] + got[3][:half].astype(F32)).astype(BF16)
    near[:half] = mine[1, :half] + got[1][:half].astype(F32)
    near[half:] = mine[3, half:] + got[3][half:].astype(F32)


def relay_kernel(near, from_behind, from_ahead, ahead, behind):
    half = ahead.shape[0]
    ahead[...] = (near[:half].astype(F32) + from_behind[:half].astype(F32)).astype(BF16)
    behind[...] = (near[half:].astype(F32) + from_ahead[:half].astype(F32)).astype(BF16)


def pass_kernel(p1, p3, from_behind, from_ahead, ahead, behind):
    half = from_behind.shape[0]
    ahead[:half] = (p1[:half].astype(F32) + from_behind[...].astype(F32)).astype(BF16)
    ahead[half:] = p1[half:]
    behind[:half] = p3[:half]
    behind[half:] = (p3[half:].astype(F32) + from_ahead[...].astype(F32)).astype(BF16)


def chunk_kernel(own, from_behind, from_ahead, last_behind, last_ahead, left, rest, total):
    half = last_behind.shape[0]
    n_l = left.shape[0]
    total[:half] = own[:half] + from_ahead[half:].astype(F32) + last_behind[...].astype(F32)
    total[half:] = own[half:] + from_behind[half:].astype(F32) + last_ahead[...].astype(F32)
    left[...] = total[:n_l].astype(BF16)
    rest[...] = total[n_l:].astype(BF16)


def stack_kernel(*refs):
    out, row = refs[-1], 0
    for part in refs[:-1]:
        out[row : row + part.shape[0]] = part[...]
        row += part.shape[0]


def second_kernel(left_pair, left_far, rest_behind, rest_ahead, ahead, behind):
    n = left_pair.shape[0]
    half = rest_behind.shape[0] // 2
    for out, piece in ((ahead, rest_behind[:half]), (behind, rest_ahead[half:])):
        out[:n] = left_pair[...]
        out[n : 2 * n] = left_far[...]
        out[2 * n :] = piece


def low_kernel(place, g0, g1, g2, g3, right, p0, out):
    acc = p0[...].astype(F32)
    for k, g in enumerate((g0, g1, g2, g3)):
        at = span(lax.rem(place.t - k + place.n_t, place.n_t), SIDE)
        acc += jnp.dot(g[...], right[at, :], preferred_element_type=F32)
    out[...] = acc


def finish_kernel(low, from_behind, from_ahead, out):
    out[...] = (low[...] + from_behind[...].astype(F32) + from_ahead[...].astype(F32)).astype(BF16)


def spread_kernel(place, *refs):
    refs, (left, right, blocks) = refs[:-3], refs[-3:]
    n_l = left.shape[0] // place.n_d
    n_r = right.shape[0] // place.n_d
    n_b = blocks.shape[0] // place.n_d
    panels = right.shape[1] // SIDE
    n_rest = panels * n_r + n_b
    n_left = place.n_t * n_l
    t = place.t
    near_t = t + 1 - 2 * lax.rem(t, 2)
    far_t = place.n_t - 1 - t
    order = (t, near_t, far_t, place.n_t - 1 - near_t)
    n = len(refs) // 2
    for core, mine in ((place.core, refs[:n]), (1 - place.core, refs[n:])):
        rest, rest_behind, rest_ahead, pair, far, behind, ahead, left_behind, left_ahead = mine
        for j, whole, lefts in (
            (0, rest, (pair, far)),
            (-1, rest_behind, (behind.at[: n_left // 2], behind.at[n_left // 2 : n_left])),
            (1, rest_ahead, (ahead.at[: n_left // 2], ahead.at[n_left // 2 : n_left])),
            (2, None, (left_behind, left_ahead)),
        ):
            at = lax.rem(place.chip + j + place.chips, place.chips) * 2 + core
            for k in range(place.n_t):
                row = k % 2 * n_l
                left[span(at, n_l), lanes(order[k])] = lefts[k // 2][row : row + n_l]

            def piece(lo, hi):
                if whole is not None:
                    return whole[lo:hi]
                if lo < n_rest // 2:
                    return behind[n_left + lo : n_left + hi]
                base = n_left - n_rest // 2
                return ahead[base + lo : base + hi]

            for p in range(panels):
                right[span(at, n_r), p * SIDE : (p + 1) * SIDE] = piece(p * n_r, (p + 1) * n_r)
            blocks[span(at, n_b)] = piece(panels * n_r, n_rest)


def shift(x, axis, n, k):
    return lax.ppermute(x, axis, [(i, (i + k) % n) for i in range(n)])


def chip_shift(x, n_data, k):
    chips = n_data // 2
    perm = [(2 * a + c, 2 * ((a + k) % chips) + c) for a in range(chips) for c in range(2)]
    return lax.ppermute(x, "dp", perm)


def core_swap(x, n_data):
    return lax.ppermute(x, "dp", [(i, i ^ 1) for i in range(n_data)])


def per_device(
    tokens, cotangent, left_factor, right_factor, block_values, block_rows, block_cols, block_counts
):
    n_f = lax.axis_size("fsdp")
    n_t = lax.axis_size("tensor")
    n_d = lax.axis_size("dp")
    place = Place(n_f, n_t, n_d)
    chips = n_d // 2
    maxb = block_values.shape[0]
    tok_rows, features = tokens.shape
    right = right_factor.reshape(right_factor.shape[0], -1)
    rank_size, quarter = right.shape
    q_blocks = quarter // SIDE
    half = tok_rows // 2
    lists = (block_counts, block_rows, block_cols)
    vm, dma = pltpu.VMEM, pltpu.SemaphoreType.DMA

    def bind(kernel, *args):
        return lambda *refs: kernel(place, *args, *refs)

    def over(n, k_shift):
        return [k_shift(k) for k in range(1, n)]

    wide, narrow = shape((tok_rows, SIDE), F32), shape((tok_rows, SIDE), BF16)
    rank, rank_low, back, *back_out, step = call(
        bind(front_kernel),
        (wide, narrow, wide, narrow, narrow, narrow),
        hbm=(tokens, left_factor, cotangent, right),
        scratch=[
            vm((tok_rows, features), BF16),
            vm((features, SIDE), BF16),
            vm((tok_rows, quarter), BF16),
            vm((rank_size, quarter), BF16),
            vm((tok_rows, rank_size), F32),
            dma((4,)),
        ],
        mib=56,
    )
    rank_in = over(n_f, lambda k: shift(rank_low, "fsdp", n_f, k))
    back_in = [shift(x, "tensor", n_t, k + 1) for k, x in enumerate(back_out)]

    part, whole = shape((half, quarter), BF16), shape((tok_rows, quarter), BF16)
    ahead, behind, p1, p3, p0, step = call(
        bind(residual_kernel, q_blocks),
        (part, part, whole, whole, whole),
        smem=lists,
        hbm=(tokens, block_values),
        scratch=[
            vm((tok_rows, features), BF16),
            vm((maxb, SIDE, SIDE), BF16),
            vm((tok_rows, quarter), F32),
            dma((2,)),
        ],
        after=(step,),
        mib=56,
    )

    rank, step = call(total_kernel, (narrow,), vmem=(rank, *rank_in), after=(step,))
    ranks = [rank] + over(n_t, lambda k: shift(rank, "tensor", n_t, k))
    back, back_low, step = call(
        total_kernel, (wide, narrow), vmem=(back, *back_in), after=(step,)
    )
    backs = [back] + over(n_f, lambda k: shift(back_low, "fsdp", n_f, k))

    n_b = maxb // n_d * SIDE
    blocks_mine, blocks_theirs, step = call(
        bind(blocks_kernel),
        (shape((chips, n_b, SIDE), F32), shape((chips, n_b, SIDE), BF16)),
        smem=lists,
        hbm=(tokens, cotangent),
        scratch=[
            vm((tok_rows, features), BF16),
            vm((PANELS, tok_rows, SIDE), BF16),
            dma((PANELS,)),
            dma,
        ],
        after=(step,),
        mib=48,
    )

    ahead, behind = pl.pallas_call(
        lambda *refs: None,
        out_shape=(part, part),
        in_specs=[HBM] * 2 + [VMEM] * 6,
        out_specs=(HBM,) * 2,
        input_output_aliases={0: 0, 1: 1},
    )(ahead, behind, *ranks[1:], *backs[1:])
    from_behind = shift(ahead, "fsdp", n_f, 1)
    from_ahead = shift(behind, "fsdp", n_f, -1)

    n_l = features // n_d
    n_r = rank_size // n_d
    n_rest = q_blocks * n_r + n_b
    n_all = n_l + n_rest
    chunk = shape((n_all, SIDE), BF16)
    mine, *theirs, step = call(
        bind(factors_kernel),
        (shape((chips, n_all, SIDE), F32),) + (chunk,) * chips,
        hbm=(tokens, cotangent),
        vmem=(*ranks, *backs, blocks_mine, blocks_theirs),
        scratch=[
            vm((tok_rows, features), BF16),
            vm((tok_rows, quarter), BF16),
            vm((features, SIDE), F32),
            vm((rank_size, quarter), F32),
            dma((2,)),
        ],
        after=(step,),
        mib=36,
    )
    got = [core_swap(x, n_d) for x in theirs]
    own, c_ahead, c_behind, c_near, step = call(
        cores_kernel,
        (shape((n_all, SIDE), F32), chunk, chunk, shape((n_all, SIDE), F32)),
        vmem=(mine, *got),
        mib=16,
    )
    c_from_behind = chip_shift(c_ahead, n_d, 1)
    c_from_ahead = chip_shift(c_behind, n_d, -1)
    low, step = call(
        bind(low_kernel),
        (shape((tok_rows, quarter), F32),),
        vmem=(*ranks, right, p0),
        after=(step,),
        mib=20,
    )
    c_ahead, c_behind, step = call(
        relay_kernel,
        (shape((n_all // 2, SIDE), BF16),) * 2,
        vmem=(c_near, c_from_behind, c_from_ahead),
        after=(step,),
    )
    c_last_behind = chip_shift(c_ahead, n_d, 1)
    c_last_ahead = chip_shift(c_behind, n_d, -1)
    ahead, behind, step = call(
        pass_kernel, (whole, whole), vmem=(p1, p3, from_behind, from_ahead), after=(step,), mib=16
    )
    last_behind = shift(ahead, "fsdp", n_f, 1)
    last_ahead = shift(behind, "fsdp", n_f, -1)
    left, rest, step = call(
        chunk_kernel,
        (shape((n_l, SIDE), BF16), shape((n_rest, SIDE), BF16)),
        vmem=(own, c_from_behind, c_from_ahead, c_last_behind, c_last_ahead),
        scratch=[vm((n_all, SIDE), F32)],
        after=(step,),
    )

    rest_behind = chip_shift(rest, n_d, 1)
    rest_ahead = chip_shift(rest, n_d, -1)
    left_near = lax.ppermute(left, "tensor", [(i, i ^ 1) for i in range(n_t)])
    left_pair, step = call(
        stack_kernel, (shape((2 * n_l, SIDE), BF16),), vmem=(left, left_near)
    )
    left_far = lax.ppermute(left_pair, "tensor", [(i, n_t - 1 - i) for i in range(n_t)])

    n_msg = n_t * n_l + n_rest // 2
    c_ahead, c_behind, step = call(
        second_kernel,
        (shape((n_msg, SIDE), BF16),) * 2,
        vmem=(left_pair, left_far, rest_behind, rest_ahead),
    )
    c_from_behind = chip_shift(c_ahead, n_d, 1)
    c_from_ahead = chip_shift(c_behind, n_d, -1)
    n_left = n_t * n_l
    left_behind = chip_shift(c_from_behind[: n_left // 2], n_d, 1)
    left_ahead = chip_shift(c_from_ahead[n_left // 2 : n_left], n_d, -1)
    ours = (
        rest, rest_behind, rest_ahead, left_pair, left_far,
        c_from_behind, c_from_ahead, left_behind, left_ahead,
    )
    partner = [core_swap(x, n_d) for x in ours]

    out_left, out_right, out_blocks, step = call(
        bind(spread_kernel),
        (
            shape((features, rank_size), BF16),
            shape((rank_size, quarter), BF16),
            shape((maxb * SIDE, SIDE), BF16),
        ),
        vmem=(*ours, *partner),
        mib=14,
    )
    mixed, _ = call(
        finish_kernel, (whole,), vmem=(low, last_behind, last_ahead), mib=12
    )
    return (
        mixed.reshape(tok_rows, 1, quarter),
        out_left,
        out_right.reshape(right_factor.shape),
        out_blocks.reshape(maxb, SIDE, SIDE),
    )


def solution(mesh):
    return jax.shard_map(
        per_device,
        mesh=mesh,
        in_specs=(
            P("dp", "fsdp"),
            P("dp", "tensor"),
            P("fsdp", None),
            P(None, "tensor", "fsdp"),
            P(("fsdp", "tensor"), None, None),
            P(("fsdp", "tensor")),
            P(("fsdp", "tensor")),
            P(),
        ),
        out_specs=(
            P("dp", "tensor", "fsdp"),
            P("fsdp", None),
            P(None, "tensor", "fsdp"),
            P(("fsdp", "tensor"), None, None),
        ),
        check_vma=False,
    )
```

```python
import jax
import jax.numpy as jnp
from jax import lax
from jax.experimental import pallas as pl
from jax.experimental.pallas import tpu as pltpu
from jax.sharding import PartitionSpec as P

F32 = jnp.float32
BF16 = jnp.bfloat16
SIDE = 128
SMEM = pl.BlockSpec(memory_space=pltpu.SMEM)
VMEM = pl.BlockSpec(memory_space=pltpu.VMEM)
HBM = pl.BlockSpec(memory_space=pl.ANY)
ROWS = (((0,), (0,)), ((), ()))
COLS = (((1,), (1,)), ((), ()))


def lanes(block):
    return pl.ds(pl.multiple_of(block * SIDE, SIDE), SIDE)


def span(block, size):
    return pl.ds(pl.multiple_of(block * size, size), size)


def shape(dims, dtype):
    return jax.ShapeDtypeStruct(dims, dtype)


def call(kernel, outs, smem=(), hbm=(), vmem=(), scratch=(), after=(), mib=8):
    n_in, n_out = len(smem) + len(hbm) + len(vmem), len(outs)

    def body(*refs):
        rest = refs[n_in + len(after) :]
        rest[n_out][0] = 0
        kernel(*refs[:n_in], *rest[:n_out], *rest[n_out + 1 :])

    return pl.pallas_call(
        body,
        out_shape=(*outs, shape((1,), jnp.int32)),
        in_specs=[SMEM] * len(smem) + [HBM] * len(hbm) + [VMEM] * len(vmem) + [SMEM] * len(after),
        out_specs=(VMEM,) * n_out + (SMEM,),
        scratch_shapes=list(scratch),
        cost_estimate=pl.CostEstimate(flops=0, bytes_accessed=0, transcendentals=0),
        compiler_params=pltpu.CompilerParams(vmem_limit_bytes=mib << 20),
    )(*smem, *hbm, *vmem, *after)


class Place:
    def __init__(self, n_f, n_t, n_d):
        self.n_f, self.n_t, self.n_d, self.chips = n_f, n_t, n_d, n_d // 2

    f = property(lambda self: lax.axis_index("fsdp"))
    t = property(lambda self: lax.axis_index("tensor"))
    chip = property(lambda self: lax.axis_index("dp") // 2)
    core = property(lambda self: lax.rem(lax.axis_index("dp"), 2))

    def live(self, counts):
        return counts[self.f * self.n_t + self.t]


def fetch(*pairs_and_sems):
    copies = [pltpu.make_async_copy(src, dst, sem) for src, dst, sem in pairs_and_sems]
    for copy in copies:
        copy.start()
    return copies


def front_kernel(
    place, tok, left, cot, right, rank, low, back, s1, s2, s3, tokv, leftv, cotv, rightv, full, sems
):
    quarter = cotv.shape[1]
    here = pl.ds(pl.multiple_of(place.f * quarter, SIDE), quarter)
    c_tok, c_left, c_cot, c_right = fetch(
        (tok, tokv, sems.at[0]),
        (left.at[:, lanes(place.t)], leftv, sems.at[1]),
        (cot.at[:, here], cotv, sems.at[2]),
        (right, rightv, sems.at[3]),
    )
    c_tok.wait()
    c_left.wait()
    rank[...] = jnp.dot(tokv[...], leftv[...], preferred_element_type=F32)
    low[...] = rank[...].astype(BF16)
    c_cot.wait()
    c_right.wait()
    full[...] = lax.dot_general(cotv[...], rightv[...], COLS, preferred_element_type=F32)
    back[...] = full[:, lanes(place.t)]
    for k, out in ((1, s1), (2, s2), (3, s3)):
        out[...] = full[:, lanes(lax.rem(place.t + k, place.n_t))].astype(BF16)


def total_kernel(own, g1, g2, g3, *outs):
    total = own[...] + g1[...].astype(F32) + g2[...].astype(F32) + g3[...].astype(F32)
    for out in outs:
        out[...] = total.astype(out.dtype)


def add_blocks(place, q_blocks, step, counts, rows, cols, tok, vals, acc):
    first = lax.rem(place.f + step, place.n_f) * q_blocks

    def body(s, carry):
        col = cols[s] - first

        @pl.when((col >= 0) & (col < q_blocks))
        def _():
            acc[:, lanes(col)] += jnp.dot(tok[:, lanes(rows[s])], vals[s], preferred_element_type=F32)

        return carry

    lax.fori_loop(0, place.live(counts), body, 0)


def residual_kernel(place, q_blocks, steps, counts, rows, cols, tok, vals, *refs):
    outs, (tokv, valv, acc, sems) = refs[:-4], refs[-4:]
    c_tok, c_val = fetch((tok, tokv, sems.at[0]), (vals, valv, sems.at[1]))
    n_out = len(outs) // len(steps)
    for i, step in enumerate(steps):
        acc[...] = jnp.zeros_like(acc)
        if i == 0:
            c_tok.wait()
            c_val.wait()
        add_blocks(place, q_blocks, step, counts, rows, cols, tokv, valv, acc)
        row = 0
        for out in outs[i * n_out : (i + 1) * n_out]:
            out[...] = acc[row : row + out.shape[0]].astype(BF16)
            row += out.shape[0]


PANELS = 8


def blocks_kernel(place, counts, rows, cols, tok, cot, mine, theirs, tokv, panels, sems, tok_sem):
    live = place.live(counts)

    def panel(s):
        slot = lax.rem(s, PANELS)
        return pltpu.make_async_copy(cot.at[:, lanes(cols[s])], panels.at[slot], sems.at[slot])

    def start(s):
        @pl.when(s < live)
        def _():
            panel(s).start()

    (c_tok,) = fetch((tok, tokv, tok_sem))
    for s in range(PANELS - 1):
        start(jnp.int32(s))
    mine[...] = jnp.zeros_like(mine)
    theirs[...] = jnp.zeros_like(theirs)
    per = mine.shape[1] // SIDE
    c_tok.wait()

    def body(s, carry):
        start(s + PANELS - 1)
        panel(s).wait()
        grad = lax.dot_general(
            tokv[:, lanes(rows[s])], panels[lax.rem(s, PANELS)], ROWS, preferred_element_type=F32
        )
        owner = s // per
        j = lax.rem(owner // 2 - place.chip + place.chips, place.chips)
        at = span(lax.rem(s, per), SIDE)
        keep = lax.rem(owner, 2) == place.core

        @pl.when(keep)
        def _():
            mine[j, at] = grad

        @pl.when(jnp.logical_not(keep))
        def _():
            theirs[j, at] = grad.astype(BF16)

        return carry

    lax.fori_loop(0, live, body, 0)


def factors_kernel(
    place, tok, cot, g0, g1, g2, g3, b0, b1, b2, b3, blocks_mine, blocks_theirs,
    mine, theirs0, theirs1, theirs2, theirs3, tokv, cotv, left, right, sems,
):
    quarter = cotv.shape[1]
    here = pl.ds(pl.multiple_of(place.f * quarter, SIDE), quarter)
    c_tok, c_cot = fetch((tok, tokv, sems.at[0]), (cot.at[:, here], cotv, sems.at[1]))
    n_l = left.shape[0] // place.n_d
    n_r = right.shape[0] // place.n_d
    n_lr = n_l + quarter // SIDE * n_r
    theirs = (theirs0, theirs1, theirs2, theirs3)
    for j in range(place.chips):
        mine[j, n_lr:] = blocks_mine[j]
        theirs[j][n_lr:] = blocks_theirs[j]
    c_tok.wait()
    back = b0[...] + b1[...].astype(F32) + b2[...].astype(F32) + b3[...].astype(F32)
    left[...] = lax.dot_general(
        back.astype(BF16), tokv[...], ROWS, preferred_element_type=F32
    ).T
    c_cot.wait()
    for k, g in enumerate((g0, g1, g2, g3)):
        at = span(lax.rem(place.t - k + place.n_t, place.n_t), SIDE)
        right[at, :] = lax.dot_general(g[...], cotv[...], ROWS, preferred_element_type=F32)
    for j in range(place.chips):
        chip = lax.rem(place.chip + j, place.chips)
        for core, out in ((place.core, mine.at[j]), (1 - place.core, theirs[j])):
            at = chip * 2 + core
            out[:n_l] = left[span(at, n_l), :].astype(out.dtype)
            for p in range(quarter // SIDE):
                out[n_l + p * n_r : n_l + (p + 1) * n_r] = right[
                    span(at, n_r), p * SIDE : (p + 1) * SIDE
                ].astype(out.dtype)


def cores_kernel(n_l, mine, got0, got1, got2, got3, own, near, ahead, behind, far):
    mid = n_l + (own.shape[0] - n_l) // 2
    got = (got0, got1, got2, got3)

    def both(k, lo, hi):
        return mine[k, lo:hi] + got[k][lo:hi].astype(F32)

    end = own.shape[0]
    half = end - mid
    own[...] = both(0, 0, end)
    far[...] = both(2, 0, n_l).astype(BF16)
    ahead[:n_l] = both(1, 0, n_l).astype(BF16)
    behind[:n_l] = both(3, 0, n_l).astype(BF16)
    ahead[n_l:mid] = both(2, n_l, mid).astype(BF16)
    behind[n_l:mid] = both(2, mid, end).astype(BF16)
    ahead[mid:] = both(1, mid, end).astype(BF16)
    behind[mid:] = both(3, n_l, mid).astype(BF16)
    near[:half] = both(1, n_l, mid)
    near[half:] = both(3, mid, end)


def relay_kernel(own, near, from_behind, from_ahead, from_far, left, ahead, behind):
    n_l, half = left.shape[0], ahead.shape[0]
    mid = n_l + half
    left[...] = (
        own[:n_l] + from_behind[:n_l].astype(F32) + from_ahead[:n_l].astype(F32)
        + from_far[...].astype(F32)
    ).astype(BF16)
    ahead[...] = (near[:half] + from_behind[n_l:mid].astype(F32)).astype(BF16)
    behind[...] = (near[half:] + from_ahead[n_l:mid].astype(F32)).astype(BF16)


def chunk_kernel(own, from_behind, from_ahead, last_behind, last_ahead, pair, far, out):
    half, n = last_behind.shape[0], pair.shape[0]
    n_l = own.shape[0] - 2 * half
    mid = n_l + half
    out[:n] = pair[...]
    out[n : 2 * n] = far[...]
    out[2 * n : 2 * n + half] = (
        own[n_l:mid] + from_ahead[mid:].astype(F32) + last_behind[...].astype(F32)
    ).astype(BF16)
    out[2 * n + half :] = (
        own[mid:] + from_behind[mid:].astype(F32) + last_ahead[...].astype(F32)
    ).astype(BF16)


def stack_kernel(a, b, out):
    out[: a.shape[0]] = a[...]
    out[a.shape[0] :] = b[...]


def pass_kernel(p1, p3, from_behind, from_ahead, ahead, behind):
    half = from_behind.shape[0]
    ahead[:half] = (p1[:half].astype(F32) + from_behind[...].astype(F32)).astype(BF16)
    ahead[half:] = p1[half:]
    behind[:half] = p3[:half]
    behind[half:] = (p3[half:].astype(F32) + from_ahead[...].astype(F32)).astype(BF16)


def low_kernel(
    place, q_blocks, counts, rows, cols, tok, vals, g0, g1, g2, g3, right, out, tokv, valv, sems
):
    c_tok, c_val = fetch((tok, tokv, sems.at[0]), (vals, valv, sems.at[1]))
    acc = jnp.zeros(out.shape, F32)
    for k, g in enumerate((g0, g1, g2, g3)):
        at = span(lax.rem(place.t - k + place.n_t, place.n_t), SIDE)
        acc += jnp.dot(g[...], right[at, :], preferred_element_type=F32)
    out[...] = acc
    c_tok.wait()
    c_val.wait()
    add_blocks(place, q_blocks, 0, counts, rows, cols, tokv, valv, out)


def finish_kernel(low, from_behind, from_ahead, out):
    out[...] = (low[...] + from_behind[...].astype(F32) + from_ahead[...].astype(F32)).astype(BF16)


def spread_kernel(place, *refs):
    refs, (left, right, blocks) = refs[:-3], refs[-3:]
    n_l = left.shape[0] // place.n_d
    n_r = right.shape[0] // place.n_d
    n_b = blocks.shape[0] // place.n_d
    panels = right.shape[1] // SIDE
    n_left = place.n_t * n_l
    t = place.t
    near_t = t + 1 - 2 * lax.rem(t, 2)
    far_t = place.n_t - 1 - t
    order = (t, near_t, far_t, place.n_t - 1 - near_t)
    n = len(refs) // 2
    for core, mine in ((place.core, refs[:n]), (1 - place.core, refs[n:])):
        own, behind, ahead, last_behind, last_ahead = mine
        half = last_behind.shape[0]
        for j, whole in ((0, own), (-1, behind), (1, ahead), (2, None)):
            at = lax.rem(place.chip + j + place.chips, place.chips) * 2 + core

            def copy(dst, where, lo, hi):
                cuts = [lo, hi] if whole is not None or not lo < half < hi else [lo, half, hi]
                for a, b in zip(cuts, cuts[1:]):
                    if whole is not None:
                        piece = whole[a:b]
                    elif a < half:
                        piece = last_behind[a:b]
                    else:
                        piece = last_ahead[a - half : b - half]
                    start = where[0] * (hi - lo) + (a - lo)
                    rows = pl.ds(pl.multiple_of(start, 16), b - a)
                    if where[1] is None:
                        dst[rows, :] = piece
                    else:
                        dst[rows, where[1]] = piece

            for k in range(place.n_t):
                copy(left, (at, lanes(order[k])), k * n_l, (k + 1) * n_l)
            for p in range(panels):
                lo = n_left + p * n_r
                copy(right, (at, pl.ds(p * SIDE, SIDE)), lo, lo + n_r)
            lo = n_left + panels * n_r
            copy(blocks, (at, None), lo, lo + n_b)


def shift(x, axis, n, k):
    return lax.ppermute(x, axis, [(i, (i + k) % n) for i in range(n)])


def chip_shift(x, n_data, k):
    chips = n_data // 2
    perm = [(2 * a + c, 2 * ((a + k) % chips) + c) for a in range(chips) for c in range(2)]
    return lax.ppermute(x, "dp", perm)


def core_swap(x, n_data):
    return lax.ppermute(x, "dp", [(i, i ^ 1) for i in range(n_data)])


def per_device(
    tokens, cotangent, left_factor, right_factor, block_values, block_rows, block_cols, block_counts
):
    n_f = lax.axis_size("fsdp")
    n_t = lax.axis_size("tensor")
    n_d = lax.axis_size("dp")
    place = Place(n_f, n_t, n_d)
    chips = n_d // 2
    maxb = block_values.shape[0]
    tok_rows, features = tokens.shape
    right = right_factor.reshape(right_factor.shape[0], -1)
    rank_size, quarter = right.shape
    q_blocks = quarter // SIDE
    half = tok_rows // 2
    lists = (block_counts, block_rows, block_cols)
    vm, dma = pltpu.VMEM, pltpu.SemaphoreType.DMA

    def bind(kernel, *args):
        return lambda *refs: kernel(place, *args, *refs)

    def over(n, k_shift):
        return [k_shift(k) for k in range(1, n)]

    wide, narrow = shape((tok_rows, SIDE), F32), shape((tok_rows, SIDE), BF16)
    rank, rank_low, back, *back_out, step = call(
        bind(front_kernel),
        (wide, narrow, wide, narrow, narrow, narrow),
        hbm=(tokens, left_factor, cotangent, right),
        scratch=[
            vm((tok_rows, features), BF16),
            vm((features, SIDE), BF16),
            vm((tok_rows, quarter), BF16),
            vm((rank_size, quarter), BF16),
            vm((tok_rows, rank_size), F32),
            dma((4,)),
        ],
        mib=56,
    )
    rank_in = over(n_f, lambda k: shift(rank_low, "fsdp", n_f, k))
    back_in = [shift(x, "tensor", n_t, k + 1) for k, x in enumerate(back_out)]

    rank, step = call(total_kernel, (narrow,), vmem=(rank, *rank_in), after=(step,))
    ranks = [rank] + over(n_t, lambda k: shift(rank, "tensor", n_t, k))
    back, back_low, step = call(
        total_kernel, (wide, narrow), vmem=(back, *back_in), after=(step,)
    )
    backs = [back] + over(n_f, lambda k: shift(back_low, "fsdp", n_f, k))

    def residual(steps, outs, after, mib):
        return call(
            bind(residual_kernel, q_blocks, steps),
            outs,
            smem=lists,
            hbm=(tokens, block_values),
            scratch=[
                vm((tok_rows, features), BF16),
                vm((maxb, SIDE, SIDE), BF16),
                vm((tok_rows, quarter), F32),
                dma((2,)),
            ],
            after=after,
            mib=mib,
        )

    part, whole = shape((half, quarter), BF16), shape((tok_rows, quarter), BF16)
    ahead, behind, step = residual((2,), (part, part), (step,), 48)

    n_b = maxb // n_d * SIDE
    blocks_mine, blocks_theirs, step = call(
        bind(blocks_kernel),
        (shape((chips, n_b, SIDE), F32), shape((chips, n_b, SIDE), BF16)),
        smem=lists,
        hbm=(tokens, cotangent),
        scratch=[
            vm((tok_rows, features), BF16),
            vm((PANELS, tok_rows, SIDE), BF16),
            dma((PANELS,)),
            dma,
        ],
        after=(step,),
        mib=48,
    )

    def hand_on(*refs):
        refs[-1][0] = 0

    ahead, behind, step = pl.pallas_call(
        hand_on,
        out_shape=(part, part, shape((1,), jnp.int32)),
        in_specs=[HBM] * 2 + [VMEM] * 6 + [SMEM],
        out_specs=(HBM, HBM, SMEM),
        input_output_aliases={0: 0, 1: 1},
        compiler_params=pltpu.CompilerParams(vmem_limit_bytes=8 << 20),
    )(ahead, behind, *ranks[1:], *backs[1:], step)
    from_behind = shift(ahead, "fsdp", n_f, 1)
    from_ahead = shift(behind, "fsdp", n_f, -1)

    n_l = features // n_d
    n_r = rank_size // n_d
    n_rest = q_blocks * n_r + n_b
    n_all = n_l + n_rest
    chunk = shape((n_all, SIDE), BF16)
    mine, *theirs, step = call(
        bind(factors_kernel),
        (shape((chips, n_all, SIDE), F32),) + (chunk,) * chips,
        hbm=(tokens, cotangent),
        vmem=(*ranks, *backs, blocks_mine, blocks_theirs),
        scratch=[
            vm((tok_rows, features), BF16),
            vm((tok_rows, quarter), BF16),
            vm((features, SIDE), F32),
            vm((rank_size, quarter), F32),
            dma((2,)),
        ],
        after=(step,),
        mib=36,
    )
    got = [core_swap(x, n_d) for x in theirs]
    p1, p3, step = residual((1, 3), (whole, whole), (step,), 24)
    own, c_near, c_ahead, c_behind, c_far, step = call(
        lambda *refs: cores_kernel(n_l, *refs),
        (
            shape((n_all, SIDE), F32),
            shape((n_rest, SIDE), F32),
            chunk,
            chunk,
            shape((n_l, SIDE), BF16),
        ),
        vmem=(mine, *got),
        after=(step,),
        mib=16,
    )
    c_from_behind = chip_shift(c_ahead, n_d, 1)
    c_from_ahead = chip_shift(c_behind, n_d, -1)
    c_from_far = chip_shift(c_far, n_d, 2)

    left, c_ahead, c_behind, step = call(
        relay_kernel,
        (shape((n_l, SIDE), BF16),) + (shape((n_rest // 2, SIDE), BF16),) * 2,
        vmem=(own, c_near, c_from_behind, c_from_ahead, c_from_far),
        after=(step,),
    )
    ahead, behind, step = call(
        pass_kernel, (whole, whole), vmem=(p1, p3, from_behind, from_ahead), after=(step,), mib=16
    )
    last_behind = shift(ahead, "fsdp", n_f, 1)
    last_ahead = shift(behind, "fsdp", n_f, -1)
    left_near = lax.ppermute(left, "tensor", [(i, i ^ 1) for i in range(n_t)])
    c_last_behind = chip_shift(c_ahead, n_d, 1)
    c_last_ahead = chip_shift(c_behind, n_d, -1)
    left_pair, step = call(
        stack_kernel, (shape((2 * n_l, SIDE), BF16),), vmem=(left, left_near), after=(step,)
    )
    left_far = lax.ppermute(left_pair, "tensor", [(i, n_t - 1 - i) for i in range(n_t)])
    low, step = call(
        bind(low_kernel, q_blocks),
        (shape((tok_rows, quarter), F32),),
        smem=lists,
        hbm=(tokens, block_values),
        vmem=(*ranks, right),
        scratch=[
            vm((tok_rows, features), BF16),
            vm((maxb, SIDE, SIDE), BF16),
            dma((2,)),
        ],
        after=(step,),
        mib=24,
    )
    n_msg = n_t * n_l + n_rest
    message, step = call(
        chunk_kernel,
        (shape((n_msg, SIDE), BF16),),
        vmem=(own, c_from_behind, c_from_ahead, c_last_behind, c_last_ahead, left_pair, left_far),
        after=(step,),
    )

    m_behind = chip_shift(message, n_d, 1)
    m_ahead = chip_shift(message, n_d, -1)
    m_last_behind = chip_shift(m_behind[: n_msg // 2], n_d, 1)
    m_last_ahead = chip_shift(m_ahead[n_msg // 2 :], n_d, -1)
    ours = (message, m_behind, m_ahead, m_last_behind, m_last_ahead)
    partner = [core_swap(x, n_d) for x in ours]

    out_left, out_right, out_blocks, step = call(
        bind(spread_kernel),
        (
            shape((features, rank_size), BF16),
            shape((rank_size, quarter), BF16),
            shape((maxb * SIDE, SIDE), BF16),
        ),
        vmem=(*ours, *partner),
        mib=14,
    )
    mixed, _ = call(
        finish_kernel, (whole,), vmem=(low, last_behind, last_ahead), mib=12
    )
    return (
        mixed.reshape(tok_rows, 1, quarter),
        out_left,
        out_right.reshape(right_factor.shape),
        out_blocks.reshape(maxb, SIDE, SIDE),
    )


def solution(mesh):
    return jax.shard_map(
        per_device,
        mesh=mesh,
        in_specs=(
            P("dp", "fsdp"),
            P("dp", "tensor"),
            P("fsdp", None),
            P(None, "tensor", "fsdp"),
            P(("fsdp", "tensor"), None, None),
            P(("fsdp", "tensor")),
            P(("fsdp", "tensor")),
            P(),
        ),
        out_specs=(
            P("dp", "tensor", "fsdp"),
            P("fsdp", None),
            P(None, "tensor", "fsdp"),
            P(("fsdp", "tensor"), None, None),
        ),
        check_vma=False,
    )
```

```python
import jax
import jax.numpy as jnp
from jax import lax
from jax.experimental import pallas as pl
from jax.experimental.pallas import tpu as pltpu
from jax.sharding import PartitionSpec as P

F32 = jnp.float32
BF16 = jnp.bfloat16
SIDE = 128
SMEM = pl.BlockSpec(memory_space=pltpu.SMEM)
VMEM = pl.BlockSpec(memory_space=pltpu.VMEM)
HBM = pl.BlockSpec(memory_space=pl.ANY)
ROWS = (((0,), (0,)), ((), ()))
COLS = (((1,), (1,)), ((), ()))


def lanes(block):
    return pl.ds(pl.multiple_of(block * SIDE, SIDE), SIDE)


def span(block, size):
    return pl.ds(pl.multiple_of(block * size, size), size)


def shape(dims, dtype):
    return jax.ShapeDtypeStruct(dims, dtype)


def call(kernel, outs, smem=(), hbm=(), vmem=(), scratch=(), after=(), mib=8):
    n_in, n_out = len(smem) + len(hbm) + len(vmem), len(outs)

    def body(*refs):
        rest = refs[n_in + len(after) :]
        rest[n_out][0] = 0
        kernel(*refs[:n_in], *rest[:n_out], *rest[n_out + 1 :])

    return pl.pallas_call(
        body,
        out_shape=(*outs, shape((1,), jnp.int32)),
        in_specs=[SMEM] * len(smem) + [HBM] * len(hbm) + [VMEM] * len(vmem) + [SMEM] * len(after),
        out_specs=(VMEM,) * n_out + (SMEM,),
        scratch_shapes=list(scratch),
        cost_estimate=pl.CostEstimate(flops=0, bytes_accessed=0, transcendentals=0),
        compiler_params=pltpu.CompilerParams(vmem_limit_bytes=mib << 20),
    )(*smem, *hbm, *vmem, *after)


class Place:
    def __init__(self, n_f, n_t, n_d):
        self.n_f, self.n_t, self.n_d, self.chips = n_f, n_t, n_d, n_d // 2

    f = property(lambda self: lax.axis_index("fsdp"))
    t = property(lambda self: lax.axis_index("tensor"))
    chip = property(lambda self: lax.axis_index("dp") // 2)
    core = property(lambda self: lax.rem(lax.axis_index("dp"), 2))

    def live(self, counts):
        return counts[self.f * self.n_t + self.t]


def fetch(*pairs_and_sems):
    copies = [pltpu.make_async_copy(src, dst, sem) for src, dst, sem in pairs_and_sems]
    for copy in copies:
        copy.start()
    return copies


def add_blocks(place, q_blocks, step, counts, rows, cols, tok, vals, acc):
    first = lax.rem(place.f + step, place.n_f) * q_blocks

    def body(s, carry):
        col = cols[s] - first

        @pl.when((col >= 0) & (col < q_blocks))
        def _():
            acc[:, lanes(col)] += jnp.dot(tok[:, lanes(rows[s])], vals[s], preferred_element_type=F32)

        return carry

    lax.fori_loop(0, place.live(counts), body, 0)


def front_kernel(
    place, q_blocks, counts, rows, cols, tok, left, cot, right, vals,
    rank, low, back, s1, s2, s3, ahead, behind,
    tokv, leftv, cotv, rightv, valv, full, acc, sems,
):
    quarter = cotv.shape[1]
    here = pl.ds(pl.multiple_of(place.f * quarter, SIDE), quarter)
    c_tok, c_left, c_val, c_cot, c_right = fetch(
        (tok, tokv, sems.at[0]),
        (left.at[:, lanes(place.t)], leftv, sems.at[1]),
        (vals, valv, sems.at[2]),
        (cot.at[:, here], cotv, sems.at[3]),
        (right, rightv, sems.at[4]),
    )
    acc[...] = jnp.zeros_like(acc)
    c_tok.wait()
    c_left.wait()
    rank[...] = jnp.dot(tokv[...], leftv[...], preferred_element_type=F32)
    low[...] = rank[...].astype(BF16)
    c_val.wait()
    add_blocks(place, q_blocks, place.n_f // 2, counts, rows, cols, tokv, valv, acc)
    half = ahead.shape[0]
    ahead[...] = acc[:half].astype(BF16)
    behind[...] = acc[half:].astype(BF16)
    c_cot.wait()
    c_right.wait()
    full[...] = lax.dot_general(cotv[...], rightv[...], COLS, preferred_element_type=F32)
    back[...] = full[:, lanes(place.t)]
    for k, out in ((1, s1), (2, s2), (3, s3)):
        out[...] = full[:, lanes(lax.rem(place.t + k, place.n_t))].astype(BF16)


def total_kernel(own, g1, g2, g3, *outs):
    total = own[...] + g1[...].astype(F32) + g2[...].astype(F32) + g3[...].astype(F32)
    for out in outs:
        out[...] = total.astype(out.dtype)


def residual_kernel(place, q_blocks, steps, counts, rows, cols, tok, vals, *refs):
    outs, acc = refs[:-1], refs[-1]
    for step, out in zip(steps, outs):
        acc[...] = jnp.zeros_like(acc)
        add_blocks(place, q_blocks, step, counts, rows, cols, tok, vals, acc)
        out[...] = acc[...].astype(BF16)


def blocks_kernel(place, counts, rows, cols, tok, cot, mine, theirs):
    live = place.live(counts)
    per = mine.shape[1] // SIDE

    def body(owner, carry):
        grads = []
        for u in range(per):
            s = owner * per + u
            grad = lax.dot_general(
                tok[:, lanes(rows[s])], cot[:, lanes(cols[s])], ROWS, preferred_element_type=F32
            )
            grads.append(jnp.where(s < live, grad, jnp.zeros_like(grad)))
        j = lax.rem(owner // 2 - place.chip + place.chips, place.chips)
        keep = lax.rem(owner, 2) == place.core

        @pl.when(keep)
        def _():
            for u, grad in enumerate(grads):
                mine[j, u * SIDE : (u + 1) * SIDE] = grad

        @pl.when(jnp.logical_not(keep))
        def _():
            for u, grad in enumerate(grads):
                theirs[j, u * SIDE : (u + 1) * SIDE] = grad.astype(BF16)

        return carry

    lax.fori_loop(0, place.n_d, body, 0)


def factors_kernel(
    place, tok, cot, g0, g1, g2, g3, b0, b1, b2, b3, blocks_mine, blocks_theirs,
    mine, out1, out2, out3, theirs0, left, right,
):
    quarter = right.shape[1]
    here = pl.ds(pl.multiple_of(place.f * quarter, SIDE), quarter)
    n_l = left.shape[0] // place.n_d
    n_r = right.shape[0] // place.n_d
    n_lr = n_l + quarter // SIDE * n_r
    outs = (out1, out2, out3)
    theirs = (theirs0, *outs)
    for j in range(place.chips):
        mine[j, n_lr:] = blocks_mine[j]
        theirs[j][n_lr : n_lr + blocks_theirs.shape[1]] = blocks_theirs[j]
    back = b0[...] + b1[...].astype(F32) + b2[...].astype(F32) + b3[...].astype(F32)
    left[...] = lax.dot_general(
        back.astype(BF16), tok[...], ROWS, preferred_element_type=F32
    ).T
    for k, g in enumerate((g0, g1, g2, g3)):
        at = span(lax.rem(place.t - k + place.n_t, place.n_t), SIDE)
        right[at, :] = lax.dot_general(
            g[...], cot[:, here], ROWS, preferred_element_type=F32
        )
    for j in range(place.chips):
        chip = lax.rem(place.chip + j, place.chips)
        for core, out in ((place.core, mine.at[j]), (1 - place.core, theirs[j])):
            at = chip * 2 + core
            out[:n_l] = left[span(at, n_l), :].astype(out.dtype)
            for p in range(quarter // SIDE):
                out[n_l + p * n_r : n_l + (p + 1) * n_r] = right[
                    span(at, n_r), p * SIDE : (p + 1) * SIDE
                ].astype(out.dtype)
    row, n_all = 0, theirs0.shape[0]
    for out in outs:
        extra = out.shape[0] - n_all
        out[n_all:] = theirs0[row : row + extra]
        row += extra


def cores_kernel(n_l, mine, got1, got2, got3, own, near, ahead, behind, far):
    mid = n_l + (own.shape[0] - n_l) // 2
    got = (None, got1, got2, got3)

    def both(k, lo, hi):
        return mine[k, lo:hi] + got[k][lo:hi].astype(F32)

    row = 0
    for g in got[1:]:
        extra = g.shape[0] - own.shape[0]
        own[row : row + extra] = mine[0, row : row + extra] + g[own.shape[0] :].astype(F32)
        row += extra

    end = own.shape[0]
    half = end - mid
    far[...] = both(2, 0, n_l).astype(BF16)
    ahead[:n_l] = both(1, 0, n_l).astype(BF16)
    behind[:n_l] = both(3, 0, n_l).astype(BF16)
    ahead[n_l:mid] = both(2, n_l, mid).astype(BF16)
    behind[n_l:mid] = both(2, mid, end).astype(BF16)
    ahead[mid:] = both(1, mid, end).astype(BF16)
    behind[mid:] = both(3, n_l, mid).astype(BF16)
    near[:half] = both(1, n_l, mid)
    near[half:] = both(3, mid, end)


def relay_kernel(own, near, from_behind, from_ahead, from_far, left, ahead, behind):
    n_l, half = left.shape[0], ahead.shape[0]
    mid = n_l + half
    left[...] = (
        own[:n_l] + from_behind[:n_l].astype(F32) + from_ahead[:n_l].astype(F32)
        + from_far[...].astype(F32)
    ).astype(BF16)
    ahead[...] = (near[:half] + from_behind[n_l:mid].astype(F32)).astype(BF16)
    behind[...] = (near[half:] + from_ahead[n_l:mid].astype(F32)).astype(BF16)


def chunk_kernel(own, from_behind, from_ahead, last_behind, last_ahead, pair, far, out):
    half, n = last_behind.shape[0], pair.shape[0]
    n_l = own.shape[0] - 2 * half
    mid = n_l + half
    out[:n] = pair[...]
    out[n : 2 * n] = far[...]
    out[2 * n : 2 * n + half] = (
        own[n_l:mid] + from_ahead[mid:].astype(F32) + last_behind[...].astype(F32)
    ).astype(BF16)
    out[2 * n + half :] = (
        own[mid:] + from_behind[mid:].astype(F32) + last_ahead[...].astype(F32)
    ).astype(BF16)


def stack_kernel(a, b, out):
    out[: a.shape[0]] = a[...]
    out[a.shape[0] :] = b[...]


def pass_kernel(p1, p3, from_behind, from_ahead, ahead, behind):
    half = from_behind.shape[0]
    ahead[:half] = (p1[:half].astype(F32) + from_behind[...].astype(F32)).astype(BF16)
    ahead[half:] = p1[half:]
    behind[:half] = p3[:half]
    behind[half:] = (p3[half:].astype(F32) + from_ahead[...].astype(F32)).astype(BF16)


def low_kernel(place, q_blocks, counts, rows, cols, tok, vals, g0, g1, g2, g3, right, out):
    acc = jnp.zeros(out.shape, F32)
    for k, g in enumerate((g0, g1, g2, g3)):
        at = span(lax.rem(place.t - k + place.n_t, place.n_t), SIDE)
        acc += jnp.dot(g[...], right[at, :], preferred_element_type=F32)
    out[...] = acc
    add_blocks(place, q_blocks, 0, counts, rows, cols, tok, vals, out)


def finish_kernel(low, from_behind, from_ahead, out):
    out[...] = (low[...] + from_behind[...].astype(F32) + from_ahead[...].astype(F32)).astype(BF16)


def spread_kernel(place, *refs):
    refs, (left, right, blocks) = refs[:-3], refs[-3:]
    n_l = left.shape[0] // place.n_d
    n_r = right.shape[0] // place.n_d
    n_b = blocks.shape[0] // place.n_d
    panels = right.shape[1] // SIDE
    n_left = place.n_t * n_l
    t = place.t
    near_t = t + 1 - 2 * lax.rem(t, 2)
    far_t = place.n_t - 1 - t
    order = (t, near_t, far_t, place.n_t - 1 - near_t)
    n = len(refs) // 2
    for core, mine in ((place.core, refs[:n]), (1 - place.core, refs[n:])):
        own, behind, ahead, last = mine
        half = last.shape[0] // 2
        last_behind, last_ahead = last.at[:half], last.at[half:]
        for j, whole in ((0, own), (-1, behind), (1, ahead), (2, None)):
            at = lax.rem(place.chip + j + place.chips, place.chips) * 2 + core

            def copy(dst, where, lo, hi):
                cuts = [lo, hi] if whole is not None or not lo < half < hi else [lo, half, hi]
                for a, b in zip(cuts, cuts[1:]):
                    if whole is not None:
                        piece = whole[a:b]
                    elif a < half:
                        piece = last_behind[a:b]
                    else:
                        piece = last_ahead[a - half : b - half]
                    start = where[0] * (hi - lo) + (a - lo)
                    rows = pl.ds(pl.multiple_of(start, 16), b - a)
                    if where[1] is None:
                        dst[rows, :] = piece
                    else:
                        dst[rows, where[1]] = piece

            for k in range(place.n_t):
                copy(left, (at, lanes(order[k])), k * n_l, (k + 1) * n_l)
            for p in range(panels):
                lo = n_left + p * n_r
                copy(right, (at, pl.ds(p * SIDE, SIDE)), lo, lo + n_r)
            lo = n_left + panels * n_r
            copy(blocks, (at, None), lo, lo + n_b)


def shift(x, axis, n, k):
    return lax.ppermute(x, axis, [(i, (i + k) % n) for i in range(n)])


def chip_shift(x, n_data, k):
    chips = n_data // 2
    perm = [(2 * a + c, 2 * ((a + k) % chips) + c) for a in range(chips) for c in range(2)]
    return lax.ppermute(x, "dp", perm)


def core_swap(x, n_data):
    return lax.ppermute(x, "dp", [(i, i ^ 1) for i in range(n_data)])


def per_device(
    tokens, cotangent, left_factor, right_factor, block_values, block_rows, block_cols, block_counts
):
    n_f = lax.axis_size("fsdp")
    n_t = lax.axis_size("tensor")
    n_d = lax.axis_size("dp")
    place = Place(n_f, n_t, n_d)
    chips = n_d // 2
    maxb = block_values.shape[0]
    tok_rows, features = tokens.shape
    right = right_factor.reshape(right_factor.shape[0], -1)
    rank_size, quarter = right.shape
    q_blocks = quarter // SIDE
    half = tok_rows // 2
    lists = (block_counts, block_rows, block_cols)
    vm, dma = pltpu.VMEM, pltpu.SemaphoreType.DMA

    def bind(kernel, *args):
        return lambda *refs: kernel(place, *args, *refs)

    def over(n, k_shift):
        return [k_shift(k) for k in range(1, n)]

    wide, narrow = shape((tok_rows, SIDE), F32), shape((tok_rows, SIDE), BF16)
    part, whole = shape((half, quarter), BF16), shape((tok_rows, quarter), BF16)
    rank, rank_low, back, *back_out, ahead, behind, step = call(
        bind(front_kernel, q_blocks),
        (wide, narrow, wide, narrow, narrow, narrow, part, part),
        smem=lists,
        hbm=(tokens, left_factor, cotangent, right, block_values),
        scratch=[
            vm((tok_rows, features), BF16),
            vm((features, SIDE), BF16),
            vm((tok_rows, quarter), BF16),
            vm((rank_size, quarter), BF16),
            vm((maxb, SIDE, SIDE), BF16),
            vm((tok_rows, rank_size), F32),
            vm((tok_rows, quarter), F32),
            dma((5,)),
        ],
        mib=50,
    )
    rank_in = over(n_f, lambda k: shift(rank_low, "fsdp", n_f, k))
    back_in = [shift(x, "tensor", n_t, k + 1) for k, x in enumerate(back_out)]

    rank, step = call(total_kernel, (narrow,), vmem=(rank, *rank_in), after=(step,))
    ranks = [rank] + over(n_t, lambda k: shift(rank, "tensor", n_t, k))
    back, back_low, step = call(
        total_kernel, (wide, narrow), vmem=(back, *back_in), after=(step,)
    )
    backs = [back] + over(n_f, lambda k: shift(back_low, "fsdp", n_f, k))

    def hand_on(*refs):
        refs[-1][0] = 0

    ahead, behind, step = pl.pallas_call(
        hand_on,
        out_shape=(part, part, shape((1,), jnp.int32)),
        in_specs=[HBM] * 2 + [VMEM] * 6 + [SMEM],
        out_specs=(HBM, HBM, SMEM),
        input_output_aliases={0: 0, 1: 1},
        compiler_params=pltpu.CompilerParams(vmem_limit_bytes=8 << 20),
    )(ahead, behind, *ranks[1:], *backs[1:], step)
    from_behind = shift(ahead, "fsdp", n_f, 1)
    from_ahead = shift(behind, "fsdp", n_f, -1)

    n_b = maxb // n_d * SIDE
    blocks_mine, blocks_theirs, step = call(
        bind(blocks_kernel),
        (shape((chips, n_b, SIDE), F32), shape((chips, n_b, SIDE), BF16)),
        smem=lists,
        vmem=(tokens, cotangent),
        after=(step,),
        mib=20,
    )

    n_l = features // n_d
    n_r = rank_size // n_d
    n_rest = q_blocks * n_r + n_b
    n_all = n_l + n_rest
    chunk = shape((n_all, SIDE), BF16)
    extra = -(-n_all // 3 // 16) * 16
    mine, *theirs, step = call(
        bind(factors_kernel),
        (shape((chips, n_all, SIDE), F32),)
        + tuple(shape((n_all + n, SIDE), BF16) for n in (extra, extra, n_all - 2 * extra)),
        vmem=(tokens, cotangent, *ranks, *backs, blocks_mine, blocks_theirs),
        scratch=[
            vm((n_all, SIDE), BF16),
            vm((features, SIDE), F32),
            vm((rank_size, quarter), F32),
        ],
        after=(step,),
        mib=36,
    )
    got = [core_swap(x, n_d) for x in theirs]
    p1, p3, step = call(
        bind(residual_kernel, q_blocks, (1, 3)),
        (whole, whole),
        smem=lists,
        vmem=(tokens, block_values),
        scratch=[vm((tok_rows, quarter), F32)],
        after=(step,),
        mib=20,
    )
    own, c_near, c_ahead, c_behind, c_far, step = call(
        lambda *refs: cores_kernel(n_l, *refs),
        (
            shape((n_all, SIDE), F32),
            shape((n_rest, SIDE), F32),
            chunk,
            chunk,
            shape((n_l, SIDE), BF16),
        ),
        vmem=(mine, *got),
        after=(step,),
        mib=16,
    )
    c_from_behind = chip_shift(c_ahead, n_d, 1)
    c_from_ahead = chip_shift(c_behind, n_d, -1)
    c_from_far = chip_shift(c_far, n_d, 2)

    ahead, behind, step = call(
        pass_kernel, (whole, whole), vmem=(p1, p3, from_behind, from_ahead), after=(step,), mib=16
    )
    last_behind = shift(ahead, "fsdp", n_f, 1)
    last_ahead = shift(behind, "fsdp", n_f, -1)
    low, step = call(
        bind(low_kernel, q_blocks),
        (shape((tok_rows, quarter), F32),),
        smem=lists,
        vmem=(tokens, block_values, *ranks, right),
        after=(step,),
        mib=20,
    )

    left, c_ahead, c_behind, step = call(
        relay_kernel,
        (shape((n_l, SIDE), BF16),) + (shape((n_rest // 2, SIDE), BF16),) * 2,
        vmem=(own, c_near, c_from_behind, c_from_ahead, c_from_far),
        after=(step,),
    )
    left_near = lax.ppermute(left, "tensor", [(i, i ^ 1) for i in range(n_t)])
    c_last_behind = chip_shift(c_ahead, n_d, 1)
    c_last_ahead = chip_shift(c_behind, n_d, -1)
    left_pair, step = call(
        stack_kernel, (shape((2 * n_l, SIDE), BF16),), vmem=(left, left_near), after=(step,)
    )
    left_far = lax.ppermute(left_pair, "tensor", [(i, n_t - 1 - i) for i in range(n_t)])
    n_msg = n_t * n_l + n_rest
    message, step = call(
        chunk_kernel,
        (shape((n_msg, SIDE), BF16),),
        vmem=(own, c_from_behind, c_from_ahead, c_last_behind, c_last_ahead, left_pair, left_far),
        after=(step,),
    )

    m_behind = chip_shift(message, n_d, 1)
    m_ahead = chip_shift(message, n_d, -1)
    m_last_behind = chip_shift(m_behind[: n_msg // 2], n_d, 1)
    m_last_ahead = chip_shift(m_ahead[n_msg // 2 :], n_d, -1)
    ours = (message, m_behind, m_ahead, jnp.concatenate([m_last_behind, m_last_ahead], axis=0))
    partner = [core_swap(x, n_d) for x in ours]

    out_left, out_right, out_blocks, step = call(
        bind(spread_kernel),
        (
            shape((features, rank_size), BF16),
            shape((rank_size, quarter), BF16),
            shape((maxb * SIDE, SIDE), BF16),
        ),
        vmem=(*ours, *partner),
        mib=14,
    )
    mixed, _ = call(
        finish_kernel, (whole,), vmem=(low, last_behind, last_ahead), mib=12
    )
    return (
        mixed.reshape(tok_rows, 1, quarter),
        out_left,
        out_right.reshape(right_factor.shape),
        out_blocks.reshape(maxb, SIDE, SIDE),
    )


def solution(mesh):
    return jax.shard_map(
        per_device,
        mesh=mesh,
        in_specs=(
            P("dp", "fsdp"),
            P("dp", "tensor"),
            P("fsdp", None),
            P(None, "tensor", "fsdp"),
            P(("fsdp", "tensor"), None, None),
            P(("fsdp", "tensor")),
            P(("fsdp", "tensor")),
            P(),
        ),
        out_specs=(
            P("dp", "tensor", "fsdp"),
            P("fsdp", None),
            P(None, "tensor", "fsdp"),
            P(("fsdp", "tensor"), None, None),
        ),
        check_vma=False,
    )
```

```python
import jax
import jax.numpy as jnp
from jax import lax
from jax.experimental import pallas as pl
from jax.experimental.pallas import tpu as pltpu
from jax.sharding import PartitionSpec as P

F32 = jnp.float32
BF16 = jnp.bfloat16
SIDE = 128
SMEM = pl.BlockSpec(memory_space=pltpu.SMEM)
VMEM = pl.BlockSpec(memory_space=pltpu.VMEM)
HBM = pl.BlockSpec(memory_space=pl.ANY)
ROWS = (((0,), (0,)), ((), ()))
COLS = (((1,), (1,)), ((), ()))


def lanes(block):
    return pl.ds(pl.multiple_of(block * SIDE, SIDE), SIDE)


def span(block, size):
    return pl.ds(pl.multiple_of(block * size, size), size)


def shape(dims, dtype):
    return jax.ShapeDtypeStruct(dims, dtype)


def call(kernel, outs, smem=(), hbm=(), vmem=(), scratch=(), after=(), mib=8):
    n_in, n_out = len(smem) + len(hbm) + len(vmem), len(outs)

    def body(*refs):
        rest = refs[n_in + len(after) :]
        rest[n_out][0] = 0
        kernel(*refs[:n_in], *rest[:n_out], *rest[n_out + 1 :])

    return pl.pallas_call(
        body,
        out_shape=(*outs, shape((1,), jnp.int32)),
        in_specs=[SMEM] * len(smem) + [HBM] * len(hbm) + [VMEM] * len(vmem) + [SMEM] * len(after),
        out_specs=(VMEM,) * n_out + (SMEM,),
        scratch_shapes=list(scratch),
        cost_estimate=pl.CostEstimate(flops=0, bytes_accessed=0, transcendentals=0),
        compiler_params=pltpu.CompilerParams(vmem_limit_bytes=mib << 20),
    )(*smem, *hbm, *vmem, *after)


class Place:
    def __init__(self, n_f, n_t, n_d):
        self.n_f, self.n_t, self.n_d, self.chips = n_f, n_t, n_d, n_d // 2

    f = property(lambda self: lax.axis_index("fsdp"))
    t = property(lambda self: lax.axis_index("tensor"))
    chip = property(lambda self: lax.axis_index("dp") // 2)
    core = property(lambda self: lax.rem(lax.axis_index("dp"), 2))

    def live(self, counts):
        return counts[self.f * self.n_t + self.t]


def fetch(*pairs_and_sems):
    copies = [pltpu.make_async_copy(src, dst, sem) for src, dst, sem in pairs_and_sems]
    for copy in copies:
        copy.start()
    return copies


def add_blocks(place, q_blocks, step, counts, rows, cols, tok, vals, acc):
    first = lax.rem(place.f + step, place.n_f) * q_blocks

    def body(s, carry):
        col = cols[s] - first

        @pl.when((col >= 0) & (col < q_blocks))
        def _():
            acc[:, lanes(col)] += jnp.dot(tok[:, lanes(rows[s])], vals[s], preferred_element_type=F32)

        return carry

    lax.fori_loop(0, place.live(counts), body, 0)


def front_kernel(
    place, q_blocks, counts, rows, cols, tok, left, cot, right, vals,
    rank, low, back, s1, s2, s3, ahead, behind,
    tokv, leftv, cotv, rightv, valv, full, acc, sems,
):
    quarter = cotv.shape[1]
    here = pl.ds(pl.multiple_of(place.f * quarter, SIDE), quarter)
    c_tok, c_left, c_val, c_cot, c_right = fetch(
        (tok, tokv, sems.at[0]),
        (left.at[:, lanes(place.t)], leftv, sems.at[1]),
        (vals, valv, sems.at[2]),
        (cot.at[:, here], cotv, sems.at[3]),
        (right, rightv, sems.at[4]),
    )
    acc[...] = jnp.zeros_like(acc)
    c_tok.wait()
    c_left.wait()
    rank[...] = jnp.dot(tokv[...], leftv[...], preferred_element_type=F32)
    low[...] = rank[...].astype(BF16)
    c_val.wait()
    add_blocks(place, q_blocks, place.n_f // 2, counts, rows, cols, tokv, valv, acc)
    half = ahead.shape[0]
    ahead[...] = acc[:half].astype(BF16)
    behind[...] = acc[half:].astype(BF16)
    c_cot.wait()
    c_right.wait()
    full[...] = lax.dot_general(cotv[...], rightv[...], COLS, preferred_element_type=F32)
    back[...] = full[:, lanes(place.t)]
    for k, out in ((1, s1), (2, s2), (3, s3)):
        out[...] = full[:, lanes(lax.rem(place.t + k, place.n_t))].astype(BF16)


def total_kernel(own, g1, g2, g3, *outs):
    total = own[...] + g1[...].astype(F32) + g2[...].astype(F32) + g3[...].astype(F32)
    for out in outs:
        out[...] = total.astype(out.dtype)


def residual_kernel(place, q_blocks, counts, rows, cols, tok, vals, p1, p3, acc):
    acc[...] = jnp.zeros_like(acc)
    n_f, f = place.n_f, place.f

    def body(s, carry):
        q = cols[s] // q_blocks
        step = lax.rem(q - f + n_f, n_f)

        @pl.when(lax.rem(step, 2) == 1)
        def _():
            acc[step // 2, :, lanes(cols[s] - q * q_blocks)] += jnp.dot(
                tok[:, lanes(rows[s])], vals[s], preferred_element_type=F32
            )

        return carry

    lax.fori_loop(0, place.live(counts), body, 0)
    p1[...] = acc[0].astype(BF16)
    p3[...] = acc[1].astype(BF16)


def blocks_kernel(place, counts, rows, cols, tok, cot, mine, theirs):
    live = place.live(counts)
    per = mine.shape[1] // SIDE

    def body(owner, carry):
        grads = []
        for u in range(per):
            s = owner * per + u
            grad = lax.dot_general(
                tok[:, lanes(rows[s])], cot[:, lanes(cols[s])], ROWS, preferred_element_type=F32
            )
            grads.append(jnp.where(s < live, grad, jnp.zeros_like(grad)))
        j = lax.rem(owner // 2 - place.chip + place.chips, place.chips)
        keep = lax.rem(owner, 2) == place.core

        @pl.when(keep)
        def _():
            for u, grad in enumerate(grads):
                mine[j, u * SIDE : (u + 1) * SIDE] = grad

        @pl.when(jnp.logical_not(keep))
        def _():
            for u, grad in enumerate(grads):
                theirs[j, u * SIDE : (u + 1) * SIDE] = grad.astype(BF16)

        return carry

    lax.fori_loop(0, place.n_d, body, 0)


def factors_kernel(
    place, tok, cot, g0, g1, g2, g3, b0, b1, b2, b3, blocks_mine, blocks_theirs,
    mine, out1, out2, out3, theirs0, tokv, cotv, left, right, sems,
):
    quarter = right.shape[1]
    here = pl.ds(pl.multiple_of(place.f * quarter, SIDE), quarter)
    c_tok, c_cot = fetch((tok, tokv, sems.at[0]), (cot.at[:, here], cotv, sems.at[1]))
    n_l = left.shape[0] // place.n_d
    n_r = right.shape[0] // place.n_d
    n_lr = n_l + quarter // SIDE * n_r
    outs = (out1, out2, out3)
    theirs = (theirs0, *outs)
    for j in range(place.chips):
        mine[j, n_lr:] = blocks_mine[j]
        theirs[j][n_lr : n_lr + blocks_theirs.shape[1]] = blocks_theirs[j]
    c_tok.wait()
    back = b0[...] + b1[...].astype(F32) + b2[...].astype(F32) + b3[...].astype(F32)
    left[...] = lax.dot_general(
        back.astype(BF16), tokv[...], ROWS, preferred_element_type=F32
    ).T
    c_cot.wait()
    for k, g in enumerate((g0, g1, g2, g3)):
        at = span(lax.rem(place.t - k + place.n_t, place.n_t), SIDE)
        right[at, :] = lax.dot_general(
            g[...], cotv[...], ROWS, preferred_element_type=F32
        )
    for j in range(place.chips):
        chip = lax.rem(place.chip + j, place.chips)
        for core, out in ((place.core, mine.at[j]), (1 - place.core, theirs[j])):
            at = chip * 2 + core
            out[:n_l] = left[span(at, n_l), :].astype(out.dtype)
            for p in range(quarter // SIDE):
                out[n_l + p * n_r : n_l + (p + 1) * n_r] = right[
                    span(at, n_r), p * SIDE : (p + 1) * SIDE
                ].astype(out.dtype)
    row, n_all = 0, theirs0.shape[0]
    for out in outs:
        extra = out.shape[0] - n_all
        out[n_all:] = theirs0[row : row + extra]
        row += extra


def cores_kernel(n_l, mine, got1, got2, got3, own, near, ahead, behind, far):
    mid = n_l + (own.shape[0] - n_l) // 2
    got = (None, got1, got2, got3)

    def both(k, lo, hi):
        return mine[k, lo:hi] + got[k][lo:hi].astype(F32)

    row = 0
    for g in got[1:]:
        extra = g.shape[0] - own.shape[0]
        own[row : row + extra] = mine[0, row : row + extra] + g[own.shape[0] :].astype(F32)
        row += extra

    end = own.shape[0]
    half = end - mid
    far[...] = both(2, 0, n_l).astype(BF16)
    ahead[:n_l] = both(1, 0, n_l).astype(BF16)
    behind[:n_l] = both(3, 0, n_l).astype(BF16)
    ahead[n_l:mid] = both(2, n_l, mid).astype(BF16)
    behind[n_l:mid] = both(2, mid, end).astype(BF16)
    ahead[mid:] = both(1, mid, end).astype(BF16)
    behind[mid:] = both(3, n_l, mid).astype(BF16)
    near[:half] = both(1, n_l, mid)
    near[half:] = both(3, mid, end)


def relay_kernel(own, near, from_behind, from_ahead, from_far, left, ahead, behind):
    n_l, half = left.shape[0], ahead.shape[0]
    mid = n_l + half
    left[...] = (
        own[:n_l] + from_behind[:n_l].astype(F32) + from_ahead[:n_l].astype(F32)
        + from_far[...].astype(F32)
    ).astype(BF16)
    ahead[...] = (near[:half] + from_behind[n_l:mid].astype(F32)).astype(BF16)
    behind[...] = (near[half:] + from_ahead[n_l:mid].astype(F32)).astype(BF16)


def chunk_kernel(own, from_behind, from_ahead, last_behind, last_ahead, pair, far, out):
    half, n = last_behind.shape[0], pair.shape[0]
    n_l = own.shape[0] - 2 * half
    mid = n_l + half
    out[:n] = pair[...]
    out[n : 2 * n] = far[...]
    out[2 * n : 2 * n + half] = (
        own[n_l:mid] + from_ahead[mid:].astype(F32) + last_behind[...].astype(F32)
    ).astype(BF16)
    out[2 * n + half :] = (
        own[mid:] + from_behind[mid:].astype(F32) + last_ahead[...].astype(F32)
    ).astype(BF16)


def stack_kernel(a, b, out):
    out[: a.shape[0]] = a[...]
    out[a.shape[0] :] = b[...]


def pass_kernel(p1, p3, from_behind, from_ahead, ahead, behind):
    half = from_behind.shape[0]
    ahead[:half] = (p1[:half].astype(F32) + from_behind[...].astype(F32)).astype(BF16)
    ahead[half:] = p1[half:]
    behind[:half] = p3[:half]
    behind[half:] = (p3[half:].astype(F32) + from_ahead[...].astype(F32)).astype(BF16)


def low_kernel(place, q_blocks, counts, rows, cols, tok, vals, g0, g1, g2, g3, right, out):
    acc = jnp.zeros(out.shape, F32)
    for k, g in enumerate((g0, g1, g2, g3)):
        at = span(lax.rem(place.t - k + place.n_t, place.n_t), SIDE)
        acc += jnp.dot(g[...], right[at, :], preferred_element_type=F32)
    out[...] = acc
    add_blocks(place, q_blocks, 0, counts, rows, cols, tok, vals, out)


def finish_kernel(low, from_behind, from_ahead, out):
    out[...] = (low[...] + from_behind[...].astype(F32) + from_ahead[...].astype(F32)).astype(BF16)


def spread_kernel(place, *refs):
    refs, (left, right, blocks) = refs[:-3], refs[-3:]
    n_l = left.shape[0] // place.n_d
    n_r = right.shape[0] // place.n_d
    n_b = blocks.shape[0] // place.n_d
    panels = right.shape[1] // SIDE
    n_left = place.n_t * n_l
    t = place.t
    near_t = t + 1 - 2 * lax.rem(t, 2)
    far_t = place.n_t - 1 - t
    order = (t, near_t, far_t, place.n_t - 1 - near_t)
    n = len(refs) // 2
    for core, mine in ((place.core, refs[:n]), (1 - place.core, refs[n:])):
        own, behind, ahead, last = mine
        half = last.shape[0] // 2
        last_behind, last_ahead = last.at[:half], last.at[half:]
        for j, whole in ((0, own), (-1, behind), (1, ahead), (2, None)):
            at = lax.rem(place.chip + j + place.chips, place.chips) * 2 + core

            def copy(dst, where, lo, hi):
                cuts = [lo, hi] if whole is not None or not lo < half < hi else [lo, half, hi]
                for a, b in zip(cuts, cuts[1:]):
                    if whole is not None:
                        piece = whole[a:b]
                    elif a < half:
                        piece = last_behind[a:b]
                    else:
                        piece = last_ahead[a - half : b - half]
                    start = where[0] * (hi - lo) + (a - lo)
                    rows = pl.ds(pl.multiple_of(start, 16), b - a)
                    if where[1] is None:
                        dst[rows, :] = piece
                    else:
                        dst[rows, where[1]] = piece

            for k in range(place.n_t):
                copy(left, (at, lanes(order[k])), k * n_l, (k + 1) * n_l)
            for p in range(panels):
                lo = n_left + p * n_r
                copy(right, (at, pl.ds(p * SIDE, SIDE)), lo, lo + n_r)
            lo = n_left + panels * n_r
            copy(blocks, (at, None), lo, lo + n_b)


def shift(x, axis, n, k):
    return lax.ppermute(x, axis, [(i, (i + k) % n) for i in range(n)])


def chip_shift(x, n_data, k):
    chips = n_data // 2
    perm = [(2 * a + c, 2 * ((a + k) % chips) + c) for a in range(chips) for c in range(2)]
    return lax.ppermute(x, "dp", perm)


def core_swap(x, n_data):
    return lax.ppermute(x, "dp", [(i, i ^ 1) for i in range(n_data)])


def per_device(
    tokens, cotangent, left_factor, right_factor, block_values, block_rows, block_cols, block_counts
):
    n_f = lax.axis_size("fsdp")
    n_t = lax.axis_size("tensor")
    n_d = lax.axis_size("dp")
    place = Place(n_f, n_t, n_d)
    chips = n_d // 2
    maxb = block_values.shape[0]
    tok_rows, features = tokens.shape
    right = right_factor.reshape(right_factor.shape[0], -1)
    rank_size, quarter = right.shape
    q_blocks = quarter // SIDE
    half = tok_rows // 2
    lists = (block_counts, block_rows, block_cols)
    vm, dma = pltpu.VMEM, pltpu.SemaphoreType.DMA

    def bind(kernel, *args):
        return lambda *refs: kernel(place, *args, *refs)

    def over(n, k_shift):
        return [k_shift(k) for k in range(1, n)]

    wide, narrow = shape((tok_rows, SIDE), F32), shape((tok_rows, SIDE), BF16)
    part, whole = shape((half, quarter), BF16), shape((tok_rows, quarter), BF16)
    rank, rank_low, back, *back_out, ahead, behind, step = call(
        bind(front_kernel, q_blocks),
        (wide, narrow, wide, narrow, narrow, narrow, part, part),
        smem=lists,
        hbm=(tokens, left_factor, cotangent, right, block_values),
        scratch=[
            vm((tok_rows, features), BF16),
            vm((features, SIDE), BF16),
            vm((tok_rows, quarter), BF16),
            vm((rank_size, quarter), BF16),
            vm((maxb, SIDE, SIDE), BF16),
            vm((tok_rows, rank_size), F32),
            vm((tok_rows, quarter), F32),
            dma((5,)),
        ],
        mib=52,
    )
    rank_in = over(n_f, lambda k: shift(rank_low, "fsdp", n_f, k))
    back_in = [shift(x, "tensor", n_t, k + 1) for k, x in enumerate(back_out)]

    rank, step = call(total_kernel, (narrow,), vmem=(rank, *rank_in), after=(step,))
    ranks = [rank] + over(n_t, lambda k: shift(rank, "tensor", n_t, k))
    back, back_low, step = call(
        total_kernel, (wide, narrow), vmem=(back, *back_in), after=(step,)
    )
    backs = [back] + over(n_f, lambda k: shift(back_low, "fsdp", n_f, k))

    n_b = maxb // n_d * SIDE
    blocks_mine, blocks_theirs, step = call(
        bind(blocks_kernel),
        (shape((chips, n_b, SIDE), F32), shape((chips, n_b, SIDE), BF16)),
        smem=lists,
        vmem=(tokens, cotangent),
        after=(step,),
        mib=20,
    )

    def hand_on(*refs):
        refs[-1][0] = 0

    ahead, behind, step = pl.pallas_call(
        hand_on,
        out_shape=(part, part, shape((1,), jnp.int32)),
        in_specs=[HBM] * 2 + [VMEM] * 6 + [SMEM],
        out_specs=(HBM, HBM, SMEM),
        input_output_aliases={0: 0, 1: 1},
        compiler_params=pltpu.CompilerParams(vmem_limit_bytes=8 << 20),
    )(ahead, behind, *ranks[1:], *backs[1:], step)
    from_behind = shift(ahead, "fsdp", n_f, 1)
    from_ahead = shift(behind, "fsdp", n_f, -1)

    n_l = features // n_d
    n_r = rank_size // n_d
    n_rest = q_blocks * n_r + n_b
    n_all = n_l + n_rest
    chunk = shape((n_all, SIDE), BF16)
    extra = -(-n_all // 3 // 16) * 16
    mine, *theirs, step = call(
        bind(factors_kernel),
        (shape((chips, n_all, SIDE), F32),)
        + tuple(shape((n_all + n, SIDE), BF16) for n in (extra, extra, n_all - 2 * extra)),
        hbm=(tokens, cotangent),
        vmem=(*ranks, *backs, blocks_mine, blocks_theirs),
        scratch=[
            vm((n_all, SIDE), BF16),
            vm((tok_rows, features), BF16),
            vm((tok_rows, quarter), BF16),
            vm((features, SIDE), F32),
            vm((rank_size, quarter), F32),
            dma((2,)),
        ],
        after=(step,),
        mib=36,
    )
    got = [core_swap(x, n_d) for x in theirs]
    p1, p3, step = call(
        bind(residual_kernel, q_blocks),
        (whole, whole),
        smem=lists,
        vmem=(tokens, block_values),
        scratch=[vm((2, tok_rows, quarter), F32)],
        after=(step,),
        mib=24,
    )
    own, c_near, c_ahead, c_behind, c_far, step = call(
        lambda *refs: cores_kernel(n_l, *refs),
        (
            shape((n_all, SIDE), F32),
            shape((n_rest, SIDE), F32),
            chunk,
            chunk,
            shape((n_l, SIDE), BF16),
        ),
        vmem=(mine, *got),
        after=(step,),
        mib=16,
    )
    c_from_behind = chip_shift(c_ahead, n_d, 1)
    c_from_ahead = chip_shift(c_behind, n_d, -1)
    c_from_far = chip_shift(c_far, n_d, 2)

    ahead, behind, step = call(
        pass_kernel, (whole, whole), vmem=(p1, p3, from_behind, from_ahead), after=(step,), mib=16
    )
    last_behind = shift(ahead, "fsdp", n_f, 1)
    last_ahead = shift(behind, "fsdp", n_f, -1)
    left, c_ahead, c_behind, step = call(
        relay_kernel,
        (shape((n_l, SIDE), BF16),) + (shape((n_rest // 2, SIDE), BF16),) * 2,
        vmem=(own, c_near, c_from_behind, c_from_ahead, c_from_far),
        after=(step,),
    )
    left_near = lax.ppermute(left, "tensor", [(i, i ^ 1) for i in range(n_t)])
    c_last_behind = chip_shift(c_ahead, n_d, 1)
    c_last_ahead = chip_shift(c_behind, n_d, -1)
    left_pair, step = call(
        stack_kernel, (shape((2 * n_l, SIDE), BF16),), vmem=(left, left_near), after=(step,)
    )
    left_far = lax.ppermute(left_pair, "tensor", [(i, n_t - 1 - i) for i in range(n_t)])
    low, step = call(
        bind(low_kernel, q_blocks),
        (shape((tok_rows, quarter), F32),),
        smem=lists,
        vmem=(tokens, block_values, *ranks, right),
        after=(step,),
        mib=20,
    )
    n_msg = n_t * n_l + n_rest
    message, step = call(
        chunk_kernel,
        (shape((n_msg, SIDE), BF16),),
        vmem=(own, c_from_behind, c_from_ahead, c_last_behind, c_last_ahead, left_pair, left_far),
        after=(step,),
    )

    m_behind = chip_shift(message, n_d, 1)
    m_ahead = chip_shift(message, n_d, -1)
    m_last_behind = chip_shift(m_behind[: n_msg // 2], n_d, 1)
    m_last_ahead = chip_shift(m_ahead[n_msg // 2 :], n_d, -1)
    ours = (message, m_behind, m_ahead, jnp.concatenate([m_last_behind, m_last_ahead], axis=0))
    partner = [core_swap(x, n_d) for x in ours]

    out_left, out_right, out_blocks, step = call(
        bind(spread_kernel),
        (
            shape((features, rank_size), BF16),
            shape((rank_size, quarter), BF16),
            shape((maxb * SIDE, SIDE), BF16),
        ),
        vmem=(*ours, *partner),
        mib=14,
    )
    mixed, _ = call(
        finish_kernel, (whole,), vmem=(low, last_behind, last_ahead), mib=12
    )
    return (
        mixed.reshape(tok_rows, 1, quarter),
        out_left,
        out_right.reshape(right_factor.shape),
        out_blocks.reshape(maxb, SIDE, SIDE),
    )


def solution(mesh):
    return jax.shard_map(
        per_device,
        mesh=mesh,
        in_specs=(
            P("dp", "fsdp"),
            P("dp", "tensor"),
            P("fsdp", None),
            P(None, "tensor", "fsdp"),
            P(("fsdp", "tensor"), None, None),
            P(("fsdp", "tensor")),
            P(("fsdp", "tensor")),
            P(),
        ),
        out_specs=(
            P("dp", "tensor", "fsdp"),
            P("fsdp", None),
            P(None, "tensor", "fsdp"),
            P(("fsdp", "tensor"), None, None),
        ),
        check_vma=False,
    )
```

```python
import jax
import jax.numpy as jnp
from jax import lax
from jax.experimental import pallas as pl
from jax.experimental.pallas import tpu as pltpu
from jax.sharding import PartitionSpec as P

F32 = jnp.float32
BF16 = jnp.bfloat16
SIDE = 128
SMEM = pl.BlockSpec(memory_space=pltpu.SMEM)
VMEM = pl.BlockSpec(memory_space=pltpu.VMEM)
HBM = pl.BlockSpec(memory_space=pl.ANY)
ROWS = (((0,), (0,)), ((), ()))
COLS = (((1,), (1,)), ((), ()))


def lanes(block):
    return pl.ds(pl.multiple_of(block * SIDE, SIDE), SIDE)


def span(block, size):
    return pl.ds(pl.multiple_of(block * size, size), size)


def shape(dims, dtype):
    return jax.ShapeDtypeStruct(dims, dtype)


def call(kernel, outs, smem=(), hbm=(), vmem=(), scratch=(), after=(), mib=8, hbm_outs=0):
    n_in, n_out = len(smem) + len(hbm) + len(vmem), len(outs)

    def body(*refs):
        rest = refs[n_in + len(after) :]
        rest[n_out][0] = 0
        kernel(*refs[:n_in], *rest[:n_out], *rest[n_out + 1 :])

    return pl.pallas_call(
        body,
        out_shape=(*outs, shape((1,), jnp.int32)),
        in_specs=[SMEM] * len(smem) + [HBM] * len(hbm) + [VMEM] * len(vmem) + [SMEM] * len(after),
        out_specs=(VMEM,) * (n_out - hbm_outs) + (HBM,) * hbm_outs + (SMEM,),
        scratch_shapes=list(scratch),
        cost_estimate=pl.CostEstimate(flops=0, bytes_accessed=0, transcendentals=0),
        compiler_params=pltpu.CompilerParams(vmem_limit_bytes=mib << 20),
    )(*smem, *hbm, *vmem, *after)


class Place:
    def __init__(self, n_f, n_t, n_d):
        self.n_f, self.n_t, self.n_d, self.chips = n_f, n_t, n_d, n_d // 2

    f = property(lambda self: lax.axis_index("fsdp"))
    t = property(lambda self: lax.axis_index("tensor"))
    chip = property(lambda self: lax.axis_index("dp") // 2)
    core = property(lambda self: lax.rem(lax.axis_index("dp"), 2))

    def live(self, counts):
        return counts[self.f * self.n_t + self.t]


def fetch(*pairs_and_sems):
    copies = [pltpu.make_async_copy(src, dst, sem) for src, dst, sem in pairs_and_sems]
    for copy in copies:
        copy.start()
    return copies


def add_blocks(place, q_blocks, step, counts, rows, cols, tok, vals, acc):
    first = lax.rem(place.f + step, place.n_f) * q_blocks

    def body(s, carry):
        col = cols[s] - first

        @pl.when((col >= 0) & (col < q_blocks))
        def _():
            acc[:, lanes(col)] += jnp.dot(tok[:, lanes(rows[s])], vals[s], preferred_element_type=F32)

        return carry

    lax.fori_loop(0, place.live(counts), body, 0)


def front_kernel(
    place, q_blocks, counts, rows, cols, tok, left, cot, right, vals,
    rank, low, back, s1, s2, s3, ahead, behind,
    tokv, leftv, cotv, rightv, valv, full, acc, stage, sems,
):
    quarter = cotv.shape[1]
    here = pl.ds(pl.multiple_of(place.f * quarter, SIDE), quarter)
    c_tok, c_left, c_val, c_cot, c_right = fetch(
        (tok, tokv, sems.at[0]),
        (left.at[:, lanes(place.t)], leftv, sems.at[1]),
        (vals, valv, sems.at[2]),
        (cot.at[:, here], cotv, sems.at[3]),
        (right, rightv, sems.at[4]),
    )
    acc[...] = jnp.zeros_like(acc)
    c_tok.wait()
    c_left.wait()
    rank[...] = jnp.dot(tokv[...], leftv[...], preferred_element_type=F32)
    low[...] = rank[...].astype(BF16)
    c_val.wait()
    add_blocks(place, q_blocks, place.n_f // 2, counts, rows, cols, tokv, valv, acc)
    half = ahead.shape[0]
    stage[...] = acc[...].astype(BF16)
    c_out = fetch((stage.at[:half], ahead, sems.at[5]), (stage.at[half:], behind, sems.at[6]))
    c_cot.wait()
    c_right.wait()
    full[...] = lax.dot_general(cotv[...], rightv[...], COLS, preferred_element_type=F32)
    back[...] = full[:, lanes(place.t)]
    for k, out in ((1, s1), (2, s2), (3, s3)):
        out[...] = full[:, lanes(lax.rem(place.t + k, place.n_t))].astype(BF16)
    for copy in c_out:
        copy.wait()


def total_kernel(own, g1, g2, g3, *outs):
    total = own[...] + g1[...].astype(F32) + g2[...].astype(F32) + g3[...].astype(F32)
    for out in outs:
        out[...] = total.astype(out.dtype)


def residual_kernel(place, q_blocks, counts, rows, cols, tok, vals, p1, p3, acc):
    acc[...] = jnp.zeros_like(acc)
    n_f, f = place.n_f, place.f

    def body(s, carry):
        q = cols[s] // q_blocks
        step = lax.rem(q - f + n_f, n_f)

        @pl.when(lax.rem(step, 2) == 1)
        def _():
            acc[step // 2, :, lanes(cols[s] - q * q_blocks)] += jnp.dot(
                tok[:, lanes(rows[s])], vals[s], preferred_element_type=F32
            )

        return carry

    lax.fori_loop(0, place.live(counts), body, 0)
    p1[...] = acc[0].astype(BF16)
    p3[...] = acc[1].astype(BF16)


def blocks_kernel(place, counts, rows, cols, tok, cot, mine, theirs):
    live = place.live(counts)
    per = mine.shape[1] // SIDE

    def body(owner, carry):
        grads = []
        for u in range(per):
            s = owner * per + u
            grad = lax.dot_general(
                tok[:, lanes(rows[s])], cot[:, lanes(cols[s])], ROWS, preferred_element_type=F32
            )
            grads.append(jnp.where(s < live, grad, jnp.zeros_like(grad)))
        j = lax.rem(owner // 2 - place.chip + place.chips, place.chips)
        keep = lax.rem(owner, 2) == place.core

        @pl.when(keep)
        def _():
            for u, grad in enumerate(grads):
                mine[j, u * SIDE : (u + 1) * SIDE] = grad

        @pl.when(jnp.logical_not(keep))
        def _():
            for u, grad in enumerate(grads):
                theirs[j, u * SIDE : (u + 1) * SIDE] = grad.astype(BF16)

        return carry

    lax.fori_loop(0, place.n_d, body, 0)


def factors_kernel(
    place, tok, cot, g0, g1, g2, g3, b0, b1, b2, b3, blocks_mine, blocks_theirs,
    mine, out1, out2, out3, theirs0, tokv, cotv, left, right, sems,
):
    quarter = right.shape[1]
    here = pl.ds(pl.multiple_of(place.f * quarter, SIDE), quarter)
    c_tok, c_cot = fetch((tok, tokv, sems.at[0]), (cot.at[:, here], cotv, sems.at[1]))
    n_l = left.shape[0] // place.n_d
    n_r = right.shape[0] // place.n_d
    n_lr = n_l + quarter // SIDE * n_r
    outs = (out1, out2, out3)
    theirs = (theirs0, *outs)
    for j in range(place.chips):
        mine[j, n_lr:] = blocks_mine[j]
        theirs[j][n_lr : n_lr + blocks_theirs.shape[1]] = blocks_theirs[j]
    c_tok.wait()
    back = b0[...] + b1[...].astype(F32) + b2[...].astype(F32) + b3[...].astype(F32)
    left[...] = lax.dot_general(
        back.astype(BF16), tokv[...], ROWS, preferred_element_type=F32
    ).T
    c_cot.wait()
    for k, g in enumerate((g0, g1, g2, g3)):
        at = span(lax.rem(place.t - k + place.n_t, place.n_t), SIDE)
        right[at, :] = lax.dot_general(
            g[...], cotv[...], ROWS, preferred_element_type=F32
        )
    for j in range(place.chips):
        chip = lax.rem(place.chip + j, place.chips)
        for core, out in ((place.core, mine.at[j]), (1 - place.core, theirs[j])):
            at = chip * 2 + core
            out[:n_l] = left[span(at, n_l), :].astype(out.dtype)
            for p in range(quarter // SIDE):
                out[n_l + p * n_r : n_l + (p + 1) * n_r] = right[
                    span(at, n_r), p * SIDE : (p + 1) * SIDE
                ].astype(out.dtype)
    row, n_all = 0, theirs0.shape[0]
    for out in outs:
        extra = out.shape[0] - n_all
        out[n_all:] = theirs0[row : row + extra]
        row += extra


def cores_kernel(n_l, mine, got1, got2, got3, own, near, ahead, behind, far):
    mid = n_l + (own.shape[0] - n_l) // 2
    got = (None, got1, got2, got3)

    def both(k, lo, hi):
        return mine[k, lo:hi] + got[k][lo:hi].astype(F32)

    row = 0
    for g in got[1:]:
        extra = g.shape[0] - own.shape[0]
        own[row : row + extra] = mine[0, row : row + extra] + g[own.shape[0] :].astype(F32)
        row += extra

    end = own.shape[0]
    half = end - mid
    far[...] = both(2, 0, n_l).astype(BF16)
    ahead[:n_l] = both(1, 0, n_l).astype(BF16)
    behind[:n_l] = both(3, 0, n_l).astype(BF16)
    ahead[n_l:mid] = both(2, n_l, mid).astype(BF16)
    behind[n_l:mid] = both(2, mid, end).astype(BF16)
    ahead[mid:] = both(1, mid, end).astype(BF16)
    behind[mid:] = both(3, n_l, mid).astype(BF16)
    near[:half] = both(1, n_l, mid)
    near[half:] = both(3, mid, end)


def relay_kernel(own, near, from_behind, from_ahead, from_far, left, ahead, behind):
    n_l, half = left.shape[0], ahead.shape[0]
    mid = n_l + half
    left[...] = (
        own[:n_l] + from_behind[:n_l].astype(F32) + from_ahead[:n_l].astype(F32)
        + from_far[...].astype(F32)
    ).astype(BF16)
    ahead[...] = (near[:half] + from_behind[n_l:mid].astype(F32)).astype(BF16)
    behind[...] = (near[half:] + from_ahead[n_l:mid].astype(F32)).astype(BF16)


def chunk_kernel(own, from_behind, from_ahead, last_behind, last_ahead, pair, far, out):
    half, n = last_behind.shape[0], pair.shape[0]
    n_l = own.shape[0] - 2 * half
    mid = n_l + half
    out[:n] = pair[...]
    out[n : 2 * n] = far[...]
    out[2 * n : 2 * n + half] = (
        own[n_l:mid] + from_ahead[mid:].astype(F32) + last_behind[...].astype(F32)
    ).astype(BF16)
    out[2 * n + half :] = (
        own[mid:] + from_behind[mid:].astype(F32) + last_ahead[...].astype(F32)
    ).astype(BF16)


def stack_kernel(*refs):
    parts, out = refs[:-1], refs[-1]
    row = 0
    for part in parts:
        out[row : row + part.shape[0]] = part[...]
        row += part.shape[0]


def pass_kernel(p1, p3, from_behind, from_ahead, ahead, behind):
    half = from_behind.shape[0]
    ahead[:half] = (p1[:half].astype(F32) + from_behind[...].astype(F32)).astype(BF16)
    ahead[half:] = p1[half:]
    behind[:half] = p3[:half]
    behind[half:] = (p3[half:].astype(F32) + from_ahead[...].astype(F32)).astype(BF16)


def pair_kernel(own, behind, ahead, first, rest):
    n = own.shape[0]
    first[:n] = own[...]
    first[n : 2 * n] = behind[...]
    cut = first.shape[0] - 2 * n
    first[2 * n :] = ahead[:cut]
    rest[...] = ahead[cut:]


def low_kernel(place, q_blocks, counts, rows, cols, tok, vals, g0, g1, g2, g3, right, out):
    acc = jnp.zeros(out.shape, F32)
    for k, g in enumerate((g0, g1, g2, g3)):
        at = span(lax.rem(place.t - k + place.n_t, place.n_t), SIDE)
        acc += jnp.dot(g[...], right[at, :], preferred_element_type=F32)
    out[...] = acc
    add_blocks(place, q_blocks, 0, counts, rows, cols, tok, vals, out)


def finish_kernel(low, from_behind, from_ahead, out):
    out[...] = (low[...] + from_behind[...].astype(F32) + from_ahead[...].astype(F32)).astype(BF16)


def spread_kernel(place, *refs):
    refs, (left, right, blocks) = refs[:-3], refs[-3:]
    n_l = left.shape[0] // place.n_d
    n_r = right.shape[0] // place.n_d
    n_b = blocks.shape[0] // place.n_d
    panels = right.shape[1] // SIDE
    n_left = place.n_t * n_l
    t = place.t
    near_t = t + 1 - 2 * lax.rem(t, 2)
    far_t = place.n_t - 1 - t
    order = (t, near_t, far_t, place.n_t - 1 - near_t)
    n = len(refs) // 2
    for core, mine in ((place.core, refs[:n]), (1 - place.core, refs[n:])):
        first, rest, last = mine
        half = last.shape[0] // 2
        behind, ahead = first.at[2 * half : 4 * half], first.at[4 * half :]
        cut = ahead.shape[0]
        for j, segments in (
            (0, ((0, first),)),
            (-1, ((0, behind),)),
            (1, ((0, ahead), (cut, rest))),
            (2, ((0, last),)),
        ):
            at = lax.rem(place.chip + j + place.chips, place.chips) * 2 + core

            def copy(dst, where, lo, hi):
                base, src = [s for s in segments if s[0] <= lo][-1]
                rows = span(where[0], hi - lo)
                if where[1] is None:
                    dst[rows, :] = src[lo - base : hi - base]
                else:
                    dst[rows, where[1]] = src[lo - base : hi - base]

            for k in range(place.n_t):
                copy(left, (at, lanes(order[k])), k * n_l, (k + 1) * n_l)
            for p in range(panels):
                lo = n_left + p * n_r
                copy(right, (at, pl.ds(p * SIDE, SIDE)), lo, lo + n_r)
            lo = n_left + panels * n_r
            copy(blocks, (at, None), lo, lo + n_b)


def shift(x, axis, n, k):
    return lax.ppermute(x, axis, [(i, (i + k) % n) for i in range(n)])


def chip_shift(x, n_data, k):
    chips = n_data // 2
    perm = [(2 * a + c, 2 * ((a + k) % chips) + c) for a in range(chips) for c in range(2)]
    return lax.ppermute(x, "dp", perm)


def core_swap(x, n_data):
    return lax.ppermute(x, "dp", [(i, i ^ 1) for i in range(n_data)])


def per_device(
    tokens, cotangent, left_factor, right_factor, block_values, block_rows, block_cols, block_counts
):
    n_f = lax.axis_size("fsdp")
    n_t = lax.axis_size("tensor")
    n_d = lax.axis_size("dp")
    place = Place(n_f, n_t, n_d)
    chips = n_d // 2
    maxb = block_values.shape[0]
    tok_rows, features = tokens.shape
    right = right_factor.reshape(right_factor.shape[0], -1)
    rank_size, quarter = right.shape
    q_blocks = quarter // SIDE
    half = tok_rows // 2
    lists = (block_counts, block_rows, block_cols)
    vm, dma = pltpu.VMEM, pltpu.SemaphoreType.DMA

    def bind(kernel, *args):
        return lambda *refs: kernel(place, *args, *refs)

    def over(n, k_shift):
        return [k_shift(k) for k in range(1, n)]

    wide, narrow = shape((tok_rows, SIDE), F32), shape((tok_rows, SIDE), BF16)
    part, whole = shape((half, quarter), BF16), shape((tok_rows, quarter), BF16)
    rank, rank_low, back, *back_out, ahead, behind, step = call(
        bind(front_kernel, q_blocks),
        (wide, narrow, wide, narrow, narrow, narrow, part, part),
        smem=lists,
        hbm=(tokens, left_factor, cotangent, right, block_values),
        scratch=[
            vm((tok_rows, features), BF16),
            vm((features, SIDE), BF16),
            vm((tok_rows, quarter), BF16),
            vm((rank_size, quarter), BF16),
            vm((maxb, SIDE, SIDE), BF16),
            vm((tok_rows, rank_size), F32),
            vm((tok_rows, quarter), F32),
            vm((tok_rows, quarter), BF16),
            dma((7,)),
        ],
        mib=52,
        hbm_outs=2,
    )
    rank_in = over(n_f, lambda k: shift(rank_low, "fsdp", n_f, k))
    back_in = [shift(x, "tensor", n_t, k + 1) for k, x in enumerate(back_out)]

    rank, step = call(total_kernel, (narrow,), vmem=(rank, *rank_in), after=(step,))
    ranks = [rank] + over(n_t, lambda k: shift(rank, "tensor", n_t, k))
    back, back_low, step = call(
        total_kernel, (wide, narrow), vmem=(back, *back_in), after=(step,)
    )
    backs = [back] + over(n_f, lambda k: shift(back_low, "fsdp", n_f, k))

    n_b = maxb // n_d * SIDE
    blocks_mine, blocks_theirs, step = call(
        bind(blocks_kernel),
        (shape((chips, n_b, SIDE), F32), shape((chips, n_b, SIDE), BF16)),
        smem=lists,
        vmem=(tokens, cotangent),
        after=(step,),
        mib=20,
    )

    def hand_on(*refs):
        refs[-1][0] = 0

    ahead, behind, step = pl.pallas_call(
        hand_on,
        out_shape=(part, part, shape((1,), jnp.int32)),
        in_specs=[HBM] * 2 + [VMEM] * 6 + [SMEM],
        out_specs=(HBM, HBM, SMEM),
        input_output_aliases={0: 0, 1: 1},
        compiler_params=pltpu.CompilerParams(vmem_limit_bytes=8 << 20),
    )(ahead, behind, *ranks[1:], *backs[1:], step)
    from_behind = shift(ahead, "fsdp", n_f, 1)
    from_ahead = shift(behind, "fsdp", n_f, -1)

    n_l = features // n_d
    n_r = rank_size // n_d
    n_rest = q_blocks * n_r + n_b
    n_all = n_l + n_rest
    chunk = shape((n_all, SIDE), BF16)
    extra = -(-n_all // 3 // 16) * 16
    mine, *theirs, step = call(
        bind(factors_kernel),
        (shape((chips, n_all, SIDE), F32),)
        + tuple(shape((n_all + n, SIDE), BF16) for n in (extra, extra, n_all - 2 * extra)),
        hbm=(tokens, cotangent),
        vmem=(*ranks, *backs, blocks_mine, blocks_theirs),
        scratch=[
            vm((n_all, SIDE), BF16),
            vm((tok_rows, features), BF16),
            vm((tok_rows, quarter), BF16),
            vm((features, SIDE), F32),
            vm((rank_size, quarter), F32),
            dma((2,)),
        ],
        after=(step,),
        mib=36,
    )
    got = [core_swap(x, n_d) for x in theirs]
    p1, p3, step = call(
        bind(residual_kernel, q_blocks),
        (whole, whole),
        smem=lists,
        vmem=(tokens, block_values),
        scratch=[vm((2, tok_rows, quarter), F32)],
        after=(step,),
        mib=24,
    )
    own, c_near, c_ahead, c_behind, c_far, step = call(
        lambda *refs: cores_kernel(n_l, *refs),
        (
            shape((n_all, SIDE), F32),
            shape((n_rest, SIDE), F32),
            chunk,
            chunk,
            shape((n_l, SIDE), BF16),
        ),
        vmem=(mine, *got),
        after=(step,),
        mib=16,
    )
    c_from_behind = chip_shift(c_ahead, n_d, 1)
    c_from_ahead = chip_shift(c_behind, n_d, -1)
    c_from_far = chip_shift(c_far, n_d, 2)

    ahead, behind, step = call(
        pass_kernel, (whole, whole), vmem=(p1, p3, from_behind, from_ahead), after=(step,), mib=16
    )
    last_behind = shift(ahead, "fsdp", n_f, 1)
    last_ahead = shift(behind, "fsdp", n_f, -1)
    left, c_ahead, c_behind, step = call(
        relay_kernel,
        (shape((n_l, SIDE), BF16),) + (shape((n_rest // 2, SIDE), BF16),) * 2,
        vmem=(own, c_near, c_from_behind, c_from_ahead, c_from_far),
        after=(step,),
    )
    left_near = lax.ppermute(left, "tensor", [(i, i ^ 1) for i in range(n_t)])
    c_last_behind = chip_shift(c_ahead, n_d, 1)
    c_last_ahead = chip_shift(c_behind, n_d, -1)
    left_pair, step = call(
        stack_kernel, (shape((2 * n_l, SIDE), BF16),), vmem=(left, left_near), after=(step,)
    )
    left_far = lax.ppermute(left_pair, "tensor", [(i, n_t - 1 - i) for i in range(n_t)])
    n_msg = n_t * n_l + n_rest
    message, step = call(
        chunk_kernel,
        (shape((n_msg, SIDE), BF16),),
        vmem=(own, c_from_behind, c_from_ahead, c_last_behind, c_last_ahead, left_pair, left_far),
        after=(step,),
    )

    m_behind = chip_shift(message, n_d, 1)
    m_ahead = chip_shift(message, n_d, -1)
    m_last_behind = chip_shift(m_behind[: n_msg // 2], n_d, 1)
    m_last_ahead = chip_shift(m_ahead[n_msg // 2 :], n_d, -1)
    low, step = call(
        bind(low_kernel, q_blocks),
        (shape((tok_rows, quarter), F32),),
        smem=lists,
        vmem=(tokens, block_values, *ranks, right),
        after=(step,),
        mib=20,
    )
    m_last, step = call(
        stack_kernel,
        (shape((n_msg, SIDE), BF16),),
        vmem=(m_last_behind, m_last_ahead),
        after=(step,),
    )
    first, rest, _ = call(
        pair_kernel,
        (shape((2 * n_msg + 3 * n_l, SIDE), BF16), shape((n_msg - 3 * n_l, SIDE), BF16)),
        vmem=(message, m_behind, m_ahead),
    )
    ours = (first, rest, m_last)
    partner = [core_swap(x, n_d) for x in ours]

    out_left, out_right, out_blocks, step = call(
        bind(spread_kernel),
        (
            shape((features, rank_size), BF16),
            shape((rank_size, quarter), BF16),
            shape((maxb * SIDE, SIDE), BF16),
        ),
        vmem=(*ours, *partner),
        mib=14,
    )
    mixed, _ = call(
        finish_kernel, (whole,), vmem=(low, last_behind, last_ahead), mib=12
    )
    return (
        mixed.reshape(tok_rows, 1, quarter),
        out_left,
        out_right.reshape(right_factor.shape),
        out_blocks.reshape(maxb, SIDE, SIDE),
    )


def solution(mesh):
    return jax.shard_map(
        per_device,
        mesh=mesh,
        in_specs=(
            P("dp", "fsdp"),
            P("dp", "tensor"),
            P("fsdp", None),
            P(None, "tensor", "fsdp"),
            P(("fsdp", "tensor"), None, None),
            P(("fsdp", "tensor")),
            P(("fsdp", "tensor")),
            P(),
        ),
        out_specs=(
            P("dp", "tensor", "fsdp"),
            P("fsdp", None),
            P(None, "tensor", "fsdp"),
            P(("fsdp", "tensor"), None, None),
        ),
        check_vma=False,
    )
```

```python
import jax
import jax.numpy as jnp
from jax import lax
from jax.experimental import pallas as pl
from jax.experimental.pallas import tpu as pltpu
from jax.sharding import PartitionSpec as P

F32 = jnp.float32
BF16 = jnp.bfloat16
SIDE = 128
SMEM = pl.BlockSpec(memory_space=pltpu.SMEM)
VMEM = pl.BlockSpec(memory_space=pltpu.VMEM)
HBM = pl.BlockSpec(memory_space=pl.ANY)
ROWS = (((0,), (0,)), ((), ()))
COLS = (((1,), (1,)), ((), ()))


def lanes(block):
    return pl.ds(pl.multiple_of(block * SIDE, SIDE), SIDE)


def span(block, size):
    return pl.ds(pl.multiple_of(block * size, size), size)


def shape(dims, dtype):
    return jax.ShapeDtypeStruct(dims, dtype)


def call(kernel, outs, smem=(), hbm=(), vmem=(), scratch=(), after=(), mib=8, hbm_outs=0):
    n_in, n_out = len(smem) + len(hbm) + len(vmem), len(outs)

    def body(*refs):
        rest = refs[n_in + len(after) :]
        rest[n_out][0] = 0
        kernel(*refs[:n_in], *rest[:n_out], *rest[n_out + 1 :])

    return pl.pallas_call(
        body,
        out_shape=(*outs, shape((1,), jnp.int32)),
        in_specs=[SMEM] * len(smem) + [HBM] * len(hbm) + [VMEM] * len(vmem) + [SMEM] * len(after),
        out_specs=(VMEM,) * (n_out - hbm_outs) + (HBM,) * hbm_outs + (SMEM,),
        scratch_shapes=list(scratch),
        cost_estimate=pl.CostEstimate(flops=0, bytes_accessed=0, transcendentals=0),
        compiler_params=pltpu.CompilerParams(vmem_limit_bytes=mib << 20),
    )(*smem, *hbm, *vmem, *after)


class Place:
    def __init__(self, n_f, n_t, n_d):
        self.n_f, self.n_t, self.n_d, self.chips = n_f, n_t, n_d, n_d // 2

    f = property(lambda self: lax.axis_index("fsdp"))
    t = property(lambda self: lax.axis_index("tensor"))
    chip = property(lambda self: lax.axis_index("dp") // 2)
    core = property(lambda self: lax.rem(lax.axis_index("dp"), 2))

    def live(self, counts):
        return counts[self.f * self.n_t + self.t]


def fetch(*pairs_and_sems):
    copies = [pltpu.make_async_copy(src, dst, sem) for src, dst, sem in pairs_and_sems]
    for copy in copies:
        copy.start()
    return copies


def add_blocks(place, q_blocks, step, counts, rows, cols, tok, vals, acc):
    first = lax.rem(place.f + step, place.n_f) * q_blocks

    def body(s, carry):
        col = cols[s] - first

        @pl.when((col >= 0) & (col < q_blocks))
        def _():
            acc[:, lanes(col)] += jnp.dot(tok[:, lanes(rows[s])], vals[s], preferred_element_type=F32)

        return carry

    lax.fori_loop(0, place.live(counts), body, 0)


def front_kernel(
    place, q_blocks, counts, rows, cols, tok, left, cot, right, vals,
    rank, low, back, s1, s2, s3, ahead, behind,
    tokv, leftv, cotv, rightv, valv, full, acc, stage, sems,
):
    quarter = cotv.shape[1]
    here = pl.ds(pl.multiple_of(place.f * quarter, SIDE), quarter)
    c_tok, c_left, c_val, c_cot, c_right = fetch(
        (tok, tokv, sems.at[0]),
        (left.at[:, lanes(place.t)], leftv, sems.at[1]),
        (vals, valv, sems.at[2]),
        (cot.at[:, here], cotv, sems.at[3]),
        (right, rightv, sems.at[4]),
    )
    acc[...] = jnp.zeros_like(acc)
    c_tok.wait()
    c_left.wait()
    rank[...] = jnp.dot(tokv[...], leftv[...], preferred_element_type=F32)
    low[...] = rank[...].astype(BF16)
    c_val.wait()
    add_blocks(place, q_blocks, place.n_f // 2, counts, rows, cols, tokv, valv, acc)
    half = ahead.shape[0]
    stage[...] = acc[...].astype(BF16)
    c_out = fetch((stage.at[:half], ahead, sems.at[5]), (stage.at[half:], behind, sems.at[6]))
    c_cot.wait()
    c_right.wait()
    full[...] = lax.dot_general(cotv[...], rightv[...], COLS, preferred_element_type=F32)
    back[...] = full[:, lanes(place.t)]
    for k, out in ((1, s1), (2, s2), (3, s3)):
        out[...] = full[:, lanes(lax.rem(place.t + k, place.n_t))].astype(BF16)
    for copy in c_out:
        copy.wait()


def residual_kernel(place, q_blocks, counts, rows, cols, tok, vals, p1, p3, acc):
    acc[...] = jnp.zeros_like(acc)
    n_f, f = place.n_f, place.f

    def body(s, carry):
        q = cols[s] // q_blocks
        step = lax.rem(q - f + n_f, n_f)

        @pl.when(lax.rem(step, 2) == 1)
        def _():
            acc[step // 2, :, lanes(cols[s] - q * q_blocks)] += jnp.dot(
                tok[:, lanes(rows[s])], vals[s], preferred_element_type=F32
            )

        return carry

    lax.fori_loop(0, place.live(counts), body, 0)
    p1[...] = acc[0].astype(BF16)
    p3[...] = acc[1].astype(BF16)


def blocks_kernel(place, counts, rows, cols, tok, cot, _, mine, theirs):
    live = place.live(counts)
    per = mine.shape[1] // SIDE

    def body(owner, carry):
        grads = []
        for u in range(per):
            s = owner * per + u
            grad = lax.dot_general(
                tok[:, lanes(rows[s])], cot[:, lanes(cols[s])], ROWS, preferred_element_type=F32
            )
            grads.append(jnp.where(s < live, grad, jnp.zeros_like(grad)))
        j = lax.rem(owner // 2 - place.chip + place.chips, place.chips)
        keep = lax.rem(owner, 2) == place.core

        @pl.when(keep)
        def _():
            for u, grad in enumerate(grads):
                mine[j, u * SIDE : (u + 1) * SIDE] = grad

        @pl.when(jnp.logical_not(keep))
        def _():
            for u, grad in enumerate(grads):
                theirs[j, u * SIDE : (u + 1) * SIDE] = grad.astype(BF16)

        return carry

    lax.fori_loop(0, place.n_d, body, 0)


def factors_kernel(
    place, tok, cot, g0, g1, g2, g3, b0, b1, b2, b3, blocks_mine, blocks_theirs,
    mine, out1, out2, out3, theirs0, tokv, cotv, left, right, sems,
):
    quarter = right.shape[1]
    here = pl.ds(pl.multiple_of(place.f * quarter, SIDE), quarter)
    c_tok, c_cot = fetch((tok, tokv, sems.at[0]), (cot.at[:, here], cotv, sems.at[1]))
    n_l = left.shape[0] // place.n_d
    n_r = right.shape[0] // place.n_d
    n_lr = n_l + quarter // SIDE * n_r
    outs = (out1, out2, out3)
    theirs = (theirs0, *outs)
    for j in range(place.chips):
        mine[j, n_lr:] = blocks_mine[j]
        theirs[j][n_lr : n_lr + blocks_theirs.shape[1]] = blocks_theirs[j]
    c_tok.wait()
    back = b0[...] + b1[...].astype(F32) + b2[...].astype(F32) + b3[...].astype(F32)
    left[...] = lax.dot_general(
        back.astype(BF16), tokv[...], ROWS, preferred_element_type=F32
    ).T
    c_cot.wait()
    for k, g in enumerate((g0, g1, g2, g3)):
        at = span(lax.rem(place.t - k + place.n_t, place.n_t), SIDE)
        right[at, :] = lax.dot_general(
            g[...], cotv[...], ROWS, preferred_element_type=F32
        )
    for j in range(place.chips):
        chip = lax.rem(place.chip + j, place.chips)
        for core, out in ((place.core, mine.at[j]), (1 - place.core, theirs[j])):
            at = chip * 2 + core
            out[:n_l] = left[span(at, n_l), :].astype(out.dtype)
            for p in range(quarter // SIDE):
                out[n_l + p * n_r : n_l + (p + 1) * n_r] = right[
                    span(at, n_r), p * SIDE : (p + 1) * SIDE
                ].astype(out.dtype)
    row, n_all = 0, theirs0.shape[0]
    for out in outs:
        extra = out.shape[0] - n_all
        out[n_all:] = theirs0[row : row + extra]
        row += extra


def cores_kernel(n_l, mine, got1, got2, got3, own, near, ahead, behind, far):
    mid = n_l + (own.shape[0] - n_l) // 2
    got = (None, got1, got2, got3)

    def both(k, lo, hi):
        return mine[k, lo:hi] + got[k][lo:hi].astype(F32)

    row = 0
    for g in got[1:]:
        extra = g.shape[0] - own.shape[0]
        own[row : row + extra] = mine[0, row : row + extra] + g[own.shape[0] :].astype(F32)
        row += extra

    end = own.shape[0]
    half = end - mid
    far[...] = both(2, 0, n_l).astype(BF16)
    ahead[:n_l] = both(1, 0, n_l).astype(BF16)
    behind[:n_l] = both(3, 0, n_l).astype(BF16)
    ahead[n_l:mid] = both(2, n_l, mid).astype(BF16)
    behind[n_l:mid] = both(2, mid, end).astype(BF16)
    ahead[mid:] = both(1, mid, end).astype(BF16)
    behind[mid:] = both(3, n_l, mid).astype(BF16)
    near[:half] = both(1, n_l, mid)
    near[half:] = both(3, mid, end)


def relay_kernel(own, near, from_behind, from_ahead, from_far, left, ahead, behind):
    n_l, half = left.shape[0], ahead.shape[0]
    mid = n_l + half
    left[...] = (
        own[:n_l] + from_behind[:n_l].astype(F32) + from_ahead[:n_l].astype(F32)
        + from_far[...].astype(F32)
    ).astype(BF16)
    ahead[...] = (near[:half] + from_behind[n_l:mid].astype(F32)).astype(BF16)
    behind[...] = (near[half:] + from_ahead[n_l:mid].astype(F32)).astype(BF16)


def chunk_kernel(own, from_behind, from_ahead, last_behind, last_ahead, pair, far, out):
    half, n = last_behind.shape[0], pair.shape[0]
    n_l = own.shape[0] - 2 * half
    mid = n_l + half
    out[:n] = pair[...]
    out[n : 2 * n] = far[...]
    out[2 * n : 2 * n + half] = (
        own[n_l:mid] + from_ahead[mid:].astype(F32) + last_behind[...].astype(F32)
    ).astype(BF16)
    out[2 * n + half :] = (
        own[mid:] + from_behind[mid:].astype(F32) + last_ahead[...].astype(F32)
    ).astype(BF16)


def stack_kernel(*refs):
    parts, out = refs[:-1], refs[-1]
    row = 0
    for part in parts:
        out[row : row + part.shape[0]] = part[...]
        row += part.shape[0]


def pass_kernel(p1, p3, from_behind, from_ahead, ahead, behind):
    half = from_behind.shape[0]
    ahead[:half] = (p1[:half].astype(F32) + from_behind[...].astype(F32)).astype(BF16)
    ahead[half:] = p1[half:]
    behind[:half] = p3[:half]
    behind[half:] = (p3[half:].astype(F32) + from_ahead[...].astype(F32)).astype(BF16)


def pair_kernel(own, behind, ahead, first, rest):
    n = own.shape[0]
    first[:n] = own[...]
    first[n : 2 * n] = behind[...]
    cut = first.shape[0] - 2 * n
    first[2 * n :] = ahead[:cut]
    rest[...] = ahead[cut:]


def low_kernel(place, q_blocks, counts, rows, cols, tok, vals, g0, g1, g2, g3, right, out):
    acc = jnp.zeros(out.shape, F32)
    for k, g in enumerate((g0, g1, g2, g3)):
        at = span(lax.rem(place.t - k + place.n_t, place.n_t), SIDE)
        acc += jnp.dot(g[...], right[at, :], preferred_element_type=F32)
    out[...] = acc
    add_blocks(place, q_blocks, 0, counts, rows, cols, tok, vals, out)


def last_kernel(place, low, from_behind, from_ahead, *refs):
    (mixed_out, left_out, right_out, blocks), (mixed, left, right, sems) = refs[-8:-4], refs[-4:]
    refs = refs[:-8]
    n_l = left.shape[0] // place.n_d
    n_r = right.shape[0] // place.n_d
    n_b = blocks.shape[0] // place.n_d
    panels = right.shape[1] // SIDE
    n_left = place.n_t * n_l
    t = place.t
    near_t = t + 1 - 2 * lax.rem(t, 2)
    far_t = place.n_t - 1 - t
    order = (t, near_t, far_t, place.n_t - 1 - near_t)
    copies = []

    def send(pair):
        copies.extend(fetch((*pair, sems.at[len(copies)])))

    chunks = []
    n = len(refs) // 2
    for core, (first, rest, last) in (
        (place.core, refs[:n]),
        (1 - place.core, refs[n:]),
    ):
        half = last.shape[0] // 2
        behind, ahead = first.at[2 * half : 4 * half], first.at[4 * half :]
        for j, segments in (
            (0, ((0, first),)),
            (-1, ((0, behind),)),
            (1, ((0, ahead), (ahead.shape[0], rest))),
            (2, ((0, last),)),
        ):
            at = lax.rem(place.chip + j + place.chips, place.chips) * 2 + core
            chunks.append((at, segments))

    def piece(segments, lo, hi):
        base, src = [s for s in segments if s[0] <= lo][-1]
        return src.at[lo - base : hi - base]

    base = n_left + panels * n_r
    for at, segments in chunks:
        send((piece(segments, base, base + n_b), blocks.at[span(at, n_b)]))
    for at, segments in chunks:
        for k in range(place.n_t):
            left[span(at, n_l), lanes(order[k])] = piece(segments, k * n_l, (k + 1) * n_l)[...]
    send((left, left_out))
    for at, segments in chunks:
        for p in range(panels):
            lo = n_left + p * n_r
            right[span(at, n_r), p * SIDE : (p + 1) * SIDE] = piece(segments, lo, lo + n_r)[...]
    send((right, right_out))
    size = mixed.shape[0] // 4
    for i in range(4):
        rows = pl.ds(i * size, size)
        total = low[rows, :] + from_behind[rows, :].astype(F32) + from_ahead[rows, :].astype(F32)
        mixed[rows, :] = total.astype(BF16)
        send((mixed.at[rows], mixed_out.at[rows]))
    for copy in copies:
        copy.wait()


def shift(x, axis, n, k):
    return lax.ppermute(x, axis, [(i, (i + k) % n) for i in range(n)])


def chip_shift(x, n_data, k):
    chips = n_data // 2
    perm = [(2 * a + c, 2 * ((a + k) % chips) + c) for a in range(chips) for c in range(2)]
    return lax.ppermute(x, "dp", perm)


def core_swap(x, n_data):
    return lax.ppermute(x, "dp", [(i, i ^ 1) for i in range(n_data)])


def per_device(
    tokens, cotangent, left_factor, right_factor, block_values, block_rows, block_cols, block_counts
):
    n_f = lax.axis_size("fsdp")
    n_t = lax.axis_size("tensor")
    n_d = lax.axis_size("dp")
    place = Place(n_f, n_t, n_d)
    chips = n_d // 2
    maxb = block_values.shape[0]
    tok_rows, features = tokens.shape
    right = right_factor.reshape(right_factor.shape[0], -1)
    rank_size, quarter = right.shape
    q_blocks = quarter // SIDE
    half = tok_rows // 2
    lists = (block_counts, block_rows, block_cols)
    vm, dma = pltpu.VMEM, pltpu.SemaphoreType.DMA

    def bind(kernel, *args):
        return lambda *refs: kernel(place, *args, *refs)

    def over(n, k_shift):
        return [k_shift(k) for k in range(1, n)]

    wide, narrow = shape((tok_rows, SIDE), F32), shape((tok_rows, SIDE), BF16)
    part, whole = shape((half, quarter), BF16), shape((tok_rows, quarter), BF16)
    rank, rank_low, back, *back_out, ahead, behind, step = call(
        bind(front_kernel, q_blocks),
        (wide, narrow, wide, narrow, narrow, narrow, part, part),
        smem=lists,
        hbm=(tokens, left_factor, cotangent, right, block_values),
        scratch=[
            vm((tok_rows, features), BF16),
            vm((features, SIDE), BF16),
            vm((tok_rows, quarter), BF16),
            vm((rank_size, quarter), BF16),
            vm((maxb, SIDE, SIDE), BF16),
            vm((tok_rows, rank_size), F32),
            vm((tok_rows, quarter), F32),
            vm((tok_rows, quarter), BF16),
            dma((7,)),
        ],
        mib=52,
        hbm_outs=2,
    )
    rank_in = over(n_f, lambda k: shift(rank_low, "fsdp", n_f, k))
    back_in = [shift(x, "tensor", n_t, k + 1) for k, x in enumerate(back_out)]

    for x in rank_in:
        rank = rank + x.astype(F32)
    rank = rank.astype(BF16)
    ranks = [rank] + over(n_t, lambda k: shift(rank, "tensor", n_t, k))
    for x in back_in:
        back = back + x.astype(F32)
    back_low = back.astype(BF16)
    backs = [back] + over(n_f, lambda k: shift(back_low, "fsdp", n_f, k))

    n_b = maxb // n_d * SIDE
    blocks_mine, blocks_theirs, step = call(
        bind(blocks_kernel),
        (shape((chips, n_b, SIDE), F32), shape((chips, n_b, SIDE), BF16)),
        smem=lists,
        vmem=(tokens, cotangent, back_low),
        after=(step,),
        mib=20,
    )

    def hand_on(*refs):
        refs[-1][0] = 0

    ahead, behind, step = pl.pallas_call(
        hand_on,
        out_shape=(part, part, shape((1,), jnp.int32)),
        in_specs=[HBM] * 2 + [VMEM] * 6 + [SMEM],
        out_specs=(HBM, HBM, SMEM),
        input_output_aliases={0: 0, 1: 1},
        compiler_params=pltpu.CompilerParams(vmem_limit_bytes=8 << 20),
    )(ahead, behind, *ranks[1:], *backs[1:], step)
    from_behind = shift(ahead, "fsdp", n_f, 1)
    from_ahead = shift(behind, "fsdp", n_f, -1)

    n_l = features // n_d
    n_r = rank_size // n_d
    n_rest = q_blocks * n_r + n_b
    n_all = n_l + n_rest
    chunk = shape((n_all, SIDE), BF16)
    extra = -(-n_all // 3 // 16) * 16
    mine, *theirs, step = call(
        bind(factors_kernel),
        (shape((chips, n_all, SIDE), F32),)
        + tuple(shape((n_all + n, SIDE), BF16) for n in (extra, extra, n_all - 2 * extra)),
        hbm=(tokens, cotangent),
        vmem=(*ranks, *backs, blocks_mine, blocks_theirs),
        scratch=[
            vm((n_all, SIDE), BF16),
            vm((tok_rows, features), BF16),
            vm((tok_rows, quarter), BF16),
            vm((features, SIDE), F32),
            vm((rank_size, quarter), F32),
            dma((2,)),
        ],
        after=(step,),
        mib=36,
    )
    got = [core_swap(x, n_d) for x in theirs]
    p1, p3, step = call(
        bind(residual_kernel, q_blocks),
        (whole, whole),
        smem=lists,
        vmem=(tokens, block_values),
        scratch=[vm((2, tok_rows, quarter), F32)],
        after=(step,),
        mib=24,
    )
    own, c_near, c_ahead, c_behind, c_far, step = call(
        lambda *refs: cores_kernel(n_l, *refs),
        (
            shape((n_all, SIDE), F32),
            shape((n_rest, SIDE), F32),
            chunk,
            chunk,
            shape((n_l, SIDE), BF16),
        ),
        vmem=(mine, *got),
        after=(step,),
        mib=16,
    )
    c_from_behind = chip_shift(c_ahead, n_d, 1)
    c_from_ahead = chip_shift(c_behind, n_d, -1)
    c_from_far = chip_shift(c_far, n_d, 2)

    ahead, behind, step = call(
        pass_kernel, (whole, whole), vmem=(p1, p3, from_behind, from_ahead), after=(step,), mib=16
    )
    last_behind = shift(ahead, "fsdp", n_f, 1)
    last_ahead = shift(behind, "fsdp", n_f, -1)
    left, c_ahead, c_behind, step = call(
        relay_kernel,
        (shape((n_l, SIDE), BF16),) + (shape((n_rest // 2, SIDE), BF16),) * 2,
        vmem=(own, c_near, c_from_behind, c_from_ahead, c_from_far),
        after=(step,),
    )
    left_near = lax.ppermute(left, "tensor", [(i, i ^ 1) for i in range(n_t)])
    c_last_behind = chip_shift(c_ahead, n_d, 1)
    c_last_ahead = chip_shift(c_behind, n_d, -1)
    left_pair, step = call(
        stack_kernel, (shape((2 * n_l, SIDE), BF16),), vmem=(left, left_near), after=(step,)
    )
    left_far = lax.ppermute(left_pair, "tensor", [(i, n_t - 1 - i) for i in range(n_t)])
    n_msg = n_t * n_l + n_rest
    message, step = call(
        chunk_kernel,
        (shape((n_msg, SIDE), BF16),),
        vmem=(own, c_from_behind, c_from_ahead, c_last_behind, c_last_ahead, left_pair, left_far),
        after=(step,),
    )

    m_behind = chip_shift(message, n_d, 1)
    m_ahead = chip_shift(message, n_d, -1)
    m_last_behind = chip_shift(m_behind[: n_msg // 2], n_d, 1)
    m_last_ahead = chip_shift(m_ahead[n_msg // 2 :], n_d, -1)
    low, step = call(
        bind(low_kernel, q_blocks),
        (shape((tok_rows, quarter), F32),),
        smem=lists,
        vmem=(tokens, block_values, *ranks, right),
        after=(step,),
        mib=20,
    )
    m_last, step = call(
        stack_kernel,
        (shape((n_msg, SIDE), BF16),),
        vmem=(m_last_behind, m_last_ahead),
        after=(step,),
    )
    first, rest, _ = call(
        pair_kernel,
        (shape((2 * n_msg + 3 * n_l, SIDE), BF16), shape((n_msg - 3 * n_l, SIDE), BF16)),
        vmem=(message, m_behind, m_ahead),
    )
    ours = (first, rest, m_last)
    partner = [core_swap(x, n_d) for x in ours]

    mixed, out_left, out_right, out_blocks, _ = call(
        bind(last_kernel),
        (
            whole,
            shape((features, rank_size), BF16),
            shape((rank_size, quarter), BF16),
            shape((maxb * SIDE, SIDE), BF16),
        ),
        vmem=(low, last_behind, last_ahead, *ours, *partner),
        scratch=[
            vm((tok_rows, quarter), BF16),
            vm((features, rank_size), BF16),
            vm((rank_size, quarter), BF16),
            dma((n_d + 6,)),
        ],
        mib=32,
        hbm_outs=4,
    )
    return (
        mixed.reshape(tok_rows, 1, quarter),
        out_left,
        out_right.reshape(right_factor.shape),
        out_blocks.reshape(maxb, SIDE, SIDE),
    )


def solution(mesh):
    return jax.shard_map(
        per_device,
        mesh=mesh,
        in_specs=(
            P("dp", "fsdp"),
            P("dp", "tensor"),
            P("fsdp", None),
            P(None, "tensor", "fsdp"),
            P(("fsdp", "tensor"), None, None),
            P(("fsdp", "tensor")),
            P(("fsdp", "tensor")),
            P(),
        ),
        out_specs=(
            P("dp", "tensor", "fsdp"),
            P("fsdp", None),
            P(None, "tensor", "fsdp"),
            P(("fsdp", "tensor"), None, None),
        ),
        check_vma=False,
    )
```

```python
import jax
import jax.numpy as jnp
from jax import lax
from jax.experimental import pallas as pl
from jax.experimental.pallas import tpu as pltpu
from jax.sharding import PartitionSpec as P

F32 = jnp.float32
BF16 = jnp.bfloat16
SIDE = 128
SMEM = pl.BlockSpec(memory_space=pltpu.SMEM)
VMEM = pl.BlockSpec(memory_space=pltpu.VMEM)
HBM = pl.BlockSpec(memory_space=pl.ANY)
ROWS = (((0,), (0,)), ((), ()))
COLS = (((1,), (1,)), ((), ()))


def lanes(block):
    return pl.ds(pl.multiple_of(block * SIDE, SIDE), SIDE)


def span(block, size):
    return pl.ds(pl.multiple_of(block * size, size), size)


def shape(dims, dtype):
    return jax.ShapeDtypeStruct(dims, dtype)


def call(kernel, outs, smem=(), hbm=(), vmem=(), scratch=(), after=(), mib=8, hbm_outs=0):
    n_in, n_out = len(smem) + len(hbm) + len(vmem), len(outs)

    def body(*refs):
        rest = refs[n_in + len(after) :]
        rest[n_out][0] = 0
        kernel(*refs[:n_in], *rest[:n_out], *rest[n_out + 1 :])

    return pl.pallas_call(
        body,
        out_shape=(*outs, shape((1,), jnp.int32)),
        in_specs=[SMEM] * len(smem) + [HBM] * len(hbm) + [VMEM] * len(vmem) + [SMEM] * len(after),
        out_specs=(VMEM,) * (n_out - hbm_outs) + (HBM,) * hbm_outs + (SMEM,),
        scratch_shapes=list(scratch),
        cost_estimate=pl.CostEstimate(flops=0, bytes_accessed=0, transcendentals=0),
        compiler_params=pltpu.CompilerParams(vmem_limit_bytes=mib << 20),
    )(*smem, *hbm, *vmem, *after)


class Place:
    def __init__(self, n_f, n_t, n_d):
        self.n_f, self.n_t, self.n_d, self.chips = n_f, n_t, n_d, n_d // 2

    f = property(lambda self: lax.axis_index("fsdp"))
    t = property(lambda self: lax.axis_index("tensor"))
    chip = property(lambda self: lax.axis_index("dp") // 2)
    core = property(lambda self: lax.rem(lax.axis_index("dp"), 2))

    def live(self, counts):
        return counts[self.f * self.n_t + self.t]


def fetch(*pairs_and_sems):
    copies = [pltpu.make_async_copy(src, dst, sem) for src, dst, sem in pairs_and_sems]
    for copy in copies:
        copy.start()
    return copies


def add_blocks(place, q_blocks, step, counts, rows, cols, tok, vals, acc):
    first = lax.rem(place.f + step, place.n_f) * q_blocks

    def body(s, carry):
        col = cols[s] - first

        @pl.when((col >= 0) & (col < q_blocks))
        def _():
            acc[:, lanes(col)] += jnp.dot(tok[:, lanes(rows[s])], vals[s], preferred_element_type=F32)

        return carry

    lax.fori_loop(0, place.live(counts), body, 0)


def front_kernel(
    place, q_blocks, counts, rows, cols, tok, left, cot, right, vals,
    rank, low, back, s1, s2, s3, ahead, behind,
    tokv, leftv, cotv, rightv, valv, full, acc, stage, sems,
):
    quarter = cotv.shape[1]
    here = pl.ds(pl.multiple_of(place.f * quarter, SIDE), quarter)
    c_tok, c_left, c_val, c_cot, c_right = fetch(
        (tok, tokv, sems.at[0]),
        (left.at[:, lanes(place.t)], leftv, sems.at[1]),
        (vals, valv, sems.at[2]),
        (cot.at[:, here], cotv, sems.at[3]),
        (right, rightv, sems.at[4]),
    )
    acc[...] = jnp.zeros_like(acc)
    c_tok.wait()
    c_left.wait()
    rank[...] = jnp.dot(tokv[...], leftv[...], preferred_element_type=F32)
    low[...] = rank[...].astype(BF16)
    c_val.wait()
    add_blocks(place, q_blocks, place.n_f // 2, counts, rows, cols, tokv, valv, acc)
    half = ahead.shape[0]
    stage[...] = acc[...].astype(BF16)
    c_out = fetch((stage.at[:half], ahead, sems.at[5]), (stage.at[half:], behind, sems.at[6]))
    c_cot.wait()
    c_right.wait()
    full[...] = lax.dot_general(cotv[...], rightv[...], COLS, preferred_element_type=F32)
    back[...] = full[:, lanes(place.t)]
    for k, out in ((1, s1), (2, s2), (3, s3)):
        out[...] = full[:, lanes(lax.rem(place.t + k, place.n_t))].astype(BF16)
    for copy in c_out:
        copy.wait()


def residual_kernel(place, q_blocks, counts, rows, cols, tok, vals, p1, p3, acc):
    acc[...] = jnp.zeros_like(acc)
    n_f, f = place.n_f, place.f

    def body(s, carry):
        q = cols[s] // q_blocks
        step = lax.rem(q - f + n_f, n_f)

        @pl.when(lax.rem(step, 2) == 1)
        def _():
            acc[step // 2, :, lanes(cols[s] - q * q_blocks)] += jnp.dot(
                tok[:, lanes(rows[s])], vals[s], preferred_element_type=F32
            )

        return carry

    lax.fori_loop(0, place.live(counts), body, 0)
    p1[...] = acc[0].astype(BF16)
    p3[...] = acc[1].astype(BF16)


def blocks_kernel(place, counts, rows, cols, tok, cot, _, mine, theirs):
    live = place.live(counts)
    per = mine.shape[1] // SIDE

    def body(owner, carry):
        grads = []
        for u in range(per):
            s = owner * per + u
            grad = lax.dot_general(
                tok[:, lanes(rows[s])], cot[:, lanes(cols[s])], ROWS, preferred_element_type=F32
            )
            grads.append(jnp.where(s < live, grad, jnp.zeros_like(grad)))
        j = lax.rem(owner // 2 - place.chip + place.chips, place.chips)
        keep = lax.rem(owner, 2) == place.core

        @pl.when(keep)
        def _():
            for u, grad in enumerate(grads):
                mine[j, u * SIDE : (u + 1) * SIDE] = grad

        @pl.when(jnp.logical_not(keep))
        def _():
            for u, grad in enumerate(grads):
                theirs[j, u * SIDE : (u + 1) * SIDE] = grad.astype(BF16)

        return carry

    lax.fori_loop(0, place.n_d, body, 0)


def factors_kernel(
    place, tok, cot, g0, g1, g2, g3, b0, b1, b2, b3, blocks_mine, blocks_theirs,
    mine, out1, out2, out3, theirs0, tokv, cotv, left, right, sems,
):
    quarter = right.shape[1]
    here = pl.ds(pl.multiple_of(place.f * quarter, SIDE), quarter)
    c_tok, c_cot = fetch((tok, tokv, sems.at[0]), (cot.at[:, here], cotv, sems.at[1]))
    n_l = left.shape[0] // place.n_d
    n_r = right.shape[0] // place.n_d
    n_lr = n_l + quarter // SIDE * n_r
    outs = (out1, out2, out3)
    theirs = (theirs0, *outs)
    for j in range(place.chips):
        mine[j, n_lr:] = blocks_mine[j]
        theirs[j][n_lr : n_lr + blocks_theirs.shape[1]] = blocks_theirs[j]
    c_tok.wait()
    back = b0[...] + b1[...].astype(F32) + b2[...].astype(F32) + b3[...].astype(F32)
    left[...] = lax.dot_general(
        back.astype(BF16), tokv[...], ROWS, preferred_element_type=F32
    ).T
    c_cot.wait()
    for k, g in enumerate((g0, g1, g2, g3)):
        at = span(lax.rem(place.t - k + place.n_t, place.n_t), SIDE)
        right[at, :] = lax.dot_general(
            g[...], cotv[...], ROWS, preferred_element_type=F32
        )
    for j in range(place.chips):
        chip = lax.rem(place.chip + j, place.chips)
        for core, out in ((place.core, mine.at[j]), (1 - place.core, theirs[j])):
            at = chip * 2 + core
            out[:n_l] = left[span(at, n_l), :].astype(out.dtype)
            for p in range(quarter // SIDE):
                out[n_l + p * n_r : n_l + (p + 1) * n_r] = right[
                    span(at, n_r), p * SIDE : (p + 1) * SIDE
                ].astype(out.dtype)
    row, n_all = 0, theirs0.shape[0]
    for out in outs:
        extra = out.shape[0] - n_all
        out[n_all:] = theirs0[row : row + extra]
        row += extra


def cores_kernel(n_l, mine, got1, got2, got3, own, near, ahead, behind, far):
    mid = n_l + (own.shape[0] - n_l) // 2
    got = (None, got1, got2, got3)

    def both(k, lo, hi):
        return mine[k, lo:hi] + got[k][lo:hi].astype(F32)

    row = 0
    for g in got[1:]:
        extra = g.shape[0] - own.shape[0]
        own[row : row + extra] = mine[0, row : row + extra] + g[own.shape[0] :].astype(F32)
        row += extra

    end = own.shape[0]
    half = end - mid
    far[...] = both(2, 0, n_l).astype(BF16)
    ahead[:n_l] = both(1, 0, n_l).astype(BF16)
    behind[:n_l] = both(3, 0, n_l).astype(BF16)
    ahead[n_l:mid] = both(2, n_l, mid).astype(BF16)
    behind[n_l:mid] = both(2, mid, end).astype(BF16)
    ahead[mid:] = both(1, mid, end).astype(BF16)
    behind[mid:] = both(3, n_l, mid).astype(BF16)
    near[:half] = both(1, n_l, mid)
    near[half:] = both(3, mid, end)


def relay_kernel(own, near, from_behind, from_ahead, from_far, left, ahead, behind):
    n_l, half = left.shape[0], ahead.shape[0]
    mid = n_l + half
    left[...] = (
        own[:n_l] + from_behind[:n_l].astype(F32) + from_ahead[:n_l].astype(F32)
        + from_far[...].astype(F32)
    ).astype(BF16)
    ahead[...] = (near[:half] + from_behind[n_l:mid].astype(F32)).astype(BF16)
    behind[...] = (near[half:] + from_ahead[n_l:mid].astype(F32)).astype(BF16)


def chunk_kernel(own, from_behind, from_ahead, last_behind, last_ahead, pair, far, out):
    half, n = last_behind.shape[0], pair.shape[0]
    n_l = own.shape[0] - 2 * half
    mid = n_l + half
    out[:n] = pair[...]
    out[n : 2 * n] = far[...]
    out[2 * n : 2 * n + half] = (
        own[n_l:mid] + from_ahead[mid:].astype(F32) + last_behind[...].astype(F32)
    ).astype(BF16)
    out[2 * n + half :] = (
        own[mid:] + from_behind[mid:].astype(F32) + last_ahead[...].astype(F32)
    ).astype(BF16)


def stack_kernel(*refs):
    parts, out = refs[:-1], refs[-1]
    row = 0
    for part in parts:
        out[row : row + part.shape[0]] = part[...]
        row += part.shape[0]


def pass_kernel(p1, p3, from_behind, from_ahead, ahead, behind):
    half = from_behind.shape[0]
    ahead[:half] = (p1[:half].astype(F32) + from_behind[...].astype(F32)).astype(BF16)
    ahead[half:] = p1[half:]
    behind[:half] = p3[:half]
    behind[half:] = (p3[half:].astype(F32) + from_ahead[...].astype(F32)).astype(BF16)


def pair_kernel(own, behind, ahead, first, rest):
    n = own.shape[0]
    first[:n] = own[...]
    first[n : 2 * n] = behind[...]
    cut = first.shape[0] - 2 * n
    first[2 * n :] = ahead[:cut]
    rest[...] = ahead[cut:]


def low_kernel(place, q_blocks, counts, rows, cols, tok, vals, g0, g1, g2, g3, right, out):
    acc = jnp.zeros(out.shape, F32)
    for k, g in enumerate((g0, g1, g2, g3)):
        at = span(lax.rem(place.t - k + place.n_t, place.n_t), SIDE)
        acc += jnp.dot(g[...], right[at, :], preferred_element_type=F32)
    out[...] = acc
    add_blocks(place, q_blocks, 0, counts, rows, cols, tok, vals, out)


def put_chunks(place, chunks, left, right, blocks, sems):
    n_l = left.shape[0] // place.n_d
    n_r = right.shape[0] // place.n_d
    n_b = blocks.shape[0] // place.n_d
    panels = right.shape[1] // SIDE
    n_left = place.n_t * n_l
    t = place.t
    near_t = t + 1 - 2 * lax.rem(t, 2)
    far_t = place.n_t - 1 - t
    order = (t, near_t, far_t, place.n_t - 1 - near_t)
    copies = []
    for at, segments in chunks:

        def put(lo, hi, dst):
            base, src = [s for s in segments if s[0] <= lo][-1]
            copies.extend(fetch((src.at[lo - base : hi - base], dst, sems.at[len(copies)])))

        for k in range(place.n_t):
            put(k * n_l, (k + 1) * n_l, left.at[span(at, n_l), lanes(order[k])])
        for p in range(panels):
            lo = n_left + p * n_r
            put(lo, lo + n_r, right.at[span(at, n_r), pl.ds(p * SIDE, SIDE)])
        lo = n_left + panels * n_r
        put(lo, lo + n_b, blocks.at[span(at, n_b)])
    return copies


def chunk_at(place, j, core):
    return lax.rem(place.chip + j + place.chips, place.chips) * 2 + core


def three_chunks(place, core, first, rest):
    n = (first.shape[0] + rest.shape[0]) // 3
    ahead = first.at[2 * n :]
    return [
        (chunk_at(place, 0, core), ((0, first),)),
        (chunk_at(place, -1, core), ((0, first.at[n : 2 * n]),)),
        (chunk_at(place, 1, core), ((0, ahead), (ahead.shape[0], rest))),
    ]


def three_kernel(place, first, rest, left, right, blocks, sems):
    chunks = three_chunks(place, place.core, first, rest)
    for copy in put_chunks(place, chunks, left, right, blocks, sems):
        copy.wait()


def last_kernel(
    place, low, from_behind, from_ahead, last, last2, first2, rest2, l_in, r_in, b_in,
    mixed_out, left, right, blocks, mixed, sems, mixed_sems,
):
    chunks = [
        (chunk_at(place, 2, core), ((0, one),))
        for core, one in ((place.core, last), (1 - place.core, last2))
    ] + three_chunks(place, 1 - place.core, first2, rest2)
    copies = put_chunks(place, chunks, left, right, blocks, sems)
    size = mixed.shape[0] // 4
    for i in range(4):
        rows = pl.ds(i * size, size)
        total = low[rows, :] + from_behind[rows, :].astype(F32) + from_ahead[rows, :].astype(F32)
        mixed[rows, :] = total.astype(BF16)
        copies.extend(fetch((mixed.at[rows], mixed_out.at[rows], mixed_sems.at[i])))
    for copy in copies:
        copy.wait()


def shift(x, axis, n, k):
    return lax.ppermute(x, axis, [(i, (i + k) % n) for i in range(n)])


def chip_shift(x, n_data, k):
    chips = n_data // 2
    perm = [(2 * a + c, 2 * ((a + k) % chips) + c) for a in range(chips) for c in range(2)]
    return lax.ppermute(x, "dp", perm)


def core_swap(x, n_data):
    return lax.ppermute(x, "dp", [(i, i ^ 1) for i in range(n_data)])


def per_device(
    tokens, cotangent, left_factor, right_factor, block_values, block_rows, block_cols, block_counts
):
    n_f = lax.axis_size("fsdp")
    n_t = lax.axis_size("tensor")
    n_d = lax.axis_size("dp")
    place = Place(n_f, n_t, n_d)
    chips = n_d // 2
    maxb = block_values.shape[0]
    tok_rows, features = tokens.shape
    right = right_factor.reshape(right_factor.shape[0], -1)
    rank_size, quarter = right.shape
    q_blocks = quarter // SIDE
    half = tok_rows // 2
    lists = (block_counts, block_rows, block_cols)
    vm, dma = pltpu.VMEM, pltpu.SemaphoreType.DMA

    def bind(kernel, *args):
        return lambda *refs: kernel(place, *args, *refs)

    def over(n, k_shift):
        return [k_shift(k) for k in range(1, n)]

    wide, narrow = shape((tok_rows, SIDE), F32), shape((tok_rows, SIDE), BF16)
    part, whole = shape((half, quarter), BF16), shape((tok_rows, quarter), BF16)
    rank, rank_low, back, *back_out, ahead, behind, step = call(
        bind(front_kernel, q_blocks),
        (wide, narrow, wide, narrow, narrow, narrow, part, part),
        smem=lists,
        hbm=(tokens, left_factor, cotangent, right, block_values),
        scratch=[
            vm((tok_rows, features), BF16),
            vm((features, SIDE), BF16),
            vm((tok_rows, quarter), BF16),
            vm((rank_size, quarter), BF16),
            vm((maxb, SIDE, SIDE), BF16),
            vm((tok_rows, rank_size), F32),
            vm((tok_rows, quarter), F32),
            vm((tok_rows, quarter), BF16),
            dma((7,)),
        ],
        mib=52,
        hbm_outs=2,
    )
    rank_in = over(n_f, lambda k: shift(rank_low, "fsdp", n_f, k))
    back_in = [shift(x, "tensor", n_t, k + 1) for k, x in enumerate(back_out)]

    for x in rank_in:
        rank = rank + x.astype(F32)
    rank, back = lax.optimization_barrier((rank.astype(BF16), back))
    ranks = [rank] + over(n_t, lambda k: shift(rank, "tensor", n_t, k))
    for x in back_in:
        back = back + x.astype(F32)
    back_low = back.astype(BF16)
    backs = [back] + over(n_f, lambda k: shift(back_low, "fsdp", n_f, k))

    n_b = maxb // n_d * SIDE
    blocks_mine, blocks_theirs, step = call(
        bind(blocks_kernel),
        (shape((chips, n_b, SIDE), F32), shape((chips, n_b, SIDE), BF16)),
        smem=lists,
        vmem=(tokens, cotangent, back_low),
        after=(step,),
        mib=20,
    )

    def hand_on(*refs):
        refs[-1][0] = 0

    ahead, behind, step = pl.pallas_call(
        hand_on,
        out_shape=(part, part, shape((1,), jnp.int32)),
        in_specs=[HBM] * 2 + [VMEM] * 6 + [SMEM],
        out_specs=(HBM, HBM, SMEM),
        input_output_aliases={0: 0, 1: 1},
        compiler_params=pltpu.CompilerParams(vmem_limit_bytes=8 << 20),
    )(ahead, behind, *ranks[1:], *backs[1:], step)
    from_behind = shift(ahead, "fsdp", n_f, 1)
    from_ahead = shift(behind, "fsdp", n_f, -1)

    n_l = features // n_d
    n_r = rank_size // n_d
    n_rest = q_blocks * n_r + n_b
    n_all = n_l + n_rest
    chunk = shape((n_all, SIDE), BF16)
    extra = -(-n_all // 3 // 16) * 16
    mine, *theirs, step = call(
        bind(factors_kernel),
        (shape((chips, n_all, SIDE), F32),)
        + tuple(shape((n_all + n, SIDE), BF16) for n in (extra, extra, n_all - 2 * extra)),
        hbm=(tokens, cotangent),
        vmem=(*ranks, *backs, blocks_mine, blocks_theirs),
        scratch=[
            vm((n_all, SIDE), BF16),
            vm((tok_rows, features), BF16),
            vm((tok_rows, quarter), BF16),
            vm((features, SIDE), F32),
            vm((rank_size, quarter), F32),
            dma((2,)),
        ],
        after=(step,),
        mib=36,
    )
    got = [core_swap(x, n_d) for x in theirs]
    p1, p3, step = call(
        bind(residual_kernel, q_blocks),
        (whole, whole),
        smem=lists,
        vmem=(tokens, block_values),
        scratch=[vm((2, tok_rows, quarter), F32)],
        after=(step,),
        mib=24,
    )
    own, c_near, c_ahead, c_behind, c_far, step = call(
        lambda *refs: cores_kernel(n_l, *refs),
        (
            shape((n_all, SIDE), F32),
            shape((n_rest, SIDE), F32),
            chunk,
            chunk,
            shape((n_l, SIDE), BF16),
        ),
        vmem=(mine, *got),
        after=(step,),
        mib=16,
    )
    c_from_behind = chip_shift(c_ahead, n_d, 1)
    c_from_ahead = chip_shift(c_behind, n_d, -1)
    c_from_far = chip_shift(c_far, n_d, 2)

    ahead, behind, step = call(
        pass_kernel, (whole, whole), vmem=(p1, p3, from_behind, from_ahead), after=(step,), mib=16
    )
    last_behind = shift(ahead, "fsdp", n_f, 1)
    last_ahead = shift(behind, "fsdp", n_f, -1)
    left, c_ahead, c_behind, step = call(
        relay_kernel,
        (shape((n_l, SIDE), BF16),) + (shape((n_rest // 2, SIDE), BF16),) * 2,
        vmem=(own, c_near, c_from_behind, c_from_ahead, c_from_far),
        after=(step,),
    )
    left_near = lax.ppermute(left, "tensor", [(i, i ^ 1) for i in range(n_t)])
    c_last_behind = chip_shift(c_ahead, n_d, 1)
    c_last_ahead = chip_shift(c_behind, n_d, -1)
    left_pair, step = call(
        stack_kernel, (shape((2 * n_l, SIDE), BF16),), vmem=(left, left_near), after=(step,)
    )
    left_far = lax.ppermute(left_pair, "tensor", [(i, n_t - 1 - i) for i in range(n_t)])
    n_msg = n_t * n_l + n_rest
    message, step = call(
        chunk_kernel,
        (shape((n_msg, SIDE), BF16),),
        vmem=(own, c_from_behind, c_from_ahead, c_last_behind, c_last_ahead, left_pair, left_far),
        after=(step,),
    )

    m_behind = chip_shift(message, n_d, 1)
    m_ahead = chip_shift(message, n_d, -1)
    m_last_behind = chip_shift(m_behind[: n_msg // 2], n_d, 1)
    m_last_ahead = chip_shift(m_ahead[n_msg // 2 :], n_d, -1)
    low, step = call(
        bind(low_kernel, q_blocks),
        (shape((tok_rows, quarter), F32),),
        smem=lists,
        vmem=(tokens, block_values, *ranks, right),
        after=(step,),
        mib=20,
    )
    first, rest, step = call(
        pair_kernel,
        (shape((2 * n_msg + 3 * n_l, SIDE), BF16), shape((n_msg - 3 * n_l, SIDE), BF16)),
        vmem=(message, m_behind, m_ahead),
        after=(step,),
    )
    per_chunk = n_t + q_blocks + 1
    outs = (
        shape((features, rank_size), BF16),
        shape((rank_size, quarter), BF16),
        shape((maxb * SIDE, SIDE), BF16),
    )
    *grads, step = call(
        bind(three_kernel),
        outs,
        vmem=(first, rest),
        scratch=[dma((3 * per_chunk,))],
        after=(step,),
        mib=16,
        hbm_outs=3,
    )
    m_last, step = call(
        stack_kernel,
        (shape((n_msg, SIDE), BF16),),
        vmem=(m_last_behind, m_last_ahead),
        after=(step,),
    )
    mixed, out_left, out_right, out_blocks = pl.pallas_call(
        bind(last_kernel),
        out_shape=(whole, *outs),
        in_specs=[VMEM] * 7 + [HBM] * 3,
        out_specs=(HBM,) * 4,
        scratch_shapes=[vm((tok_rows, quarter), BF16), dma((5 * per_chunk,)), dma((4,))],
        input_output_aliases={7: 1, 8: 2, 9: 3},
        compiler_params=pltpu.CompilerParams(vmem_limit_bytes=20 << 20),
    )(low, last_behind, last_ahead, m_last, *(core_swap(x, n_d) for x in (m_last, first, rest)), *grads)
    return (
        mixed.reshape(tok_rows, 1, quarter),
        out_left,
        out_right.reshape(right_factor.shape),
        out_blocks.reshape(maxb, SIDE, SIDE),
    )


def solution(mesh):
    return jax.shard_map(
        per_device,
        mesh=mesh,
        in_specs=(
            P("dp", "fsdp"),
            P("dp", "tensor"),
            P("fsdp", None),
            P(None, "tensor", "fsdp"),
            P(("fsdp", "tensor"), None, None),
            P(("fsdp", "tensor")),
            P(("fsdp", "tensor")),
            P(),
        ),
        out_specs=(
            P("dp", "tensor", "fsdp"),
            P("fsdp", None),
            P(None, "tensor", "fsdp"),
            P(("fsdp", "tensor"), None, None),
        ),
        check_vma=False,
    )
```

```python
import jax
import jax.numpy as jnp
from jax import lax
from jax.experimental import pallas as pl
from jax.experimental.pallas import tpu as pltpu
from jax.sharding import PartitionSpec as P

F32 = jnp.float32
BF16 = jnp.bfloat16
SIDE = 128
SMEM = pl.BlockSpec(memory_space=pltpu.SMEM)
VMEM = pl.BlockSpec(memory_space=pltpu.VMEM)
HBM = pl.BlockSpec(memory_space=pl.ANY)
ROWS = (((0,), (0,)), ((), ()))
COLS = (((1,), (1,)), ((), ()))


def lanes(block):
    return pl.ds(pl.multiple_of(block * SIDE, SIDE), SIDE)


def span(block, size):
    return pl.ds(pl.multiple_of(block * size, size), size)


def shape(dims, dtype):
    return jax.ShapeDtypeStruct(dims, dtype)


def call(kernel, outs, smem=(), hbm=(), vmem=(), scratch=(), after=(), mib=8, hbm_outs=0):
    n_in, n_out = len(smem) + len(hbm) + len(vmem), len(outs)

    def body(*refs):
        rest = refs[n_in + len(after) :]
        rest[n_out][0] = 0
        kernel(*refs[:n_in], *rest[:n_out], *rest[n_out + 1 :])

    return pl.pallas_call(
        body,
        out_shape=(*outs, shape((1,), jnp.int32)),
        in_specs=[SMEM] * len(smem) + [HBM] * len(hbm) + [VMEM] * len(vmem) + [SMEM] * len(after),
        out_specs=(VMEM,) * (n_out - hbm_outs) + (HBM,) * hbm_outs + (SMEM,),
        scratch_shapes=list(scratch),
        cost_estimate=pl.CostEstimate(flops=0, bytes_accessed=0, transcendentals=0),
        compiler_params=pltpu.CompilerParams(vmem_limit_bytes=mib << 20),
    )(*smem, *hbm, *vmem, *after)


class Place:
    def __init__(self, n_f, n_t, n_d):
        self.n_f, self.n_t, self.n_d, self.chips = n_f, n_t, n_d, n_d // 2

    f = property(lambda self: lax.axis_index("fsdp"))
    t = property(lambda self: lax.axis_index("tensor"))
    chip = property(lambda self: lax.axis_index("dp") // 2)
    core = property(lambda self: lax.rem(lax.axis_index("dp"), 2))

    def live(self, counts):
        return counts[self.f * self.n_t + self.t]


class Part:
    def __init__(self, ref, start):
        self.ref, self.start = ref, start

    def __getitem__(self, i):
        return self.ref[self.start + i]


def fetch(*pairs_and_sems):
    copies = [pltpu.make_async_copy(src, dst, sem) for src, dst, sem in pairs_and_sems]
    for copy in copies:
        copy.start()
    return copies


def add_blocks(place, q_blocks, step, counts, rows, cols, tok, vals, acc):
    first = lax.rem(place.f + step, place.n_f) * q_blocks

    def body(s, carry):
        col = cols[s] - first

        @pl.when((col >= 0) & (col < q_blocks))
        def _():
            acc[:, lanes(col)] += jnp.dot(tok[:, lanes(rows[s])], vals[s], preferred_element_type=F32)

        return carry

    lax.fori_loop(0, place.live(counts), body, 0)


def front_kernel(
    place, q_blocks, counts, rows, cols, tok, left, cot, right, vals,
    rank, low, back, s1, s2, s3, ahead, behind,
    tokv, leftv, cotv, rightv, valv, full, acc, stage, sems,
):
    quarter = cotv.shape[1]
    here = pl.ds(pl.multiple_of(place.f * quarter, SIDE), quarter)
    c_tok, c_left, c_val, c_cot, c_right = fetch(
        (tok, tokv, sems.at[0]),
        (left.at[:, lanes(place.t)], leftv, sems.at[1]),
        (vals, valv, sems.at[2]),
        (cot.at[:, here], cotv, sems.at[3]),
        (right, rightv, sems.at[4]),
    )
    acc[...] = jnp.zeros_like(acc)
    c_tok.wait()
    c_left.wait()
    rank[...] = jnp.dot(tokv[...], leftv[...], preferred_element_type=F32)
    low[...] = rank[...].astype(BF16)
    c_val.wait()
    add_blocks(place, q_blocks, place.n_f // 2, counts, rows, cols, tokv, valv, acc)
    half = ahead.shape[0]
    stage[...] = acc[...].astype(BF16)
    c_out = fetch((stage.at[:half], ahead, sems.at[5]), (stage.at[half:], behind, sems.at[6]))
    c_cot.wait()
    c_right.wait()
    full[...] = lax.dot_general(cotv[...], rightv[...], COLS, preferred_element_type=F32)
    back[...] = full[:, lanes(place.t)]
    for k, out in ((1, s1), (2, s2), (3, s3)):
        out[...] = full[:, lanes(lax.rem(place.t + k, place.n_t))].astype(BF16)
    for copy in c_out:
        copy.wait()


def residual_kernel(place, q_blocks, counts, rows, cols, tok, vals, p1, p3, acc):
    acc[...] = jnp.zeros_like(acc)
    n_f, f = place.n_f, place.f

    def body(s, carry):
        q = cols[s] // q_blocks
        step = lax.rem(q - f + n_f, n_f)

        @pl.when(lax.rem(step, 2) == 1)
        def _():
            acc[step // 2, :, lanes(cols[s] - q * q_blocks)] += jnp.dot(
                tok[:, lanes(rows[s])], vals[s], preferred_element_type=F32
            )

        return carry

    lax.fori_loop(0, place.live(counts), body, 0)
    p1[...] = acc[0].astype(BF16)
    p3[...] = acc[1].astype(BF16)


def blocks_kernel(place, _q, counts, rows, cols, tok, cot, _, mine, theirs):
    live = place.live(counts)
    per = mine.shape[1] // SIDE

    def body(owner, carry):
        grads = []
        for u in range(per):
            s = owner * per + u
            grad = lax.dot_general(
                tok[:, lanes(rows[s])], cot[:, lanes(cols[s])], ROWS, preferred_element_type=F32
            )
            grads.append(jnp.where(s < live, grad, jnp.zeros_like(grad)))
        j = lax.rem(owner // 2 - place.chip + place.chips, place.chips)
        keep = lax.rem(owner, 2) == place.core

        @pl.when(keep)
        def _():
            for u, grad in enumerate(grads):
                mine[j, u * SIDE : (u + 1) * SIDE] = grad

        @pl.when(jnp.logical_not(keep))
        def _():
            for u, grad in enumerate(grads):
                theirs[j, u * SIDE : (u + 1) * SIDE] = grad.astype(BF16)

        return carry

    lax.fori_loop(0, place.n_d, body, 0)


def factors_kernel(
    place, tok, cot, g0, g1, g2, g3, b0, b1, b2, b3, blocks_mine, blocks_theirs,
    mine, out1, out2, out3, theirs0, tokv, cotv, left, right, sems,
):
    quarter = right.shape[1]
    here = pl.ds(pl.multiple_of(place.f * quarter, SIDE), quarter)
    c_tok, c_cot = fetch((tok, tokv, sems.at[0]), (cot.at[:, here], cotv, sems.at[1]))
    n_l = left.shape[0] // place.n_d
    n_r = right.shape[0] // place.n_d
    n_lr = n_l + quarter // SIDE * n_r
    outs = (out1, out2, out3)
    theirs = (theirs0, *outs)
    for j in range(place.chips):
        mine[j, n_lr:] = blocks_mine[j]
        theirs[j][n_lr : n_lr + blocks_theirs.shape[1]] = blocks_theirs[j]
    c_tok.wait()
    back = b0[...] + b1[...].astype(F32) + b2[...].astype(F32) + b3[...].astype(F32)
    left[...] = lax.dot_general(
        back.astype(BF16), tokv[...], ROWS, preferred_element_type=F32
    ).T
    c_cot.wait()
    for k, g in enumerate((g0, g1, g2, g3)):
        at = span(lax.rem(place.t - k + place.n_t, place.n_t), SIDE)
        right[at, :] = lax.dot_general(
            g[...], cotv[...], ROWS, preferred_element_type=F32
        )
    for j in range(place.chips):
        chip = lax.rem(place.chip + j, place.chips)
        for core, out in ((place.core, mine.at[j]), (1 - place.core, theirs[j])):
            at = chip * 2 + core
            out[:n_l] = left[span(at, n_l), :].astype(out.dtype)
            for p in range(quarter // SIDE):
                out[n_l + p * n_r : n_l + (p + 1) * n_r] = right[
                    span(at, n_r), p * SIDE : (p + 1) * SIDE
                ].astype(out.dtype)
    row, n_all = 0, theirs0.shape[0]
    for out in outs:
        extra = out.shape[0] - n_all
        out[n_all:] = theirs0[row : row + extra]
        row += extra


def cores_kernel(n_l, mine, got1, got2, got3, own, near, ahead, behind, far):
    mid = n_l + (own.shape[0] - n_l) // 2
    got = (None, got1, got2, got3)

    def both(k, lo, hi):
        return mine[k, lo:hi] + got[k][lo:hi].astype(F32)

    row = 0
    for g in got[1:]:
        extra = g.shape[0] - own.shape[0]
        own[row : row + extra] = mine[0, row : row + extra] + g[own.shape[0] :].astype(F32)
        row += extra

    end = own.shape[0]
    half = end - mid
    far[...] = both(2, 0, n_l).astype(BF16)
    ahead[:n_l] = both(1, 0, n_l).astype(BF16)
    behind[:n_l] = both(3, 0, n_l).astype(BF16)
    ahead[n_l:mid] = both(2, n_l, mid).astype(BF16)
    behind[n_l:mid] = both(2, mid, end).astype(BF16)
    ahead[mid:] = both(1, mid, end).astype(BF16)
    behind[mid:] = both(3, n_l, mid).astype(BF16)
    near[:half] = both(1, n_l, mid)
    near[half:] = both(3, mid, end)


def relay_kernel(own, near, from_behind, from_ahead, from_far, left, ahead, behind):
    n_l, half = left.shape[0], ahead.shape[0]
    mid = n_l + half
    left[...] = (
        own[:n_l] + from_behind[:n_l].astype(F32) + from_ahead[:n_l].astype(F32)
        + from_far[...].astype(F32)
    ).astype(BF16)
    ahead[...] = (near[:half] + from_behind[n_l:mid].astype(F32)).astype(BF16)
    behind[...] = (near[half:] + from_ahead[n_l:mid].astype(F32)).astype(BF16)


def chunk_kernel(own, from_behind, from_ahead, last_behind, last_ahead, pair, far, out):
    half, n = last_behind.shape[0], pair.shape[0]
    n_l = own.shape[0] - 2 * half
    mid = n_l + half
    out[:n] = pair[...]
    out[n : 2 * n] = far[...]
    out[2 * n : 2 * n + half] = (
        own[n_l:mid] + from_ahead[mid:].astype(F32) + last_behind[...].astype(F32)
    ).astype(BF16)
    out[2 * n + half :] = (
        own[mid:] + from_behind[mid:].astype(F32) + last_ahead[...].astype(F32)
    ).astype(BF16)


def stack_kernel(*refs):
    parts, out = refs[:-1], refs[-1]
    row = 0
    for part in parts:
        out[row : row + part.shape[0]] = part[...]
        row += part.shape[0]


def pass_kernel(p1, p3, from_behind, from_ahead, ahead, behind):
    half = from_behind.shape[0]
    ahead[:half] = (p1[:half].astype(F32) + from_behind[...].astype(F32)).astype(BF16)
    ahead[half:] = p1[half:]
    behind[:half] = p3[:half]
    behind[half:] = (p3[half:].astype(F32) + from_ahead[...].astype(F32)).astype(BF16)


def pair_kernel(own, behind, ahead, first, rest):
    n = own.shape[0]
    first[:n] = own[...]
    first[n : 2 * n] = behind[...]
    cut = first.shape[0] - 2 * n
    first[2 * n :] = ahead[:cut]
    rest[...] = ahead[cut:]


def low_kernel(place, q_blocks, counts, rows, cols, tok, vals, g0, g1, g2, g3, right, out):
    acc = jnp.zeros(out.shape, F32)
    for k, g in enumerate((g0, g1, g2, g3)):
        at = span(lax.rem(place.t - k + place.n_t, place.n_t), SIDE)
        acc += jnp.dot(g[...], right[at, :], preferred_element_type=F32)
    out[...] = acc
    add_blocks(place, q_blocks, 0, counts, rows, cols, tok, vals, out)


def put_chunks(place, chunks, left, right, blocks, sems):
    n_l = left.shape[0] // place.n_d
    n_r = right.shape[0] // place.n_d
    n_b = blocks.shape[0] // place.n_d
    panels = right.shape[1] // SIDE
    n_left = place.n_t * n_l
    t = place.t
    near_t = t + 1 - 2 * lax.rem(t, 2)
    far_t = place.n_t - 1 - t
    order = (t, near_t, far_t, place.n_t - 1 - near_t)
    copies = []
    for at, segments in chunks:

        def put(lo, hi, dst):
            base, src = [s for s in segments if s[0] <= lo][-1]
            copies.extend(fetch((src.at[lo - base : hi - base], dst, sems.at[len(copies)])))

        for k in range(place.n_t):
            put(k * n_l, (k + 1) * n_l, left.at[span(at, n_l), lanes(order[k])])
        for p in range(panels):
            lo = n_left + p * n_r
            put(lo, lo + n_r, right.at[span(at, n_r), pl.ds(p * SIDE, SIDE)])
        lo = n_left + panels * n_r
        put(lo, lo + n_b, blocks.at[span(at, n_b)])
    return copies


def chunk_at(place, j, core):
    return lax.rem(place.chip + j + place.chips, place.chips) * 2 + core


def three_chunks(place, core, first, rest):
    n = (first.shape[0] + rest.shape[0]) // 3
    ahead = first.at[2 * n :]
    return [
        (chunk_at(place, 0, core), ((0, first),)),
        (chunk_at(place, -1, core), ((0, first.at[n : 2 * n]),)),
        (chunk_at(place, 1, core), ((0, ahead), (ahead.shape[0], rest))),
    ]


def three_kernel(place, first, rest, left, right, blocks, sems):
    chunks = three_chunks(place, place.core, first, rest)
    for copy in put_chunks(place, chunks, left, right, blocks, sems):
        copy.wait()


def last_kernel(
    place, low, from_behind, from_ahead, last, last2, first2, rest2, l_in, r_in, b_in,
    mixed_out, left, right, blocks, mixed, sems, mixed_sems,
):
    chunks = [
        (chunk_at(place, 2, core), ((0, one),))
        for core, one in ((place.core, last), (1 - place.core, last2))
    ] + three_chunks(place, 1 - place.core, first2, rest2)
    copies = put_chunks(place, chunks, left, right, blocks, sems)
    size = mixed.shape[0] // 4
    for i in range(4):
        rows = pl.ds(i * size, size)
        total = low[rows, :] + from_behind[rows, :].astype(F32) + from_ahead[rows, :].astype(F32)
        mixed[rows, :] = total.astype(BF16)
        copies.extend(fetch((mixed.at[rows], mixed_out.at[rows], mixed_sems.at[i])))
    for copy in copies:
        copy.wait()


def shift(x, axis, n, k):
    return lax.ppermute(x, axis, [(i, (i + k) % n) for i in range(n)])


def chip_shift(x, n_data, k):
    chips = n_data // 2
    perm = [(2 * a + c, 2 * ((a + k) % chips) + c) for a in range(chips) for c in range(2)]
    return lax.ppermute(x, "dp", perm)


def core_swap(x, n_data):
    return lax.ppermute(x, "dp", [(i, i ^ 1) for i in range(n_data)])


def per_device(
    tokens, cotangent, left_factor, right_factor, block_values, block_rows, block_cols, block_counts
):
    n_f = lax.axis_size("fsdp")
    n_t = lax.axis_size("tensor")
    n_d = lax.axis_size("dp")
    place = Place(n_f, n_t, n_d)
    chips = n_d // 2
    maxb = block_values.shape[0]
    tok_rows, features = tokens.shape
    right = right_factor.reshape(right_factor.shape[0], -1)
    rank_size, quarter = right.shape
    q_blocks = quarter // SIDE
    half = tok_rows // 2
    lists = (jnp.concatenate([block_counts, block_rows, block_cols]),)
    n_owners = block_counts.shape[0]
    vm, dma = pltpu.VMEM, pltpu.SemaphoreType.DMA

    def bind(kernel, *args):
        return lambda *refs: kernel(place, *args, *refs)

    def listed(kernel):
        parts = (0, n_owners, n_owners + maxb)
        return lambda ints, *refs: kernel(
            place, q_blocks, *(Part(ints, start) for start in parts), *refs
        )

    def over(n, k_shift):
        return [k_shift(k) for k in range(1, n)]

    wide, narrow = shape((tok_rows, SIDE), F32), shape((tok_rows, SIDE), BF16)
    part, whole = shape((half, quarter), BF16), shape((tok_rows, quarter), BF16)
    rank, rank_low, back, *back_out, ahead, behind, step = call(
        listed(front_kernel),
        (wide, narrow, wide, narrow, narrow, narrow, part, part),
        smem=lists,
        hbm=(tokens, left_factor, cotangent, right, block_values),
        scratch=[
            vm((tok_rows, features), BF16),
            vm((features, SIDE), BF16),
            vm((tok_rows, quarter), BF16),
            vm((rank_size, quarter), BF16),
            vm((maxb, SIDE, SIDE), BF16),
            vm((tok_rows, rank_size), F32),
            vm((tok_rows, quarter), F32),
            vm((tok_rows, quarter), BF16),
            dma((7,)),
        ],
        mib=52,
        hbm_outs=2,
    )
    rank_in = over(n_f, lambda k: shift(rank_low, "fsdp", n_f, k))
    back_in = [shift(x, "tensor", n_t, k + 1) for k, x in enumerate(back_out)]

    for x in rank_in:
        rank = rank + x.astype(F32)
    rank = rank.astype(BF16)
    ranks = [rank] + over(n_t, lambda k: shift(rank, "tensor", n_t, k))
    for x in back_in:
        back = back + x.astype(F32)
    back_low = back.astype(BF16)
    backs = [back] + over(n_f, lambda k: shift(back_low, "fsdp", n_f, k))

    n_b = maxb // n_d * SIDE
    blocks_mine, blocks_theirs, step = call(
        listed(blocks_kernel),
        (shape((chips, n_b, SIDE), F32), shape((chips, n_b, SIDE), BF16)),
        smem=lists,
        vmem=(tokens, cotangent, back_low),
        after=(step,),
        mib=20,
    )

    def hand_on(*refs):
        refs[-1][0] = 0

    ahead, behind, step = pl.pallas_call(
        hand_on,
        out_shape=(part, part, shape((1,), jnp.int32)),
        in_specs=[HBM] * 2 + [VMEM] * 6 + [SMEM],
        out_specs=(HBM, HBM, SMEM),
        input_output_aliases={0: 0, 1: 1},
        compiler_params=pltpu.CompilerParams(vmem_limit_bytes=8 << 20),
    )(ahead, behind, *ranks[1:], *backs[1:], step)
    from_behind = shift(ahead, "fsdp", n_f, 1)
    from_ahead = shift(behind, "fsdp", n_f, -1)

    n_l = features // n_d
    n_r = rank_size // n_d
    n_rest = q_blocks * n_r + n_b
    n_all = n_l + n_rest
    chunk = shape((n_all, SIDE), BF16)
    extra = -(-n_all // 3 // 16) * 16
    mine, *theirs, step = call(
        bind(factors_kernel),
        (shape((chips, n_all, SIDE), F32),)
        + tuple(shape((n_all + n, SIDE), BF16) for n in (extra, extra, n_all - 2 * extra)),
        hbm=(tokens, cotangent),
        vmem=(*ranks, *backs, blocks_mine, blocks_theirs),
        scratch=[
            vm((n_all, SIDE), BF16),
            vm((tok_rows, features), BF16),
            vm((tok_rows, quarter), BF16),
            vm((features, SIDE), F32),
            vm((rank_size, quarter), F32),
            dma((2,)),
        ],
        after=(step,),
        mib=36,
    )
    got = [core_swap(x, n_d) for x in theirs]
    p1, p3, step = call(
        listed(residual_kernel),
        (whole, whole),
        smem=lists,
        vmem=(tokens, block_values),
        scratch=[vm((2, tok_rows, quarter), F32)],
        after=(step,),
        mib=24,
    )
    own, c_near, c_ahead, c_behind, c_far, step = call(
        lambda *refs: cores_kernel(n_l, *refs),
        (
            shape((n_all, SIDE), F32),
            shape((n_rest, SIDE), F32),
            chunk,
            chunk,
            shape((n_l, SIDE), BF16),
        ),
        vmem=(mine, *got),
        after=(step,),
        mib=16,
    )
    c_from_behind = chip_shift(c_ahead, n_d, 1)
    c_from_ahead = chip_shift(c_behind, n_d, -1)
    c_from_far = chip_shift(c_far, n_d, 2)

    ahead, behind, step = call(
        pass_kernel, (whole, whole), vmem=(p1, p3, from_behind, from_ahead), after=(step,), mib=16
    )
    last_behind = shift(ahead, "fsdp", n_f, 1)
    last_ahead = shift(behind, "fsdp", n_f, -1)
    left, c_ahead, c_behind, step = call(
        relay_kernel,
        (shape((n_l, SIDE), BF16),) + (shape((n_rest // 2, SIDE), BF16),) * 2,
        vmem=(own, c_near, c_from_behind, c_from_ahead, c_from_far),
        after=(step,),
    )
    left_near = lax.ppermute(left, "tensor", [(i, i ^ 1) for i in range(n_t)])
    c_last_behind = chip_shift(c_ahead, n_d, 1)
    c_last_ahead = chip_shift(c_behind, n_d, -1)
    left_pair, step = call(
        stack_kernel, (shape((2 * n_l, SIDE), BF16),), vmem=(left, left_near), after=(step,)
    )
    left_far = lax.ppermute(left_pair, "tensor", [(i, n_t - 1 - i) for i in range(n_t)])
    n_msg = n_t * n_l + n_rest
    message, step = call(
        chunk_kernel,
        (shape((n_msg, SIDE), BF16),),
        vmem=(own, c_from_behind, c_from_ahead, c_last_behind, c_last_ahead, left_pair, left_far),
        after=(step,),
    )

    m_behind = chip_shift(message, n_d, 1)
    m_ahead = chip_shift(message, n_d, -1)
    m_last_behind = chip_shift(m_behind[: n_msg // 2], n_d, 1)
    m_last_ahead = chip_shift(m_ahead[n_msg // 2 :], n_d, -1)
    low, step = call(
        listed(low_kernel),
        (shape((tok_rows, quarter), F32),),
        smem=lists,
        vmem=(tokens, block_values, *ranks, right),
        after=(step,),
        mib=20,
    )
    first, rest, step = call(
        pair_kernel,
        (shape((2 * n_msg + 3 * n_l, SIDE), BF16), shape((n_msg - 3 * n_l, SIDE), BF16)),
        vmem=(message, m_behind, m_ahead),
        after=(step,),
    )
    per_chunk = n_t + q_blocks + 1
    outs = (
        shape((features, rank_size), BF16),
        shape((rank_size, quarter), BF16),
        shape((maxb * SIDE, SIDE), BF16),
    )
    *grads, step = call(
        bind(three_kernel),
        outs,
        vmem=(first, rest),
        scratch=[dma((3 * per_chunk,))],
        after=(step,),
        mib=16,
        hbm_outs=3,
    )
    m_last, step = call(
        stack_kernel,
        (shape((n_msg, SIDE), BF16),),
        vmem=(m_last_behind, m_last_ahead),
        after=(step,),
    )
    mixed, out_left, out_right, out_blocks = pl.pallas_call(
        bind(last_kernel),
        out_shape=(whole, *outs),
        in_specs=[VMEM] * 7 + [HBM] * 3,
        out_specs=(HBM,) * 4,
        scratch_shapes=[vm((tok_rows, quarter), BF16), dma((5 * per_chunk,)), dma((4,))],
        input_output_aliases={7: 1, 8: 2, 9: 3},
        compiler_params=pltpu.CompilerParams(vmem_limit_bytes=20 << 20),
    )(low, last_behind, last_ahead, m_last, *(core_swap(x, n_d) for x in (m_last, first, rest)), *grads)
    return (
        mixed.reshape(tok_rows, 1, quarter),
        out_left,
        out_right.reshape(right_factor.shape),
        out_blocks.reshape(maxb, SIDE, SIDE),
    )


def solution(mesh):
    return jax.shard_map(
        per_device,
        mesh=mesh,
        in_specs=(
            P("dp", "fsdp"),
            P("dp", "tensor"),
            P("fsdp", None),
            P(None, "tensor", "fsdp"),
            P(("fsdp", "tensor"), None, None),
            P(("fsdp", "tensor")),
            P(("fsdp", "tensor")),
            P(),
        ),
        out_specs=(
            P("dp", "tensor", "fsdp"),
            P("fsdp", None),
            P(None, "tensor", "fsdp"),
            P(("fsdp", "tensor"), None, None),
        ),
        check_vma=False,
    )
```

```python
import jax
import jax.numpy as jnp
from jax import lax
from jax.experimental import pallas as pl
from jax.experimental.pallas import tpu as pltpu
from jax.sharding import PartitionSpec as P

F32 = jnp.float32
BF16 = jnp.bfloat16
SIDE = 128
SMEM = pl.BlockSpec(memory_space=pltpu.SMEM)
VMEM = pl.BlockSpec(memory_space=pltpu.VMEM)
HBM = pl.BlockSpec(memory_space=pl.ANY)
ROWS = (((0,), (0,)), ((), ()))
COLS = (((1,), (1,)), ((), ()))


def lanes(block):
    return pl.ds(pl.multiple_of(block * SIDE, SIDE), SIDE)


def span(block, size):
    return pl.ds(pl.multiple_of(block * size, size), size)


def shape(dims, dtype):
    return jax.ShapeDtypeStruct(dims, dtype)


def call(kernel, outs, smem=(), hbm=(), vmem=(), scratch=(), after=(), mib=8, hbm_outs=0):
    n_in, n_out = len(smem) + len(hbm) + len(vmem), len(outs)

    def body(*refs):
        rest = refs[n_in + len(after) :]
        rest[n_out][0] = 0
        kernel(*refs[:n_in], *rest[:n_out], *rest[n_out + 1 :])

    return pl.pallas_call(
        body,
        out_shape=(*outs, shape((1,), jnp.int32)),
        in_specs=[SMEM] * len(smem) + [HBM] * len(hbm) + [VMEM] * len(vmem) + [SMEM] * len(after),
        out_specs=(VMEM,) * (n_out - hbm_outs) + (HBM,) * hbm_outs + (SMEM,),
        scratch_shapes=list(scratch),
        cost_estimate=pl.CostEstimate(flops=0, bytes_accessed=0, transcendentals=0),
        compiler_params=pltpu.CompilerParams(vmem_limit_bytes=mib << 20),
    )(*smem, *hbm, *vmem, *after)


class Place:
    def __init__(self, n_f, n_t, n_d):
        self.n_f, self.n_t, self.n_d, self.chips = n_f, n_t, n_d, n_d // 2

    f = property(lambda self: lax.axis_index("fsdp"))
    t = property(lambda self: lax.axis_index("tensor"))
    chip = property(lambda self: lax.axis_index("dp") // 2)
    core = property(lambda self: lax.rem(lax.axis_index("dp"), 2))

    def live(self, counts):
        return counts[self.f * self.n_t + self.t]


class Part:
    def __init__(self, ref, start):
        self.ref, self.start = ref, start

    def __getitem__(self, i):
        return self.ref[self.start + i]


def fetch(*pairs_and_sems):
    copies = [pltpu.make_async_copy(src, dst, sem) for src, dst, sem in pairs_and_sems]
    for copy in copies:
        copy.start()
    return copies


def add_blocks(place, q_blocks, step, counts, rows, cols, tok, vals, acc):
    first = lax.rem(place.f + step, place.n_f) * q_blocks

    def body(s, carry):
        col = cols[s] - first

        @pl.when((col >= 0) & (col < q_blocks))
        def _():
            acc[:, lanes(col)] += jnp.dot(tok[:, lanes(rows[s])], vals[s], preferred_element_type=F32)

        return carry

    lax.fori_loop(0, place.live(counts), body, 0)


def front_kernel(
    place, q_blocks, counts, rows, cols, tok, left, cot, right, vals,
    rank, low, back, s1, s2, s3, ahead, behind,
    tokv, leftv, cotv, rightv, valv, full, acc, stage, sems,
):
    quarter = cotv.shape[1]
    here = pl.ds(pl.multiple_of(place.f * quarter, SIDE), quarter)
    c_tok, c_left, c_val, c_cot, c_right = fetch(
        (tok, tokv, sems.at[0]),
        (left.at[:, lanes(place.t)], leftv, sems.at[1]),
        (vals, valv, sems.at[2]),
        (cot.at[:, here], cotv, sems.at[3]),
        (right, rightv, sems.at[4]),
    )
    acc[...] = jnp.zeros_like(acc)
    c_tok.wait()
    c_left.wait()
    rank[...] = jnp.dot(tokv[...], leftv[...], preferred_element_type=F32)
    low[...] = rank[...].astype(BF16)
    c_val.wait()
    add_blocks(place, q_blocks, place.n_f // 2, counts, rows, cols, tokv, valv, acc)
    half = ahead.shape[0]
    stage[...] = acc[...].astype(BF16)
    c_out = fetch((stage.at[:half], ahead, sems.at[5]), (stage.at[half:], behind, sems.at[6]))
    c_cot.wait()
    c_right.wait()
    full[...] = lax.dot_general(cotv[...], rightv[...], COLS, preferred_element_type=F32)
    back[...] = full[:, lanes(place.t)]
    for k, out in ((1, s1), (2, s2), (3, s3)):
        out[...] = full[:, lanes(lax.rem(place.t + k, place.n_t))].astype(BF16)
    for copy in c_out:
        copy.wait()


def residual_kernel(place, q_blocks, counts, rows, cols, tok, vals, p1, p3, acc):
    acc[...] = jnp.zeros_like(acc)
    n_f, f = place.n_f, place.f

    def body(s, carry):
        q = cols[s] // q_blocks
        step = lax.rem(q - f + n_f, n_f)

        @pl.when(lax.rem(step, 2) == 1)
        def _():
            acc[step // 2, :, lanes(cols[s] - q * q_blocks)] += jnp.dot(
                tok[:, lanes(rows[s])], vals[s], preferred_element_type=F32
            )

        return carry

    lax.fori_loop(0, place.live(counts), body, 0)
    p1[...] = acc[0].astype(BF16)
    p3[...] = acc[1].astype(BF16)


def blocks_kernel(place, _q, counts, rows, cols, tok, cot, _, mine, theirs):
    live = place.live(counts)
    per = mine.shape[1] // SIDE

    def body(owner, carry):
        grads = []
        for u in range(per):
            s = owner * per + u
            grad = lax.dot_general(
                tok[:, lanes(rows[s])], cot[:, lanes(cols[s])], ROWS, preferred_element_type=F32
            )
            grads.append(jnp.where(s < live, grad, jnp.zeros_like(grad)))
        j = lax.rem(owner // 2 - place.chip + place.chips, place.chips)
        keep = lax.rem(owner, 2) == place.core

        @pl.when(keep)
        def _():
            for u, grad in enumerate(grads):
                mine[j, u * SIDE : (u + 1) * SIDE] = grad

        @pl.when(jnp.logical_not(keep))
        def _():
            for u, grad in enumerate(grads):
                theirs[j, u * SIDE : (u + 1) * SIDE] = grad.astype(BF16)

        return carry

    lax.fori_loop(0, place.n_d, body, 0)


def factors_kernel(
    place, tok, cot, g0, g1, g2, g3, b0, b1, b2, b3, blocks_mine, blocks_theirs,
    mine, out1, out2, out3, theirs0, tokv, cotv, left, right, sems,
):
    quarter = right.shape[1]
    here = pl.ds(pl.multiple_of(place.f * quarter, SIDE), quarter)
    c_tok, c_cot = fetch((tok, tokv, sems.at[0]), (cot.at[:, here], cotv, sems.at[1]))
    n_l = left.shape[0] // place.n_d
    n_r = right.shape[0] // place.n_d
    n_lr = n_l + quarter // SIDE * n_r
    outs = (out1, out2, out3)
    theirs = (theirs0, *outs)
    for j in range(place.chips):
        mine[j, n_lr:] = blocks_mine[j]
        theirs[j][n_lr : n_lr + blocks_theirs.shape[1]] = blocks_theirs[j]
    c_tok.wait()
    back = b0[...] + b1[...].astype(F32) + b2[...].astype(F32) + b3[...].astype(F32)
    left[...] = lax.dot_general(
        back.astype(BF16), tokv[...], ROWS, preferred_element_type=F32
    ).T
    c_cot.wait()
    for k, g in enumerate((g0, g1, g2, g3)):
        at = span(lax.rem(place.t - k + place.n_t, place.n_t), SIDE)
        right[at, :] = lax.dot_general(
            g[...], cotv[...], ROWS, preferred_element_type=F32
        )
    for j in range(place.chips):
        chip = lax.rem(place.chip + j, place.chips)
        for core, out in ((place.core, mine.at[j]), (1 - place.core, theirs[j])):
            at = chip * 2 + core
            out[:n_l] = left[span(at, n_l), :].astype(out.dtype)
            for p in range(quarter // SIDE):
                out[n_l + p * n_r : n_l + (p + 1) * n_r] = right[
                    span(at, n_r), p * SIDE : (p + 1) * SIDE
                ].astype(out.dtype)
    row, n_all = 0, theirs0.shape[0]
    for out in outs:
        extra = out.shape[0] - n_all
        out[n_all:] = theirs0[row : row + extra]
        row += extra


def cores_kernel(n_l, mine, got1, got2, got3, own, near, ahead, behind, far):
    mid = n_l + (own.shape[0] - n_l) // 2
    got = (None, got1, got2, got3)

    def both(k, lo, hi):
        return mine[k, lo:hi] + got[k][lo:hi].astype(F32)

    row = 0
    for g in got[1:]:
        extra = g.shape[0] - own.shape[0]
        own[row : row + extra] = mine[0, row : row + extra] + g[own.shape[0] :].astype(F32)
        row += extra

    end = own.shape[0]
    half = end - mid
    far[...] = both(2, 0, n_l).astype(BF16)
    ahead[:n_l] = both(1, 0, n_l).astype(BF16)
    behind[:n_l] = both(3, 0, n_l).astype(BF16)
    ahead[n_l:mid] = both(2, n_l, mid).astype(BF16)
    behind[n_l:mid] = both(2, mid, end).astype(BF16)
    ahead[mid:] = both(1, mid, end).astype(BF16)
    behind[mid:] = both(3, n_l, mid).astype(BF16)
    near[:half] = both(1, n_l, mid)
    near[half:] = both(3, mid, end)


def relay_kernel(own, near, from_behind, from_ahead, from_far, left, ahead, behind):
    n_l, half = left.shape[0], ahead.shape[0]
    mid = n_l + half
    left[...] = (
        own[:n_l] + from_behind[:n_l].astype(F32) + from_ahead[:n_l].astype(F32)
        + from_far[...].astype(F32)
    ).astype(BF16)
    ahead[...] = (near[:half] + from_behind[n_l:mid].astype(F32)).astype(BF16)
    behind[...] = (near[half:] + from_ahead[n_l:mid].astype(F32)).astype(BF16)


def chunk_kernel(own, from_behind, from_ahead, last_behind, last_ahead, pair, far, out):
    half, n = last_behind.shape[0], pair.shape[0]
    n_l = own.shape[0] - 2 * half
    mid = n_l + half
    out[:n] = pair[...]
    out[n : 2 * n] = far[...]
    out[2 * n : 2 * n + half] = (
        own[n_l:mid] + from_ahead[mid:].astype(F32) + last_behind[...].astype(F32)
    ).astype(BF16)
    out[2 * n + half :] = (
        own[mid:] + from_behind[mid:].astype(F32) + last_ahead[...].astype(F32)
    ).astype(BF16)


def stack_kernel(*refs):
    parts, out = refs[:-1], refs[-1]
    row = 0
    for part in parts:
        out[row : row + part.shape[0]] = part[...]
        row += part.shape[0]


def pass_kernel(p1, p3, from_behind, from_ahead, ahead, behind):
    half = from_behind.shape[0]
    ahead[:half] = (p1[:half].astype(F32) + from_behind[...].astype(F32)).astype(BF16)
    ahead[half:] = p1[half:]
    behind[:half] = p3[:half]
    behind[half:] = (p3[half:].astype(F32) + from_ahead[...].astype(F32)).astype(BF16)


def pair_kernel(own, behind, ahead, first, rest):
    n = own.shape[0]
    first[:n] = own[...]
    first[n : 2 * n] = behind[...]
    cut = first.shape[0] - 2 * n
    first[2 * n :] = ahead[:cut]
    rest[...] = ahead[cut:]


def low_kernel(place, q_blocks, counts, rows, cols, tok, vals, g0, g1, g2, g3, right, out):
    acc = jnp.zeros(out.shape, F32)
    for k, g in enumerate((g0, g1, g2, g3)):
        at = span(lax.rem(place.t - k + place.n_t, place.n_t), SIDE)
        acc += jnp.dot(g[...], right[at, :], preferred_element_type=F32)
    out[...] = acc
    add_blocks(place, q_blocks, 0, counts, rows, cols, tok, vals, out)


def put_chunks(place, chunks, left, right, blocks, sems):
    n_l = left.shape[0] // place.n_d
    n_r = right.shape[0] // place.n_d
    n_b = blocks.shape[0] // place.n_d
    panels = right.shape[1] // SIDE
    n_left = place.n_t * n_l
    t = place.t
    near_t = t + 1 - 2 * lax.rem(t, 2)
    far_t = place.n_t - 1 - t
    order = (t, near_t, far_t, place.n_t - 1 - near_t)
    copies = []
    for at, segments in chunks:

        def put(lo, hi, dst):
            base, src = [s for s in segments if s[0] <= lo][-1]
            copies.extend(fetch((src.at[lo - base : hi - base], dst, sems.at[len(copies)])))

        for k in range(place.n_t):
            put(k * n_l, (k + 1) * n_l, left.at[span(at, n_l), lanes(order[k])])
        for p in range(panels):
            lo = n_left + p * n_r
            put(lo, lo + n_r, right.at[span(at, n_r), pl.ds(p * SIDE, SIDE)])
        lo = n_left + panels * n_r
        put(lo, lo + n_b, blocks.at[span(at, n_b)])
    return copies


def chunk_at(place, j, core):
    return lax.rem(place.chip + j + place.chips, place.chips) * 2 + core


def three_chunks(place, core, first, rest):
    n = (first.shape[0] + rest.shape[0]) // 3
    ahead = first.at[2 * n :]
    return [
        (chunk_at(place, 0, core), ((0, first),)),
        (chunk_at(place, -1, core), ((0, first.at[n : 2 * n]),)),
        (chunk_at(place, 1, core), ((0, ahead), (ahead.shape[0], rest))),
    ]


def three_kernel(place, first, rest, left, right, blocks, sems):
    chunks = three_chunks(place, place.core, first, rest)
    for copy in put_chunks(place, chunks, left, right, blocks, sems):
        copy.wait()


def last_kernel(
    place, low, from_behind, from_ahead, last, last2, first2, rest2, l_in, r_in, b_in,
    mixed_out, left, right, blocks, mixed, sems, mixed_sems,
):
    chunks = [
        (chunk_at(place, 2, core), ((0, one),))
        for core, one in ((place.core, last), (1 - place.core, last2))
    ] + three_chunks(place, 1 - place.core, first2, rest2)
    copies = put_chunks(place, chunks, left, right, blocks, sems)
    size = mixed.shape[0] // 4
    for i in range(4):
        rows = pl.ds(i * size, size)
        total = low[rows, :] + from_behind[rows, :].astype(F32) + from_ahead[rows, :].astype(F32)
        mixed[rows, :] = total.astype(BF16)
        copies.extend(fetch((mixed.at[rows], mixed_out.at[rows], mixed_sems.at[i])))
    for copy in copies:
        copy.wait()


def shift(x, axis, n, k):
    return lax.ppermute(x, axis, [(i, (i + k) % n) for i in range(n)])


def chip_shift(x, n_data, k):
    chips = n_data // 2
    perm = [(2 * a + c, 2 * ((a + k) % chips) + c) for a in range(chips) for c in range(2)]
    return lax.ppermute(x, "dp", perm)


def core_swap(x, n_data):
    return lax.ppermute(x, "dp", [(i, i ^ 1) for i in range(n_data)])


def per_device(
    tokens, cotangent, left_factor, right_factor, block_values, block_rows, block_cols, block_counts
):
    n_f = lax.axis_size("fsdp")
    n_t = lax.axis_size("tensor")
    n_d = lax.axis_size("dp")
    place = Place(n_f, n_t, n_d)
    chips = n_d // 2
    maxb = block_values.shape[0]
    tok_rows, features = tokens.shape
    right = right_factor.reshape(right_factor.shape[0], -1)
    rank_size, quarter = right.shape
    q_blocks = quarter // SIDE
    half = tok_rows // 2
    lists = (jnp.concatenate([block_counts, block_rows, block_cols]),)
    n_owners = block_counts.shape[0]
    vm, dma = pltpu.VMEM, pltpu.SemaphoreType.DMA

    def bind(kernel, *args):
        return lambda *refs: kernel(place, *args, *refs)

    def listed(kernel):
        parts = (0, n_owners, n_owners + maxb)
        return lambda ints, *refs: kernel(
            place, q_blocks, *(Part(ints, start) for start in parts), *refs
        )

    def over(n, k_shift):
        return [k_shift(k) for k in range(1, n)]

    wide, narrow = shape((tok_rows, SIDE), F32), shape((tok_rows, SIDE), BF16)
    part, whole = shape((half, quarter), BF16), shape((tok_rows, quarter), BF16)
    rank, rank_low, back, *back_out, ahead, behind, step = call(
        listed(front_kernel),
        (wide, narrow, wide, narrow, narrow, narrow, part, part),
        smem=lists,
        hbm=(tokens, left_factor, cotangent, right, block_values),
        scratch=[
            vm((tok_rows, features), BF16),
            vm((features, SIDE), BF16),
            vm((tok_rows, quarter), BF16),
            vm((rank_size, quarter), BF16),
            vm((maxb, SIDE, SIDE), BF16),
            vm((tok_rows, rank_size), F32),
            vm((tok_rows, quarter), F32),
            vm((tok_rows, quarter), BF16),
            dma((7,)),
        ],
        mib=48,
        hbm_outs=2,
    )
    rank_in = over(n_f, lambda k: shift(rank_low, "fsdp", n_f, k))
    back_in = [shift(x, "tensor", n_t, k + 1) for k, x in enumerate(back_out)]

    for x in rank_in:
        rank = rank + x.astype(F32)
    rank = rank.astype(BF16)
    ranks = [rank] + over(n_t, lambda k: shift(rank, "tensor", n_t, k))
    for x in back_in:
        back = back + x.astype(F32)
    back_low = back.astype(BF16)
    backs = [back] + over(n_f, lambda k: shift(back_low, "fsdp", n_f, k))

    n_b = maxb // n_d * SIDE
    blocks_mine, blocks_theirs, step = call(
        listed(blocks_kernel),
        (shape((chips, n_b, SIDE), F32), shape((chips, n_b, SIDE), BF16)),
        smem=lists,
        vmem=(tokens, cotangent, back_low),
        after=(step,),
        mib=20,
    )

    def hand_on(*refs):
        refs[-1][0] = 0

    ahead, behind, step = pl.pallas_call(
        hand_on,
        out_shape=(part, part, shape((1,), jnp.int32)),
        in_specs=[HBM] * 2 + [VMEM] * 6 + [SMEM],
        out_specs=(HBM, HBM, SMEM),
        input_output_aliases={0: 0, 1: 1},
        compiler_params=pltpu.CompilerParams(vmem_limit_bytes=8 << 20),
    )(ahead, behind, *ranks[1:], *backs[1:], step)
    from_behind = shift(ahead, "fsdp", n_f, 1)
    from_ahead = shift(behind, "fsdp", n_f, -1)

    n_l = features // n_d
    n_r = rank_size // n_d
    n_rest = q_blocks * n_r + n_b
    n_all = n_l + n_rest
    chunk = shape((n_all, SIDE), BF16)
    extra = -(-n_all // 3 // 16) * 16
    mine, *theirs, step = call(
        bind(factors_kernel),
        (shape((chips, n_all, SIDE), F32),)
        + tuple(shape((n_all + n, SIDE), BF16) for n in (extra, extra, n_all - 2 * extra)),
        hbm=(tokens, cotangent),
        vmem=(*ranks, *backs, blocks_mine, blocks_theirs),
        scratch=[
            vm((n_all, SIDE), BF16),
            vm((tok_rows, features), BF16),
            vm((tok_rows, quarter), BF16),
            vm((features, SIDE), F32),
            vm((rank_size, quarter), F32),
            dma((2,)),
        ],
        after=(step,),
        mib=36,
    )
    got = [core_swap(x, n_d) for x in theirs]
    p1, p3, step = call(
        listed(residual_kernel),
        (whole, whole),
        smem=lists,
        vmem=(tokens, block_values),
        scratch=[vm((2, tok_rows, quarter), F32)],
        after=(step,),
        mib=24,
    )
    own, c_near, c_ahead, c_behind, c_far, step = call(
        lambda *refs: cores_kernel(n_l, *refs),
        (
            shape((n_all, SIDE), F32),
            shape((n_rest, SIDE), F32),
            chunk,
            chunk,
            shape((n_l, SIDE), BF16),
        ),
        vmem=(mine, *got),
        after=(step,),
        mib=16,
    )
    c_from_behind = chip_shift(c_ahead, n_d, 1)
    c_from_ahead = chip_shift(c_behind, n_d, -1)
    c_from_far = chip_shift(c_far, n_d, 2)

    ahead, behind, step = call(
        pass_kernel, (whole, whole), vmem=(p1, p3, from_behind, from_ahead), after=(step,), mib=16
    )
    last_behind = shift(ahead, "fsdp", n_f, 1)
    last_ahead = shift(behind, "fsdp", n_f, -1)
    left, c_ahead, c_behind, step = call(
        relay_kernel,
        (shape((n_l, SIDE), BF16),) + (shape((n_rest // 2, SIDE), BF16),) * 2,
        vmem=(own, c_near, c_from_behind, c_from_ahead, c_from_far),
        after=(step,),
    )
    left_near = lax.ppermute(left, "tensor", [(i, i ^ 1) for i in range(n_t)])
    c_last_behind = chip_shift(c_ahead, n_d, 1)
    c_last_ahead = chip_shift(c_behind, n_d, -1)
    left_pair, step = call(
        stack_kernel, (shape((2 * n_l, SIDE), BF16),), vmem=(left, left_near), after=(step,)
    )
    left_far = lax.ppermute(left_pair, "tensor", [(i, n_t - 1 - i) for i in range(n_t)])
    n_msg = n_t * n_l + n_rest
    message, step = call(
        chunk_kernel,
        (shape((n_msg, SIDE), BF16),),
        vmem=(own, c_from_behind, c_from_ahead, c_last_behind, c_last_ahead, left_pair, left_far),
        after=(step,),
    )

    m_behind = chip_shift(message, n_d, 1)
    m_ahead = chip_shift(message, n_d, -1)
    m_last_behind = chip_shift(m_behind[: n_msg // 2], n_d, 1)
    m_last_ahead = chip_shift(m_ahead[n_msg // 2 :], n_d, -1)
    low, step = call(
        listed(low_kernel),
        (shape((tok_rows, quarter), F32),),
        smem=lists,
        vmem=(tokens, block_values, *ranks, right),
        after=(step,),
        mib=20,
    )
    first, rest, step = call(
        pair_kernel,
        (shape((2 * n_msg + 3 * n_l, SIDE), BF16), shape((n_msg - 3 * n_l, SIDE), BF16)),
        vmem=(message, m_behind, m_ahead),
        after=(step,),
    )
    per_chunk = n_t + q_blocks + 1
    outs = (
        shape((features, rank_size), BF16),
        shape((rank_size, quarter), BF16),
        shape((maxb * SIDE, SIDE), BF16),
    )
    *grads, step = call(
        bind(three_kernel),
        outs,
        vmem=(first, rest),
        scratch=[dma((3 * per_chunk,))],
        after=(step,),
        mib=16,
        hbm_outs=3,
    )
    m_last, step = call(
        stack_kernel,
        (shape((n_msg, SIDE), BF16),),
        vmem=(m_last_behind, m_last_ahead),
        after=(step,),
    )
    mixed, out_left, out_right, out_blocks = pl.pallas_call(
        bind(last_kernel),
        out_shape=(whole, *outs),
        in_specs=[VMEM] * 7 + [HBM] * 3,
        out_specs=(HBM,) * 4,
        scratch_shapes=[vm((tok_rows, quarter), BF16), dma((5 * per_chunk,)), dma((4,))],
        input_output_aliases={7: 1, 8: 2, 9: 3},
        compiler_params=pltpu.CompilerParams(vmem_limit_bytes=20 << 20),
    )(low, last_behind, last_ahead, m_last, *(core_swap(x, n_d) for x in (m_last, first, rest)), *grads)
    return (
        mixed.reshape(tok_rows, 1, quarter),
        out_left,
        out_right.reshape(right_factor.shape),
        out_blocks.reshape(maxb, SIDE, SIDE),
    )


def solution(mesh):
    return jax.shard_map(
        per_device,
        mesh=mesh,
        in_specs=(
            P("dp", "fsdp"),
            P("dp", "tensor"),
            P("fsdp", None),
            P(None, "tensor", "fsdp"),
            P(("fsdp", "tensor"), None, None),
            P(("fsdp", "tensor")),
            P(("fsdp", "tensor")),
            P(),
        ),
        out_specs=(
            P("dp", "tensor", "fsdp"),
            P("fsdp", None),
            P(None, "tensor", "fsdp"),
            P(("fsdp", "tensor"), None, None),
        ),
        check_vma=False,
    )
```
